256 devices in a mesh: dp: 8 (over z), ctx: 8 (over x, core), seq: 4 (over y).
Axes of the slice: x: 4, y: 4, z: 8, core: 2. Of those that a mesh axis runs over, the one named last changes fastest.
Arguments:
- query_nope: bfloat16 [8, 2048, 16, 128], P('dp', ('ctx', 'seq')), may hold values from -6 to 6
- query_rope: bfloat16 [8, 2048, 16, 64], P('dp', ('ctx', 'seq')), may hold values from -8 to 8
- latent: bfloat16 [8, 2048, 512], P('dp', ('ctx', 'seq')), may hold values from -6 to 6
- key_rope: bfloat16 [8, 2048, 64], P('dp', ('ctx', 'seq')), may hold values from -8 to 8
- out_grad: bfloat16 [8, 2048, 2048], P('dp', ('ctx', 'seq')), may hold values from -6 to 6
- key_weight: bfloat16 [512, 2048], P(None, 'ctx'), may hold values from -0.25 to 0.25
- value_weight: bfloat16 [512, 2048], P(None, 'ctx'), may hold values from -0.25 to 0.25
- block_doc: int32 [8, 32], P('dp'), may hold values from 0 to 3, never falling along the last dimension, each value on 1 to 16 neighbouring positions
- block_image: int32 [8, 32], P('dp'), may hold values from 0 to 15, never falling along the last dimension, each value on 1 to 4 neighbouring positions
- block_flag: int32 [8, 32], P('dp'), may hold values 0 or 1
Outputs:
- attended: bfloat16 [8, 2048, 2048], P('dp', ('ctx', 'seq'))
- query_nope_grad: bfloat16 [8, 2048, 16, 128], P('dp', ('ctx', 'seq'))
- query_rope_grad: bfloat16 [8, 2048, 16, 64], P('dp', ('ctx', 'seq'))
- latent_grad: bfloat16 [8, 2048, 512], P('dp', ('ctx', 'seq'))
- key_rope_grad: bfloat16 [8, 2048, 64], P('dp', ('ctx', 'seq'))
- key_weight_grad: float32 [512, 2048], P(('dp', 'seq'), 'ctx')
- value_weight_grad: float32 [512, 2048], P(('dp', 'seq'), 'ctx')
The draws below stay inside these ranges and needn't reach their ends.
Inputs may be any that keep to these rules, and one draw needn't show every extreme that they name: `block_doc`: never falls along a sequence; each document spans 1 to 16 blocks, one exactly that many. `block_image`: never falls along a sequence; each segment spans 1 to 4 blocks.
All inputs are finite; a program needn't handle non-finite values. No bound on the sum of `block_flag` on one device may be relied on, other than what follows from the above.
Results may differ from the reference program's by a relative error of at most 0.0095.
Values may be sent and summed in bfloat16 or wider, within the bound.
A program may use at most 64 MiB of HBM per device.

```python
import math
import jax
import jax.numpy as jnp
import numpy as np
from jax import lax

LATENT = 512
NOPE = 128
ROPE = 64
BLOCK = 64
DOCS = 4
HEADS = 16
BATCH = 8
SEQLEN = 2048
NBLK = 32


def draw_query_rope(key, part):
    key = jax.random.fold_in(key, 1)
    shape = (BATCH, SEQLEN, HEADS, ROPE)
    base = jnp.clip(jax.random.normal(key, shape, jnp.float32), -4.0, 4.0)
    return base.astype(jnp.bfloat16)


def draw_key_rope(key, part):
    key = jax.random.fold_in(key, 2)
    shape = (BATCH, SEQLEN, ROPE)
    base = jnp.clip(jax.random.normal(key, shape, jnp.float32), -4.0, 4.0)
    return base.astype(jnp.bfloat16)


def place_ends(drawn, key, least, top_value):
    longest = drawn.shape.index(max(drawn.shape))
    spots = []
    for shift in (0, 1):
        where = [jax.random.randint(jax.random.fold_in(key, axis), (), 0, length) for axis, length in enumerate(drawn.shape)]
        where[longest] = (where[longest] + shift) % drawn.shape[longest]
        spots.append(tuple(where))
    return drawn.at[spots[0]].set(least).at[spots[1]].set(top_value)


def levels(stream_key, extent, split, smallest, top_value):
    def one(dim, blocks):
        draws = jax.random.uniform(jax.random.fold_in(jax.random.fold_in(stream_key, 6), dim), (blocks,), jnp.float32, smallest / len(split), top_value / len(split))
        return jnp.repeat(jnp.exp(draws), extent[dim] // blocks).reshape((-1,) + (1,) * (len(extent) - dim - 1))

    gain = one(*split[0])
    for cut in split[1:]:
        gain = gain * one(*cut)
    return gain


def profile(count, total, bound, lean):
    portions = [(1 << 20) // math.isqrt(grade ** lean) + 1 for grade in range(2, count + 1)]
    surplus, holding = total - bound - (count - 1), [1] * (count - 1)
    while surplus > 0:
        movable = [i for i in range(count - 1) if holding[i] < bound]
        mass, budget = sum([portions[i] for i in movable]), surplus
        for i in movable:
            more = min(bound - holding[i], max(1, budget * portions[i] // mass), surplus)
            holding[i] = holding[i] + more
            surplus = surplus - more
    return np.array([bound] + holding)


def uneven_parts(stream_key, number_of, total, reach, skew):
    if number_of == 2:
        one = jax.random.randint(stream_key, (), max(1, total - reach), min(reach, total - 1) + 1)
        return jnp.stack([one, total - one])
    tallies = jnp.asarray(profile(number_of, total, reach, skew), jnp.int32)
    pairs = (number_of - 1) // 2
    giver, receiver = tallies[1:1 + 2 * pairs:2], tallies[2:2 + 2 * pairs:2]
    slack = jnp.minimum(giver - 1, reach - receiver)
    passed = jax.random.randint(jax.random.fold_in(stream_key, 1), (pairs,), 0, 1 << 20) % (slack + 1)
    tallies = tallies.at[1:1 + 2 * pairs:2].set(giver - passed).at[2:2 + 2 * pairs:2].set(receiver + passed)
    return tallies[jax.random.permutation(jax.random.fold_in(stream_key, 2), number_of)]


def noise(key, shape, width, bound, shards=(), held_as=jnp.bfloat16):
    values = jax.random.normal(key, shape, jnp.float32) * width
    if len(shards) > 0:
        values = levels(key, shape, shards, -0.22, 0.18) * values
    return jnp.clip(values, min=-bound, max=bound).astype(held_as)


def setup_inputs(seed: int = 0) -> dict:
    streams_of = jax.random.split(jax.random.key(seed), 11)
    return {
        "query_nope": noise(streams_of[0], (BATCH, SEQLEN, HEADS, NOPE), 1.0, 6.0, ((0, 8), (1, 32))),
        "query_rope": draw_query_rope(jax.random.fold_in(streams_of[10], 71), 0),
        "latent": noise(streams_of[2], (BATCH, SEQLEN, LATENT), 1.0, 6.0, ((0, 8), (1, 32))),
        "key_rope": draw_key_rope(jax.random.fold_in(streams_of[10], 71), 0),
        "out_grad": noise(streams_of[4], (BATCH, SEQLEN, HEADS * NOPE), 1.0, 6.0, ((0, 8), (1, 32))),
        "key_weight": noise(streams_of[5], (LATENT, HEADS * NOPE), LATENT ** -0.5, 0.25, ((1, 8),)),
        "value_weight": noise(streams_of[6], (LATENT, HEADS * NOPE), LATENT ** -0.5, 0.25, ((1, 8),)),
        "block_doc": jax.vmap(lambda own: jnp.searchsorted(jnp.cumsum(uneven_parts(own, DOCS, NBLK, NBLK // 2, 2)), jnp.arange(NBLK), side="right"))(jax.random.split(streams_of[7], BATCH)).reshape((BATCH, NBLK)).astype(jnp.int32),
        "block_image": jax.vmap(lambda own: jnp.searchsorted(jnp.cumsum(uneven_parts(own, NBLK // 2, NBLK, 4, 0)), jnp.arange(NBLK), side="right"))(jax.random.split(streams_of[8], BATCH)).reshape((BATCH, NBLK)).astype(jnp.int32),
        "block_flag": place_ends((jax.random.randint(streams_of[9], (BATCH, NBLK), 0, 2) < 1).astype(jnp.int32), jax.random.fold_in(streams_of[9], 1), 0, 1),
    }


NEG = -1e+30

def attend_head(query_n, query_r, grad_o, key_n, values, key_r, allowed):
    score_scale = 1.0 / math.sqrt(NOPE + ROPE)
    scores = (jnp.dot(query_n, key_n.T, preferred_element_type=jnp.float32) + jnp.dot(query_r, key_r.T, preferred_element_type=jnp.float32)) * score_scale
    masked = jnp.where(allowed, scores, NEG)
    row_max = lax.optimization_barrier(jnp.max(masked, axis=1))
    log_total = row_max + jnp.log(lax.optimization_barrier(jnp.sum(jnp.where(allowed, jnp.exp(scores - row_max[:, None]), 0.0), axis=1)))
    probs = jnp.where(allowed, jnp.exp(scores - log_total[:, None]), 0.0)
    probs_b = probs.astype(jnp.bfloat16)
    output = jnp.dot(probs_b, values, preferred_element_type=jnp.float32)
    row_delta = lax.optimization_barrier(jnp.sum(grad_o.astype(jnp.float32) * output, axis=1))
    grad_probs = jnp.dot(grad_o, values.T, preferred_element_type=jnp.float32)
    score_grad = (score_scale * probs * (grad_probs - row_delta[:, None])).astype(jnp.bfloat16)
    values_grad = jnp.dot(probs_b.T, grad_o, preferred_element_type=jnp.float32)
    qn_grad = jnp.dot(score_grad, key_n, preferred_element_type=jnp.float32)
    qr_grad = jnp.dot(score_grad, key_r, preferred_element_type=jnp.float32)
    kn_grad = jnp.dot(score_grad.T, query_n, preferred_element_type=jnp.float32)
    kr_grad = jnp.dot(score_grad.T, query_r, preferred_element_type=jnp.float32)
    return (output, qn_grad, qr_grad, kn_grad, values_grad, kr_grad)

def reference(query_nope, query_rope, latent, key_rope, out_grad, key_weight, value_weight, block_doc, block_image, block_flag):
    high = lax.Precision.HIGHEST
    weight_k32 = key_weight.astype(jnp.float32)
    weight_v32 = value_weight.astype(jnp.float32)
    wk_total = jnp.zeros((LATENT, HEADS * NOPE), jnp.float32)
    wv_total = jnp.zeros((LATENT, HEADS * NOPE), jnp.float32)
    outs_a, outs_qn, outs_qr, outs_lat, outs_kr = ([], [], [], [], [])
    position = jnp.arange(SEQLEN, dtype=jnp.int32)
    for batch_row in range(BATCH):
        key_n = jnp.dot(latent[batch_row], key_weight, preferred_element_type=jnp.float32).astype(jnp.bfloat16).reshape(SEQLEN, HEADS, NOPE)
        values = jnp.dot(latent[batch_row], value_weight, preferred_element_type=jnp.float32).astype(jnp.bfloat16).reshape(SEQLEN, HEADS, NOPE)
        doc_ids = jnp.repeat(block_doc[batch_row], BLOCK)
        image_ids = jnp.repeat(block_image[batch_row], BLOCK)
        flags = jnp.repeat(block_flag[batch_row], BLOCK)
        bidir = (flags[:, None] == 1) & (flags[None, :] == 1) & (image_ids[:, None] == image_ids[None, :])
        allowed = (doc_ids[:, None] == doc_ids[None, :]) & ((position[None, :] <= position[:, None]) | bidir)
        grad_o = out_grad[batch_row].reshape(SEQLEN, HEADS, NOPE)
        key_r = key_rope[batch_row]
        stacks = (jnp.transpose(query_nope[batch_row], (1, 0, 2)), jnp.transpose(query_rope[batch_row], (1, 0, 2)), jnp.transpose(grad_o, (1, 0, 2)), jnp.transpose(key_n, (1, 0, 2)), jnp.transpose(values, (1, 0, 2)))
        output, qn_grad, qr_grad, kn_grad, values_grad, kr_grad = lax.map(lambda items: attend_head(items[0], items[1], items[2], items[3], items[4], key_r, allowed), stacks)
        outs_a.append(jnp.transpose(output, (1, 0, 2)).reshape(SEQLEN, HEADS * NOPE).astype(jnp.bfloat16))
        outs_qn.append(jnp.transpose(qn_grad, (1, 0, 2)).astype(jnp.bfloat16))
        outs_qr.append(jnp.transpose(qr_grad, (1, 0, 2)).astype(jnp.bfloat16))
        kn_flat = jnp.transpose(kn_grad, (1, 0, 2)).reshape(SEQLEN, HEADS * NOPE)
        vg_flat = jnp.transpose(values_grad, (1, 0, 2)).reshape(SEQLEN, HEADS * NOPE)
        lat_grad = jnp.dot(kn_flat, weight_k32.T, precision=high) + jnp.dot(vg_flat, weight_v32.T, precision=high)
        outs_lat.append(lat_grad.astype(jnp.bfloat16))
        outs_kr.append(lax.optimization_barrier(jnp.sum(kr_grad, axis=0)).astype(jnp.bfloat16))
        lat32 = latent[batch_row].astype(jnp.float32)
        wk_total = wk_total + jnp.dot(lat32.T, kn_flat, precision=high)
        wv_total = wv_total + jnp.dot(lat32.T, vg_flat, precision=high)
    return (jnp.stack(outs_a), jnp.stack(outs_qn), jnp.stack(outs_qr), jnp.stack(outs_lat), jnp.stack(outs_kr), wk_total, wv_total)
```

```python
import functools
import math

import jax
import jax.numpy as jnp
from jax import lax
from jax.experimental import pallas as pl
from jax.experimental.pallas import tpu as pltpu
from jax.sharding import PartitionSpec as P

NEG = -1e30
MESH = pl.DeviceIdType.MESH
VM = pl.BlockSpec(memory_space=pltpu.VMEM)
SM = pl.BlockSpec(memory_space=pltpu.SMEM)
ANY = pl.BlockSpec(memory_space=pl.ANY)
DMA = pltpu.SemaphoreType.DMA
BF = jnp.bfloat16
F32 = jnp.float32

NX, NC, NY, NZ = 4, 2, 4, 8
NCTX = NX * NC
TOK, HEADS, HD, RD, LAT = 64, 16, 128, 64, 512
PACK = 640
NQ = NCTX * TOK
NK = NX * NC * NY * TOK
CHUNK = 256
NCH = NK // CHUNK
SCALE = 1.0 / math.sqrt(HD + RD)
SCALE2 = SCALE * math.log2(math.e)


def rc(src, dst, send, recv, dev):
    return pltpu.make_async_remote_copy(
        src_ref=src, dst_ref=dst, send_sem=send, recv_sem=recv, device_id=dev, device_id_type=MESH
    )


def enter(axes):
    barrier = pltpu.get_barrier_semaphore()
    total = 0
    for axis, size in axes:
        me = lax.axis_index(axis)
        for d in range(1, size):
            pl.semaphore_signal(
                barrier, inc=1, device_id={axis: lax.rem(me + d, size)}, device_id_type=MESH
            )
            total += 1
    return barrier, total


def gather_kernel(
    qn_ref, qr_ref, do_ref, lat_ref, kr_ref, q_all, lat_all, comb, pack,
    xs, xr, us, ur, ds, dr, fs, fr, ws, wr, qs, qrs, loc,
):
    ctx = lax.axis_index("ctx")
    y = lax.axis_index("seq")
    x = ctx // NC
    k = lax.rem(ctx, NC)
    sib = {"ctx": x * NC + 1 - k}
    up = {"seq": lax.rem(y + 1, NY)}
    down = {"seq": lax.rem(y + NY - 1, NY)}
    barrier, total = enter((("ctx", NCTX), ("seq", NY)))
    comb[:, 0:LAT] = lat_ref[0]
    comb[:, LAT : LAT + RD] = kr_ref[0]
    comb[:, LAT + RD :] = kr_ref[0]
    pl.semaphore_wait(barrier, total)
    mine = lat_all.at[x, k, y]
    sends = []

    def go(copy):
        copy.start()
        sends.append(copy)
        return copy

    xcp = []
    for d in range(1, NX):
        dev = {"ctx": lax.rem(x + d, NX) * NC + k}
        xcp.append(go(rc(comb, mine, xs.at[d - 1], xr.at[d - 1], dev)))
    ups, downs = [], []
    ups.append(go(rc(comb, mine, us.at[0], ur.at[0], up)))
    downs.append(go(rc(comb, mine, ds.at[0], dr.at[0], down)))
    swaps = [go(rc(comb, mine, ws.at[0], wr.at[0], sib))]
    own = pltpu.make_async_copy(comb, mine, loc.at[0])
    own.start()
    qn = qn_ref[0].reshape(TOK, HEADS * HD)
    qr = qr_ref[0].reshape(TOK, HEADS * RD)
    for c in range(NCTX):
        pack[c, :, 0:256] = qn[:, c * 256 : (c + 1) * 256]
        pack[c, :, 256:512] = do_ref[0, :, c * 256 : (c + 1) * 256]
        pack[c, :, 512:640] = qr[:, c * 128 : (c + 1) * 128]
    qcp = []
    for d in range(1, NCTX):
        to = lax.rem(ctx + d, NCTX)
        qcp.append(go(rc(pack.at[to], q_all.at[ctx], qs.at[d - 1], qrs.at[d - 1], {"ctx": to})))
    ownq = pltpu.make_async_copy(pack.at[ctx], q_all.at[ctx], loc.at[1])
    ownq.start()

    def at(d, yy):
        return lat_all.at[lax.rem(x + NX - d, NX), k, yy]

    for d in range(1, NX):
        xcp[d - 1].wait_recv()
        blk = at(d, y)
        ups.append(go(rc(blk, blk, us.at[d], ur.at[d], up)))
        downs.append(go(rc(blk, blk, ds.at[d], dr.at[d], down)))
        swaps.append(go(rc(blk, blk, ws.at[d], wr.at[d], sib)))
    yd, yu, yo = lax.rem(y + NY - 1, NY), lax.rem(y + 1, NY), lax.rem(y + 2, NY)
    fwd = []
    for d in range(NX):
        ups[d].wait_recv()
        blk = at(d, yd)
        if d < 2:
            fwd.append(go(rc(blk, blk, fs.at[d], fr.at[d], up)))
        swaps.append(go(rc(blk, blk, ws.at[4 + d], wr.at[4 + d], sib)))
        downs[d].wait_recv()
        blk = at(d, yu)
        if d >= 2:
            fwd.append(go(rc(blk, blk, fs.at[d], fr.at[d], down)))
        swaps.append(go(rc(blk, blk, ws.at[8 + d], wr.at[8 + d], sib)))
    for d in range(NX):
        fwd[d].wait_recv()
        blk = at(d, yo)
        swaps.append(go(rc(blk, blk, ws.at[12 + d], wr.at[12 + d], sib)))
    for copy in swaps + qcp:
        copy.wait_recv()
    for copy in sends:
        copy.wait_send()
    own.wait()
    ownq.wait()


def gather(query_nope, query_rope, out_grad, latent, key_rope):
    return pl.pallas_call(
        gather_kernel,
        out_shape=(
            jax.ShapeDtypeStruct((NCTX, TOK, PACK), BF),
            jax.ShapeDtypeStruct((NX, NC, NY, TOK, PACK), BF),
        ),
        in_specs=[VM] * 5,
        out_specs=(ANY, ANY),
        scratch_shapes=[
            pltpu.VMEM((TOK, PACK), BF),
            pltpu.VMEM((NCTX, TOK, PACK), BF),
            DMA((3,)), DMA((3,)), DMA((4,)), DMA((4,)), DMA((4,)), DMA((4,)),
            DMA((4,)), DMA((4,)), DMA((16,)), DMA((16,)), DMA((7,)), DMA((7,)), DMA((2,)),
        ],
        compiler_params=pltpu.CompilerParams(
            collective_id=0, has_side_effects=True, vmem_limit_bytes=24 * 2**20
        ),
        name="gather",
    )(query_nope, query_rope, out_grad, latent, key_rope)


def dot(a, b):
    return jnp.dot(a, b, preferred_element_type=F32)


def attend_kernel(
    doc_ref, img_ref, flag_ref, q_ref, lat_ref, wk_ref, wv_ref, oq_ref, lk_ref, wg_ref,
    w_all, w_t, lat_t, kc, kct, v, vt, qc, qct, dot_t, sc, grads, o_t, dq_t,
):
    s = lax.axis_index("seq")
    w_all[:, 0:256] = wk_ref[...]
    w_all[:, 256:512] = wv_ref[...]
    w_t[...] = w_all[...].T
    lane_k = lax.broadcasted_iota(jnp.int32, (CHUNK, 128), 1)
    row_k = lax.broadcasted_iota(jnp.int32, (128, CHUNK), 0)
    zero = jnp.zeros((), BF)
    for j in range(NCH):
        r = slice(j * CHUNK, (j + 1) * CHUNK)
        lat = lat_ref[r, 0:LAT]
        kr = lat_ref[r, LAT:PACK]
        lat_t[:, r] = lat.T
        kv = dot(lat, w_all[...]).astype(BF)
        kvt = dot(w_t[...], lat_t[:, r]).astype(BF)
        krt = kr.T
        for h in range(2):
            kc[h, r, 0:128] = kv[:, h * 128 : (h + 1) * 128]
            kc[h, r, 128:256] = jnp.where((lane_k < RD) == (h == 0), kr, zero)
            kct[h, 0:128, r] = kvt[h * 128 : (h + 1) * 128]
            kct[h, 128:256, r] = jnp.where((row_k < RD) == (h == 0), krt, zero)
            v[h, r, :] = kv[:, 256 + h * 128 : 256 + (h + 1) * 128]
            vt[h, :, r] = kvt[256 + h * 128 : 256 + (h + 1) * 128]
    for h in range(2):
        qc[h, :, 0:128] = q_ref[:, h * 128 : (h + 1) * 128]
        qc[h, :, 128:256] = q_ref[:, 512:640]
        qct[h] = qc[h].T
        dot_t[h] = q_ref[:, 256 + h * 128 : 256 + (h + 1) * 128].T

    lane_q = lax.broadcasted_iota(jnp.int32, (1, NQ), 1)
    grp = lane_q // TOK
    qdoc = jnp.zeros((1, NQ), jnp.int32)
    qcode = jnp.zeros((1, NQ), jnp.int32)
    for c in range(NCTX):
        b = 4 * c + s
        qdoc = jnp.where(grp == c, doc_ref[0, b], qdoc)
        code = jnp.where(flag_ref[0, b] == 1, doc_ref[0, b] * 64 + img_ref[0, b], -1)
        qcode = jnp.where(grp == c, code, qcode)
    qpos = (4 * grp + s) * TOK + lane_q % TOK
    sub = lax.broadcasted_iota(jnp.int32, (TOK, 1), 0)

    spans = []
    for j in range(NCH):
        lo = max(0, j - 1) // 2 * 2
        hi = min(NCTX, (min(NCTX, j + 5) + 1) // 2 * 2)
        spans.append((lo * TOK, hi * TOK))

    neg = jnp.full((1, NQ), NEG, F32)
    mx = [neg, neg]
    for j in range(NCH):
        a, b = spans[j]
        r = slice(j * CHUNK, (j + 1) * CHUNK)
        thr = []
        for i in range(CHUNK // TOK):
            kb = j * (CHUNK // TOK) + i
            kcode = jnp.where(flag_ref[0, kb] == 1, doc_ref[0, kb] * 64 + img_ref[0, kb], -2)
            t = jnp.where(qdoc[:, a:b] == doc_ref[0, kb], qpos[:, a:b] - kb * TOK, -1)
            thr.append(jnp.where(qcode[:, a:b] == kcode, NK, t))
        for h in range(2):
            raw = dot(kc[h, r, :], qct[h, :, a:b])
            part = None
            for i in range(CHUNK // TOK):
                rows = slice(i * TOK, (i + 1) * TOK)
                m = jnp.where(sub <= thr[i], raw[rows] * SCALE2, NEG)
                sc[h, j * CHUNK + i * TOK : j * CHUNK + (i + 1) * TOK, a:b] = m
                top = jnp.max(m, axis=0, keepdims=True)
                part = top if part is None else jnp.maximum(part, top)
            new = jnp.maximum(mx[h][:, a:b], part)
            pieces = [mx[h][:, 0:a]] if a else []
            pieces.append(new)
            if b < NQ:
                pieces.append(mx[h][:, b:])
            mx[h] = jnp.concatenate(pieces, axis=1) if len(pieces) > 1 else new

    tot = [jnp.zeros((1, NQ), F32)] * 2
    o_t[...] = jnp.zeros_like(o_t)
    dq_t[...] = jnp.zeros_like(dq_t)
    for j in range(NCH):
        a, b = spans[j]
        r = slice(j * CHUNK, (j + 1) * CHUNK)
        for h in range(2):
            p = jnp.exp2(sc[h, r, a:b] - mx[h][:, a:b])
            sc[h, r, a:b] = p
            new = tot[h][:, a:b] + jnp.sum(p, axis=0, keepdims=True)
            pieces = [tot[h][:, 0:a]] if a else []
            pieces.append(new)
            if b < NQ:
                pieces.append(tot[h][:, b:])
            tot[h] = jnp.concatenate(pieces, axis=1) if len(pieces) > 1 else new
            o_t[h, :, a:b] += dot(vt[h, :, r], p.astype(BF))
    inv = [1.0 / tot[h] for h in range(2)]
    delta = []
    for h in range(2):
        out = o_t[h] * inv[h]
        oq_ref[:, h * 128 : (h + 1) * 128] = out.T.astype(BF)
        delta.append(jnp.sum(out * dot_t[h].astype(F32), axis=0, keepdims=True))

    for j in range(NCH):
        a, b = spans[j]
        r = slice(j * CHUNK, (j + 1) * CHUNK)
        kr_g = []
        for h in range(2):
            p = sc[h, r, a:b] * inv[h][:, a:b]
            dp = dot(v[h, r, :], dot_t[h, :, a:b])
            ds = (p * (dp - delta[h][:, a:b])).astype(BF)
            dv = dot(p.astype(BF), q_ref[a:b, 256 + h * 128 : 256 + (h + 1) * 128])
            dk = dot(ds, qc[h, a:b, :]) * SCALE
            dq_t[h, :, a:b] += dot(kct[h, :, r], ds)
            grads[r, h * 128 : (h + 1) * 128] = dk[:, 0:128].astype(BF)
            grads[r, 256 + h * 128 : 256 + (h + 1) * 128] = dv.astype(BF)
            kr_g.append(dk[:, 128:256])
        lk_ref[r, LAT:PACK] = jnp.where(lane_k < RD, kr_g[0], kr_g[1]).astype(BF)
        lk_ref[r, 0:LAT] = dot(grads[r, :], w_t[...]).astype(BF)
    for h in range(2):
        oq_ref[:, 256 + h * 128 : 256 + (h + 1) * 128] = (dq_t[h, 0:128, :] * SCALE).T.astype(BF)
    oq_ref[:, 512:640] = ((dq_t[0, 128:256, :] + dq_t[1, 128:256, :]) * SCALE).T.astype(BF)
    for i in range(2):
        rows = slice(i * 256, (i + 1) * 256)
        wg_ref[rows, :] = dot(lat_t[rows, :], grads[...]).astype(BF)


def attend(block_doc, block_image, block_flag, q_all, lat_all, key_weight, value_weight):
    return pl.pallas_call(
        attend_kernel,
        out_shape=(
            jax.ShapeDtypeStruct((NQ, PACK), BF),
            jax.ShapeDtypeStruct((NK, PACK), BF),
            jax.ShapeDtypeStruct((LAT, 512), BF),
        ),
        in_specs=[SM] * 3 + [VM] * 4,
        out_specs=(VM, VM, VM),
        scratch_shapes=[
            pltpu.VMEM((LAT, 512), BF),
            pltpu.VMEM((512, LAT), BF),
            pltpu.VMEM((LAT, NK), BF),
            pltpu.VMEM((2, NK, 256), BF),
            pltpu.VMEM((2, 256, NK), BF),
            pltpu.VMEM((2, NK, 128), BF),
            pltpu.VMEM((2, 128, NK), BF),
            pltpu.VMEM((2, NQ, 256), BF),
            pltpu.VMEM((2, 256, NQ), BF),
            pltpu.VMEM((2, 128, NQ), BF),
            pltpu.VMEM((2, NK, NQ), F32),
            pltpu.VMEM((NK, 512), BF),
            pltpu.VMEM((2, 128, NQ), F32),
            pltpu.VMEM((2, 256, NQ), F32),
        ],
        compiler_params=pltpu.CompilerParams(vmem_limit_bytes=52 * 2**20),
        name="attend",
    )(block_doc, block_image, block_flag, q_all, lat_all, key_weight, value_weight)


def scatter_kernel(
    oq_ref, lk_ref, wg_ref, att_ref, qn_ref, qr_ref, lat_ref, kr_ref, wk_ref, wv_ref,
    oq_in, sw_in, y_out, y_in, x_out, x_in, z_in, z_out, w_in, f_own,
    qs, qrs, ss, sr, ys, yr, xs, xr, zs, zr, ws, wr,
):
    ctx = lax.axis_index("ctx")
    y = lax.axis_index("seq")
    z = lax.axis_index("dp")
    x = ctx // NC
    k = lax.rem(ctx, NC)
    sib = {"ctx": x * NC + 1 - k}
    barrier, total = enter((("ctx", NCTX), ("seq", NY), ("dp", NZ)))
    pl.semaphore_wait(barrier, total)
    sends = []

    def go(copy):
        copy.start()
        sends.append(copy)
        return copy

    swap = []
    for d in (1, 2, 3, 0):
        yy = lax.rem(y + d, NY)
        swap.append(go(rc(lk_ref.at[:, 1 - k, yy], sw_in.at[d], ss.at[d], sr.at[d], sib)))
    zc = []
    for d in range(1, NZ):
        to = lax.rem(z + d, NZ)
        zc.append(go(rc(wg_ref.at[to], z_in.at[d - 1], zs.at[d - 1], zr.at[d - 1], {"dp": to})))
    qc = []
    for d in range(1, NCTX):
        to = lax.rem(ctx + d, NCTX)
        qc.append(go(rc(oq_ref.at[to], oq_in.at[ctx], qs.at[d - 1], qrs.at[d - 1], {"ctx": to})))
    oq_in[ctx] = oq_ref[ctx]
    yc = []
    for n, d in enumerate((1, 2, 3, 0)):
        yy = lax.rem(y + d, NY)
        swap[n].wait_recv()

        def add(i, carry, d=d, yy=yy):
            y_out[d, i] = (lk_ref[i, k, yy].astype(F32) + sw_in[d, i].astype(F32)).astype(BF)
            return carry

        lax.fori_loop(0, NX, add, 0)
        if d:
            yc.append(go(rc(y_out.at[d], y_in.at[d - 1], ys.at[d - 1], yr.at[d - 1], {"seq": yy})))
    for copy in yc:
        copy.wait_recv()

    def add_y(i, carry):
        t = y_out[0, i].astype(F32)
        for d in range(NY - 1):
            t = t + y_in[d, i].astype(F32)
        x_out[i] = t.astype(BF)
        return carry

    lax.fori_loop(0, NX, add_y, 0)
    xc = []
    for d in range(1, NX):
        to = lax.rem(x + d, NX)
        xc.append(
            go(rc(x_out.at[to], x_in.at[d - 1], xs.at[d - 1], xr.at[d - 1], {"ctx": to * NC + k}))
        )
    for copy in zc:
        copy.wait_recv()
    t = wg_ref[z].astype(F32)
    for d in range(NZ - 1):
        t = t + z_in[d].astype(F32)
    z_out[...] = t.astype(BF).reshape(NY, 16, 512)
    wc = []
    for d in range(1, NY):
        to = lax.rem(y + d, NY)
        wc.append(go(rc(z_out.at[to], w_in.at[d - 1], ws.at[d - 1], wr.at[d - 1], {"seq": to})))
    for copy in qc:
        copy.wait_recv()
    for c in range(NCTX):
        att_ref[0, :, c * 256 : (c + 1) * 256] = oq_in[c, :, 0:256]
        for h in range(2):
            qn_ref[0, :, 2 * c + h, :] = oq_in[c, :, 256 + h * 128 : 256 + (h + 1) * 128]
            qr_ref[0, :, 2 * c + h, :] = oq_in[c, :, 512 + h * RD : 512 + (h + 1) * RD]
    for copy in xc:
        copy.wait_recv()
    t = x_out[x].astype(F32)
    for d in range(NX - 1):
        t = t + x_in[d].astype(F32)
    lat_ref[0] = t[:, 0:LAT].astype(BF)
    kr_ref[0] = (t[:, LAT : LAT + RD] + t[:, LAT + RD :]).astype(BF)
    for copy in wc:
        copy.wait_recv()
    t = z_out[y].astype(F32)
    for d in range(NY - 1):
        t = t + w_in[d].astype(F32)
    wk_ref[...] = t[:, 0:256]
    wv_ref[...] = t[:, 256:512]
    for copy in sends:
        copy.wait_send()


def scatter(oq, lk, wg):
    return pl.pallas_call(
        scatter_kernel,
        out_shape=(
            jax.ShapeDtypeStruct((1, TOK, HEADS * HD), BF),
            jax.ShapeDtypeStruct((1, TOK, HEADS, HD), BF),
            jax.ShapeDtypeStruct((1, TOK, HEADS, RD), BF),
            jax.ShapeDtypeStruct((1, TOK, LAT), BF),
            jax.ShapeDtypeStruct((1, TOK, RD), BF),
            jax.ShapeDtypeStruct((16, 256), F32),
            jax.ShapeDtypeStruct((16, 256), F32),
        ),
        in_specs=[VM] * 3,
        out_specs=(VM,) * 7,
        scratch_shapes=[
            pltpu.VMEM((NCTX, TOK, PACK), BF),
            pltpu.VMEM((NY, NX, TOK, PACK), BF),
            pltpu.VMEM((NY, NX, TOK, PACK), BF),
            pltpu.VMEM((NY - 1, NX, TOK, PACK), BF),
            pltpu.VMEM((NX, TOK, PACK), BF),
            pltpu.VMEM((NX - 1, TOK, PACK), BF),
            pltpu.VMEM((NZ - 1, TOK, 512), BF),
            pltpu.VMEM((NY, 16, 512), BF),
            pltpu.VMEM((NY - 1, 16, 512), BF),
            pltpu.VMEM((8, 128), F32),
            DMA((7,)), DMA((7,)), DMA((4,)), DMA((4,)), DMA((3,)), DMA((3,)),
            DMA((3,)), DMA((3,)), DMA((7,)), DMA((7,)), DMA((3,)), DMA((3,)),
        ],
        compiler_params=pltpu.CompilerParams(
            collective_id=1, has_side_effects=True, vmem_limit_bytes=40 * 2**20
        ),
        name="scatter",
    )(
        oq.reshape(NCTX, TOK, PACK),
        lk.reshape(NX, NC, NY, TOK, PACK),
        wg.reshape(NZ, LAT // NZ, 512),
    )


def on_device(
    query_nope, query_rope, latent, key_rope, out_grad,
    key_weight, value_weight, block_doc, block_image, block_flag,
):
    q_all, lat_all = gather(query_nope, query_rope, out_grad, latent, key_rope)
    oq, lk, wg = attend(
        block_doc, block_image, block_flag,
        q_all.reshape(NQ, PACK), lat_all.reshape(NK, PACK), key_weight, value_weight,
    )
    return scatter(oq, lk, wg)


def solution(mesh):
    return jax.shard_map(
        on_device,
        mesh=mesh,
        in_specs=(
            P("dp", ("ctx", "seq"), None, None),
            P("dp", ("ctx", "seq"), None, None),
            P("dp", ("ctx", "seq"), None),
            P("dp", ("ctx", "seq"), None),
            P("dp", ("ctx", "seq"), None),
            P(None, "ctx"),
            P(None, "ctx"),
            P("dp", None),
            P("dp", None),
            P("dp", None),
        ),
        out_specs=(
            P("dp", ("ctx", "seq"), None),
            P("dp", ("ctx", "seq"), None, None),
            P("dp", ("ctx", "seq"), None, None),
            P("dp", ("ctx", "seq"), None),
            P("dp", ("ctx", "seq"), None),
            P(("dp", "seq"), "ctx"),
            P(("dp", "seq"), "ctx"),
        ),
        check_vma=False,
    )
```

```python
import math

import jax
import jax.numpy as jnp
from jax import lax
from jax.experimental import pallas as pl
from jax.experimental.pallas import tpu as pltpu
from jax.sharding import PartitionSpec as P

NEG = -1e30
MESH = pl.DeviceIdType.MESH
ANY = pl.BlockSpec(memory_space=pl.ANY)
DMA = pltpu.SemaphoreType.DMA
BF = jnp.bfloat16
F32 = jnp.float32

NX, NC, NY, NZ = 4, 2, 4, 8
NCTX = NX * NC
TOK, HEADS, HD, RD, LAT = 64, 16, 128, 64, 512
PACK = 640
NQ = NCTX * TOK
NK = NX * NC * NY * TOK
CHUNK = 256
NCH = NK // CHUNK
SCALE = 1.0 / math.sqrt(HD + RD)
SCALE2 = SCALE * math.log2(math.e)


def rc(src, dst, send, recv, dev):
    return pltpu.make_async_remote_copy(
        src_ref=src, dst_ref=dst, send_sem=send, recv_sem=recv, device_id=dev, device_id_type=MESH
    )


def dot(a, b):
    return jnp.dot(a, b, preferred_element_type=F32)


class Exchange:
    def __init__(self, src, dst, relay, ss, rs, sends):
        ctx = lax.axis_index("ctx")
        self.me = ctx
        x, k = ctx // NC, lax.rem(ctx, NC)
        self.right, self.left = lax.rem(x + 1, NX) * NC, lax.rem(x + NX - 1, NX) * NC
        self.far = lax.rem(x + 2, NX) * NC
        self.x, self.k = x * NC, k
        self.src, self.dst, self.mid = src, dst, relay
        self.ss, self.rs, self.sends = ss, rs, sends
        self.slots = {}

    def go(self, slot, src, dst, send, recv, to):
        copy = rc(src, dst, self.ss.at[send], self.rs.at[recv], {"ctx": to})
        copy.start()
        self.sends.append(copy)
        self.slots[slot] = copy

    def start_far(self):
        k = self.k
        self.go(7, self.src(self.far + k), self.mid.at[0], 5, 7, self.right + k)
        self.go(8, self.src(self.far + 1 - k), self.mid.at[1], 6, 8, self.left + k)

    def start_near(self):
        k, me = self.k, self.me
        for slot, to in (
            (1, self.right + k), (3, self.left + k),
            (2, self.right + 1 - k), (4, self.left + 1 - k),
            (0, self.x + 1 - k),
        ):
            self.go(slot, self.src(to), self.dst(me), slot, slot, to)

    def relay(self):
        k = self.k
        self.slots[7].wait_recv()
        self.go(5, self.mid.at[0], self.dst(self.left + k), 7, 5, self.right + k)
        self.slots[8].wait_recv()
        self.go(6, self.mid.at[1], self.dst(self.right + k), 8, 6, self.left + 1 - k)

    def finish(self):
        for slot in range(7):
            self.slots[slot].wait_recv()


def core_kernel(
    qn_h, qr_h, do_h, lat_h, kr_h, wk_h, wv_h, doc_h, img_h, flag_h,
    att_h, qng_h, qrg_h, latg_h, krg_h, wkg_h, wvg_h,
    att_ref, qng_ref, qrg_ref, latg_ref, krg_ref, wkg_ref, wvg_ref, rows_n, rows_r, outs,
    qn_v, qr_v, do_v, lat_v, kr_v, wk_v, wv_v, doc_ref, img_ref, flag_ref,
    comb, pack, q_all, q_mid, lat_all,
    w_all, w_t, lat_t, kc, kct, v, vt, qc, qct, dot_t, sc, gk, gv, o_t, dq_t,
    o_out, o_in, o_mid, d_out, d_in, d_mid,
    lk, sw_in, yb, y_mid, y_up, y_dn, xb, x_mid, x_up, x_dn,
    zk_out, zv_out, zk_in, zv_in, z_out, w_in,
    loc, xs, xr, us, ur, ds, dr, fs, fr, ws, wr,
    qs, qrs, os, ors, gs, grs, ss, sr, ys, yr, x2s, x2r, zks, zkr, zvs, zvr, w2s, w2r,
):
    ctx = lax.axis_index("ctx")
    y = lax.axis_index("seq")
    z = lax.axis_index("dp")
    x = ctx // NC
    k = lax.rem(ctx, NC)
    xu, xd, xo = lax.rem(x + 1, NX), lax.rem(x + NX - 1, NX), lax.rem(x + 2, NX)
    yu, yd, yo = lax.rem(y + 1, NY), lax.rem(y + NY - 1, NY), lax.rem(y + 2, NY)
    sib = {"ctx": x * NC + 1 - k}
    right, left = {"ctx": xu * NC + k}, {"ctx": xd * NC + k}
    up, down = {"seq": yu}, {"seq": yd}

    loads = []
    for n, (a, b) in enumerate((
        (lat_h, lat_v), (kr_h, kr_v), (qn_h, qn_v), (qr_h, qr_v), (do_h, do_v),
        (wk_h, wk_v), (wv_h, wv_v), (doc_h, doc_ref), (img_h, img_ref), (flag_h, flag_ref),
    )):
        loads.append(pltpu.make_async_copy(a, b, loc.at[n]))
        loads[-1].start()

    barrier = pltpu.get_barrier_semaphore()
    greet = [sib, right, left, {"ctx": xu * NC + 1 - k}, {"ctx": xd * NC + 1 - k}]
    greet += [{"seq": lax.rem(y + d, NY)} for d in range(1, NY)]
    greet += [{"dp": lax.rem(z + d, NZ)} for d in range(1, NZ)]
    for dev in greet:
        pl.semaphore_signal(barrier, inc=1, device_id=dev, device_id_type=MESH)
    loads[0].wait()
    loads[1].wait()
    comb[:, 0:LAT] = lat_v[0]
    comb[:, LAT : LAT + RD] = kr_v[0]
    comb[:, LAT + RD :] = kr_v[0]
    lat_all[x, k, y] = comb[...]
    pl.semaphore_wait(barrier, len(greet))
    sends = []

    def go(copy):
        copy.start()
        sends.append(copy)
        return copy

    mine = lat_all.at[x, k, y]
    xc = [go(rc(comb, mine, xs.at[0], xr.at[0], right)), go(rc(comb, mine, xs.at[1], xr.at[1], left))]
    ups = [go(rc(comb, mine, us.at[0], ur.at[0], up))]
    downs = [go(rc(comb, mine, ds.at[0], dr.at[0], down))]
    swaps = {0: go(rc(comb, mine, ws.at[0], wr.at[0], sib))}
    for n in range(2, 5):
        loads[n].wait()
    rows_n[...] = qn_v[0].astype(F32).reshape(TOK * HEADS, HD)
    rows_r[:, 0:RD] = qr_v[0].astype(F32).reshape(TOK * HEADS, RD)
    lane_t = lax.broadcasted_iota(jnp.int32, (TOK, 128), 1)

    def head(n):
        return pl.ds(n, TOK, stride=HEADS)

    for c in range(NCTX):
        for h in range(2):
            pack[c, :, h * 128 : (h + 1) * 128] = rows_n[head(2 * c + h), :].astype(BF)
        pack[c, :, 256:512] = do_v[0, :, c * 256 : (c + 1) * 256]
        pair = jnp.where(
            lane_t < RD, rows_r[head(2 * c), :], pltpu.roll(rows_r[head(2 * c + 1), :], RD, 1)
        )
        pack[c, :, 512:640] = pair.astype(BF)
    qx = Exchange(lambda c: pack.at[c], lambda c: q_all.at[c], q_mid, qs, qrs, sends)
    qx.start_far()

    half = TOK // 2
    blocks = (x, xd, xu, xo)

    def blk(e, yy):
        return lat_all.at[blocks[e], k, yy]

    def spread(e):
        b = blk(e, y)
        ups.append(go(rc(b, b, us.at[e], ur.at[e], up)))
        downs.append(go(rc(b, b, ds.at[e], dr.at[e], down)))
        swaps[e] = go(rc(b, b, ws.at[e], wr.at[e], sib))

    xc[0].wait_recv()
    b = lat_all.at[xd, k, y, pl.ds(0, half)]
    xc.append(go(rc(b, b, xs.at[2], xr.at[2], right)))
    xc[1].wait_recv()
    b = lat_all.at[xu, k, y, pl.ds(half, half)]
    xc.append(go(rc(b, b, xs.at[3], xr.at[3], left)))
    spread(1)
    spread(2)
    qx.start_near()
    q_all[ctx] = pack[ctx]
    for n in range(5, 7):
        loads[n].wait()
    w_all[:, 0:256] = wk_v[...]
    w_all[:, 256:512] = wv_v[...]
    w_t[...] = w_all[...].T
    xc[2].wait_recv()
    xc[3].wait_recv()
    spread(3)

    lane_k = lax.broadcasted_iota(jnp.int32, (CHUNK, 128), 1)
    row_k = lax.broadcasted_iota(jnp.int32, (128, CHUNK), 0)
    zero = jnp.zeros((), BF)

    def project(xx, kk):
        j = xx * NC + kk
        lat = lat_all[xx, kk, :, :, 0:LAT].reshape(CHUNK, LAT)
        kr = lat_all[xx, kk, :, :, LAT:PACK].reshape(CHUNK, 128)
        lt = lat.T
        lat_t[:, pl.ds(pl.multiple_of(j * CHUNK, CHUNK), CHUNK)] = lt
        kv = dot(lat, w_all[...]).astype(BF)
        kvt = dot(w_t[...], lt).astype(BF)
        krt = kr.T
        for h in range(2):
            kc[h, j, :, 0:128] = kv[:, h * 128 : (h + 1) * 128]
            kc[h, j, :, 128:256] = jnp.where((lane_k < RD) == (h == 0), kr, zero)
            kct[h, j, 0:128] = kvt[h * 128 : (h + 1) * 128]
            kct[h, j, 128:256] = jnp.where((row_k < RD) == (h == 0), krt, zero)
            v[h, j] = kv[:, 256 + h * 128 : 256 + (h + 1) * 128]
            vt[h, j] = kvt[256 + h * 128 : 256 + (h + 1) * 128]

    fwd = []
    for e in range(NX):
        ups[e].wait_recv()
        b = blk(e, yd)
        if e < 2:
            fwd.append(go(rc(b, b, fs.at[e], fr.at[e], up)))
        swaps[4 + e] = go(rc(b, b, ws.at[4 + e], wr.at[4 + e], sib))
        downs[e].wait_recv()
        b = blk(e, yu)
        if e >= 2:
            fwd.append(go(rc(b, b, fs.at[e], fr.at[e], down)))
        swaps[8 + e] = go(rc(b, b, ws.at[8 + e], wr.at[8 + e], sib))
        if e == 1:
            qx.relay()
        if e >= 2:
            n = e - 2
            fwd[n].wait_recv()
            b = blk(n, yo)
            swaps[12 + n] = go(rc(b, b, ws.at[12 + n], wr.at[12 + n], sib))
            project(blocks[n], k)
    for n in (2, 3):
        fwd[n].wait_recv()
        b = blk(n, yo)
        swaps[12 + n] = go(rc(b, b, ws.at[12 + n], wr.at[12 + n], sib))
        project(blocks[n], k)
    for e in range(NX):
        for slot in (e, 4 + e, 8 + e, 12 + e):
            swaps[slot].wait_recv()
        project(blocks[e], 1 - k)
    qx.finish()

    for h in range(2):
        for c in range(NCTX):
            r = slice(c * TOK, (c + 1) * TOK)
            qc[h, r, 0:128] = q_all[c, :, h * 128 : (h + 1) * 128]
            qc[h, r, 128:256] = q_all[c, :, 512:640]
        qct[h] = qc[h].T
        dot_t[h] = q_all[:, :, 256 + h * 128 : 256 + (h + 1) * 128].reshape(NQ, 128).T
    for n in range(7, 10):
        loads[n].wait()
    lane_q = lax.broadcasted_iota(jnp.int32, (1, NQ), 1)
    grp = lane_q // TOK
    qdoc = jnp.zeros((1, NQ), jnp.int32)
    qcode = jnp.zeros((1, NQ), jnp.int32)
    for c in range(NCTX):
        b = NY * c + y
        qdoc = jnp.where(grp == c, doc_ref[0, b], qdoc)
        code = jnp.where(flag_ref[0, b] == 1, doc_ref[0, b] * 64 + img_ref[0, b], -1)
        qcode = jnp.where(grp == c, code, qcode)
    qpos = (NY * grp + y) * TOK + lane_q % TOK
    sub = lax.broadcasted_iota(jnp.int32, (TOK, 1), 0)

    spans = []
    for j in range(NCH):
        lo = max(0, j - 1) // 2 * 2
        hi = min(NCTX, (min(NCTX, j + 5) + 1) // 2 * 2)
        spans.append((lo * TOK, hi * TOK))

    def splice(full, part, a, b):
        pieces = [full[:, 0:a]] if a else []
        pieces.append(part)
        if b < NQ:
            pieces.append(full[:, b:])
        return jnp.concatenate(pieces, axis=1) if len(pieces) > 1 else part

    neg = jnp.full((1, NQ), NEG, F32)
    mx = [neg, neg]
    for j in range(NCH):
        a, b = spans[j]
        thr = []
        for i in range(CHUNK // TOK):
            kb = j * (CHUNK // TOK) + i
            kcode = jnp.where(flag_ref[0, kb] == 1, doc_ref[0, kb] * 64 + img_ref[0, kb], -2)
            t = jnp.where(qdoc[:, a:b] == doc_ref[0, kb], qpos[:, a:b] - kb * TOK, -1)
            thr.append(jnp.where(qcode[:, a:b] == kcode, NK, t))
        for h in range(2):
            raw = dot(kc[h, j], qct[h, :, a:b])
            part = None
            for i in range(CHUNK // TOK):
                rows = slice(i * TOK, (i + 1) * TOK)
                m = jnp.where(sub <= thr[i], raw[rows] * SCALE2, NEG)
                sc[h, j * CHUNK + i * TOK : j * CHUNK + (i + 1) * TOK, a:b] = m
                top = jnp.max(m, axis=0, keepdims=True)
                part = top if part is None else jnp.maximum(part, top)
            mx[h] = splice(mx[h], jnp.maximum(mx[h][:, a:b], part), a, b)

    tot = [jnp.zeros((1, NQ), F32)] * 2
    o_t[...] = jnp.zeros_like(o_t)
    dq_t[...] = jnp.zeros_like(dq_t)
    for j in range(NCH):
        a, b = spans[j]
        r = slice(j * CHUNK, (j + 1) * CHUNK)
        for h in range(2):
            p = jnp.exp2(sc[h, r, a:b] - mx[h][:, a:b])
            sc[h, r, a:b] = p
            tot[h] = splice(tot[h], tot[h][:, a:b] + jnp.sum(p, axis=0, keepdims=True), a, b)
            o_t[h, :, a:b] += dot(vt[h, j], p.astype(BF))
    inv = [1.0 / tot[h] for h in range(2)]
    delta = []
    for h in range(2):
        out = o_t[h] * inv[h]
        o_out[:, :, h * 128 : (h + 1) * 128] = out.T.astype(BF).reshape(NCTX, TOK, 128)
        delta.append(jnp.sum(out * dot_t[h].astype(F32), axis=0, keepdims=True))
    ox = Exchange(lambda c: o_out.at[c], lambda c: o_in.at[c], o_mid, os, ors, sends)
    ox.start_far()
    ox.start_near()
    o_in[ctx] = o_out[ctx]

    for j in range(NCH):
        a, b = spans[j]
        r = slice(j * CHUNK, (j + 1) * CHUNK)
        for h in range(2):
            p = sc[h, r, a:b] * inv[h][:, a:b]
            sc[h, r, a:b] = p
            do = q_all[a // TOK : b // TOK, :, 256 + h * 128 : 256 + (h + 1) * 128].reshape(b - a, 128)
            gv[r, h * 128 : (h + 1) * 128] = dot(p.astype(BF), do).astype(BF)

    def weight_grad(buf, g):
        for i in range(2):
            part = dot(lat_t[i * 256 : (i + 1) * 256, :], g[...]).astype(BF)
            buf[i * 4 : (i + 1) * 4] = part.reshape(4, TOK, 256)

    def send_z(buf, inbox, s_sem, r_sem):
        out = []
        for d in (4, 3, 5, 2, 6, 1, 7):
            to = lax.rem(z + d, NZ)
            out.append(go(rc(buf.at[to], inbox.at[d - 1], s_sem.at[d - 1], r_sem.at[d - 1], {"dp": to})))
        return out

    weight_grad(zv_out, gv)
    zv = send_z(zv_out, zv_in, zvs, zvr)

    swc = []
    ycp = {}

    def merge(xx):
        swc[xx].wait_recv()

        def add(i, carry):
            yb[xx, i] = (lk[xx, k, i].astype(F32) + sw_in[xx, i].astype(F32)).astype(BF)
            return carry

        lax.fori_loop(0, NY, add, 0)

    lo2, hi2 = pl.ds(0, 2), pl.ds(2, 2)
    for j in range(NCH):
        a, b = spans[j]
        r = slice(j * CHUNK, (j + 1) * CHUNK)
        kr_g = []
        for h in range(2):
            dp = dot(v[h, j], dot_t[h, :, a:b])
            g = (sc[h, r, a:b] * (dp - delta[h][:, a:b])).astype(BF)
            dk = dot(g, qc[h, a:b, :]) * SCALE
            dq_t[h, :, a:b] += dot(kct[h, j], g)
            gk[r, h * 128 : (h + 1) * 128] = dk[:, 0:128].astype(BF)
            kr_g.append(dk[:, 128:256])
        xx, kk = j // NC, j % NC
        kr_part = jnp.where(lane_k < RD, kr_g[0], kr_g[1]).astype(BF)
        lk[xx, kk, :, :, LAT:PACK] = kr_part.reshape(NY, TOK, 128)
        lat_part = (dot(gk[r, :], w_t[0:256, :]) + dot(gv[r, :], w_t[256:512, :])).astype(BF)
        lk[xx, kk, :, :, 0:LAT] = lat_part.reshape(NY, TOK, LAT)
        if kk == 1:
            swc.append(go(rc(lk.at[xx, 1 - k], sw_in.at[xx], ss.at[xx], sr.at[xx], sib)))
        if j == 2:
            ox.relay()
        if j == 4:
            merge(0)
        if j == 5:
            merge(1)
            ycp[0] = go(rc(yb.at[lo2, yo], y_mid.at[0], ys.at[0], yr.at[0], up))
            ycp[1] = go(rc(yb.at[lo2, yd], y_dn.at[lo2], ys.at[1], yr.at[1], down))
    d_cols = [(dq_t[h, 0:128, :] * SCALE).T.astype(BF) for h in range(2)]
    d_cols.append(((dq_t[0, 128:256, :] + dq_t[1, 128:256, :]) * SCALE).T.astype(BF))
    for n in range(3):
        d_out[:, :, n * 128 : (n + 1) * 128] = d_cols[n].reshape(NCTX, TOK, 128)
    dx = Exchange(lambda c: d_out.at[c], lambda c: d_in.at[c], d_mid, gs, grs, sends)
    dx.start_far()
    dx.start_near()
    d_in[ctx] = d_out[ctx]
    weight_grad(zk_out, gk)
    zk = send_z(zk_out, zk_in, zks, zkr)
    merge(2)
    merge(3)
    ycp[2] = go(rc(yb.at[hi2, yo], y_mid.at[1], ys.at[2], yr.at[2], down))
    ycp[3] = go(rc(yb.at[hi2, yu], y_up.at[hi2], ys.at[3], yr.at[3], up))
    ycp[0].wait_recv()
    for i in range(2):
        yb[i, yu] = (yb[i, yu].astype(F32) + y_mid[0, i].astype(F32)).astype(BF)
    ycp[4] = go(rc(yb.at[lo2, yu], y_up.at[lo2], ys.at[4], yr.at[4], up))
    dx.relay()
    ycp[2].wait_recv()
    for i in range(2):
        yb[2 + i, yd] = (yb[2 + i, yd].astype(F32) + y_mid[1, i].astype(F32)).astype(BF)
    ycp[5] = go(rc(yb.at[hi2, yd], y_dn.at[hi2], ys.at[5], yr.at[5], down))

    ox.finish()
    results = []

    def put(n, a, b):
        results.append(pltpu.make_async_copy(a, b, outs.at[n]))
        results[-1].start()

    for c in range(NCTX):
        att_ref[0, :, c * 256 : (c + 1) * 256] = o_in[c]
    put(0, att_ref, att_h)
    for n in (1, 3, 4, 5):
        ycp[n].wait_recv()

    def total_y(i, carry):
        t = yb[i, y].astype(F32) + y_up[i].astype(F32) + y_dn[i].astype(F32)
        xb[i] = t.astype(BF)
        return carry

    lax.fori_loop(0, NX, total_y, 0)
    top, bot = pl.ds(0, half), pl.ds(half, half)
    xcp = {}
    xcp[0] = go(rc(xb.at[xo, top], x_mid.at[0], x2s.at[0], x2r.at[0], right))
    xcp[1] = go(rc(xb.at[xo, bot], x_mid.at[1], x2s.at[1], x2r.at[1], left))
    xcp[2] = go(rc(xb.at[xu, bot], x_up.at[bot], x2s.at[2], x2r.at[2], right))
    xcp[3] = go(rc(xb.at[xd, top], x_dn.at[top], x2s.at[3], x2r.at[3], left))
    for copy in zv:
        copy.wait_recv()

    def total_z(buf, inbox):
        t = buf[z].astype(F32)
        for d in range(NZ - 1):
            t = t + inbox[d].astype(F32)
        return t.astype(BF).reshape(NY, 16, 256)

    z_out[:, :, 256:512] = total_z(zv_out, zv_in)
    xcp[0].wait_recv()
    xb[xu, top] = (xb[xu, top].astype(F32) + x_mid[0].astype(F32)).astype(BF)
    xcp[4] = go(rc(xb.at[xu, top], x_up.at[top], x2s.at[4], x2r.at[4], right))
    xcp[1].wait_recv()
    xb[xd, bot] = (xb[xd, bot].astype(F32) + x_mid[1].astype(F32)).astype(BF)
    xcp[5] = go(rc(xb.at[xd, bot], x_dn.at[bot], x2s.at[5], x2r.at[5], left))
    for copy in zk:
        copy.wait_recv()
    z_out[:, :, 0:256] = total_z(zk_out, zk_in)
    wc = []
    for d in range(1, NY):
        to = lax.rem(y + d, NY)
        wc.append(go(rc(z_out.at[to], w_in.at[d - 1], w2s.at[d - 1], w2r.at[d - 1], {"seq": to})))
    dx.finish()
    for c in range(NCTX):
        for h in range(2):
            rows_n[head(2 * c + h), :] = d_in[c, :, h * 128 : (h + 1) * 128].astype(F32)
        pair = d_in[c, :, 256:384].astype(F32)
        rows_r[head(2 * c), :] = pair
        rows_r[head(2 * c + 1), :] = pltpu.roll(pair, RD, 1)
    qng_ref[0] = rows_n[...].reshape(TOK, HEADS, HD).astype(BF)
    qrg_ref[0] = rows_r[:, 0:RD].reshape(TOK, HEADS, RD).astype(BF)
    put(1, qng_ref, qng_h)
    put(2, qrg_ref, qrg_h)
    for n in range(2, 6):
        xcp[n].wait_recv()
    t = xb[x].astype(F32) + x_up[...].astype(F32) + x_dn[...].astype(F32)
    latg_ref[0] = t[:, 0:LAT].astype(BF)
    krg_ref[0] = (t[:, LAT : LAT + RD] + t[:, LAT + RD :]).astype(BF)
    put(3, latg_ref, latg_h)
    put(4, krg_ref, krg_h)
    for copy in wc:
        copy.wait_recv()
    t = z_out[y].astype(F32)
    for d in range(NY - 1):
        t = t + w_in[d].astype(F32)
    wkg_ref[...] = t[:, 0:256]
    wvg_ref[...] = t[:, 256:512]
    put(5, wkg_ref, wkg_h)
    put(6, wvg_ref, wvg_h)
    for copy in sends:
        copy.wait_send()
    for copy in results:
        copy.wait()


OUTS = (
    ((1, TOK, HEADS * HD), BF),
    ((1, TOK, HEADS, HD), BF),
    ((1, TOK, HEADS, RD), BF),
    ((1, TOK, LAT), BF),
    ((1, TOK, RD), BF),
    ((16, 256), F32),
    ((16, 256), F32),
)


def core(*args):
    def vm(*shape, dtype=BF):
        return pltpu.VMEM(shape, dtype)

    table = pltpu.SMEM((1, NX * NC * NY), jnp.int32)
    return pl.pallas_call(
        core_kernel,
        out_shape=tuple(jax.ShapeDtypeStruct(s, d) for s, d in OUTS),
        in_specs=[ANY] * 10,
        out_specs=(ANY,) * 7,
        scratch_shapes=[
            *(pltpu.VMEM(s, d) for s, d in OUTS),
            vm(TOK * HEADS, 128, dtype=F32), vm(TOK * HEADS, 128, dtype=F32), DMA((7,)),
            vm(1, TOK, HEADS, HD), vm(1, TOK, HEADS, RD), vm(1, TOK, HEADS * HD),
            vm(1, TOK, LAT), vm(1, TOK, RD), vm(LAT, 256), vm(LAT, 256),
            table, table, table,
            vm(TOK, PACK), vm(NCTX, TOK, PACK), vm(NCTX, TOK, PACK), vm(2, TOK, PACK),
            vm(NX, NC, NY, TOK, PACK),
            vm(LAT, 512), vm(512, LAT), vm(LAT, NK),
            vm(2, NCH, CHUNK, 256), vm(2, NCH, 256, CHUNK),
            vm(2, NCH, CHUNK, 128), vm(2, NCH, 128, CHUNK),
            vm(2, NQ, 256), vm(2, 256, NQ), vm(2, 128, NQ),
            vm(2, NK, NQ, dtype=F32), vm(NK, 256), vm(NK, 256),
            vm(2, 128, NQ, dtype=F32), vm(2, 256, NQ, dtype=F32),
            vm(NCTX, TOK, 256), vm(NCTX, TOK, 256), vm(2, TOK, 256),
            vm(NCTX, TOK, 384), vm(NCTX, TOK, 384), vm(2, TOK, 384),
            vm(NX, NC, NY, TOK, PACK), vm(NX, NY, TOK, PACK), vm(NX, NY, TOK, PACK),
            vm(2, 2, TOK, PACK), vm(NX, TOK, PACK), vm(NX, TOK, PACK),
            vm(NX, TOK, PACK), vm(2, TOK // 2, PACK), vm(TOK, PACK), vm(TOK, PACK),
            vm(NZ, TOK, 256), vm(NZ, TOK, 256), vm(NZ - 1, TOK, 256), vm(NZ - 1, TOK, 256),
            vm(NY, 16, 512), vm(NY - 1, 16, 512),
            DMA((10,)), DMA((4,)), DMA((4,)), DMA((4,)), DMA((4,)), DMA((4,)), DMA((4,)),
            DMA((4,)), DMA((4,)), DMA((16,)), DMA((16,)),
            DMA((9,)), DMA((9,)), DMA((9,)), DMA((9,)), DMA((9,)), DMA((9,)),
            DMA((4,)), DMA((4,)), DMA((6,)), DMA((6,)), DMA((6,)), DMA((6,)),
            DMA((7,)), DMA((7,)), DMA((7,)), DMA((7,)), DMA((3,)), DMA((3,)),
        ],
        compiler_params=pltpu.CompilerParams(
            collective_id=0, has_side_effects=True, vmem_limit_bytes=60 * 2**20
        ),
        name="core",
    )(*args)


def store_kernel(*refs):
    src, dst, mid, lsem, ssem = refs[0:7], refs[7:14], refs[14:21], refs[21], refs[22]
    reads = [pltpu.make_async_copy(src[n], mid[n], lsem.at[n]) for n in range(7)]
    writes = [pltpu.make_async_copy(mid[n], dst[n], ssem.at[n]) for n in range(7)]
    for copy in reads:
        copy.start()
    for n in range(7):
        reads[n].wait()
        writes[n].start()
    for copy in writes:
        copy.wait()


def store(*arrays):
    return pl.pallas_call(
        store_kernel,
        out_shape=tuple(jax.ShapeDtypeStruct(s, d) for s, d in OUTS),
        in_specs=[ANY] * 7,
        out_specs=(ANY,) * 7,
        scratch_shapes=[*(pltpu.VMEM(s, d) for s, d in OUTS), DMA((7,)), DMA((7,))],
        compiler_params=pltpu.CompilerParams(vmem_limit_bytes=60 * 2**20),
        name="store",
    )(*arrays)


def on_device(
    query_nope, query_rope, latent, key_rope, out_grad,
    key_weight, value_weight, block_doc, block_image, block_flag,
):
    return store(*core(
        query_nope, query_rope, out_grad, latent, key_rope,
        key_weight, value_weight, block_doc, block_image, block_flag,
    ))


def solution(mesh):
    return jax.shard_map(
        on_device,
        mesh=mesh,
        in_specs=(
            P("dp", ("ctx", "seq"), None, None),
            P("dp", ("ctx", "seq"), None, None),
            P("dp", ("ctx", "seq"), None),
            P("dp", ("ctx", "seq"), None),
            P("dp", ("ctx", "seq"), None),
            P(None, "ctx"),
            P(None, "ctx"),
            P("dp", None),
            P("dp", None),
            P("dp", None),
        ),
        out_specs=(
            P("dp", ("ctx", "seq"), None),
            P("dp", ("ctx", "seq"), None, None),
            P("dp", ("ctx", "seq"), None, None),
            P("dp", ("ctx", "seq"), None),
            P("dp", ("ctx", "seq"), None),
            P(("dp", "seq"), "ctx"),
            P(("dp", "seq"), "ctx"),
        ),
        check_vma=False,
    )
```

```python
import math

import jax
import jax.numpy as jnp
from jax import lax
from jax.experimental import pallas as pl
from jax.experimental.pallas import tpu as pltpu
from jax.sharding import PartitionSpec as P

NEG = -1e30
MESH = pl.DeviceIdType.MESH
ANY = pl.BlockSpec(memory_space=pl.ANY)
DMA = pltpu.SemaphoreType.DMA
BF = jnp.bfloat16
F32 = jnp.float32

NX, NC, NY, NZ = 4, 2, 4, 8
NCTX = NX * NC
TOK, HEADS, HD, RD, LAT = 64, 16, 128, 64, 512
PACK = 640
NQ = NCTX * TOK
NK = NX * NC * NY * TOK
CHUNK = 256
NCH = NK // CHUNK
SCALE = 1.0 / math.sqrt(HD + RD)
SCALE2 = SCALE * math.log2(math.e)


def rc(src, dst, send, recv, dev):
    return pltpu.make_async_remote_copy(
        src_ref=src, dst_ref=dst, send_sem=send, recv_sem=recv, device_id=dev, device_id_type=MESH
    )


def dot(a, b):
    return jnp.dot(a, b, preferred_element_type=F32)


class Exchange:
    def __init__(self, src, dst, relay, ss, rs, sends):
        ctx = lax.axis_index("ctx")
        self.me = ctx
        x, k = ctx // NC, lax.rem(ctx, NC)
        self.right, self.left = lax.rem(x + 1, NX) * NC, lax.rem(x + NX - 1, NX) * NC
        self.far = lax.rem(x + 2, NX) * NC
        self.x, self.k = x * NC, k
        self.src, self.dst, self.mid = src, dst, relay
        self.ss, self.rs, self.sends = ss, rs, sends
        self.slots = {}

    def go(self, slot, src, dst, send, recv, to):
        copy = rc(src, dst, self.ss.at[send], self.rs.at[recv], {"ctx": to})
        copy.start()
        self.sends.append(copy)
        self.slots[slot] = copy

    def start_far(self):
        k = self.k
        self.go(7, self.src(self.far + k), self.mid.at[0], 5, 7, self.right + k)
        self.go(8, self.src(self.far + 1 - k), self.mid.at[1], 6, 8, self.left + k)

    def start_near(self):
        k, me = self.k, self.me
        for slot, to in (
            (1, self.right + k), (3, self.left + k),
            (2, self.right + 1 - k), (4, self.left + 1 - k),
            (0, self.x + 1 - k),
        ):
            self.go(slot, self.src(to), self.dst(me), slot, slot, to)

    def relay(self):
        k = self.k
        self.slots[7].wait_recv()
        self.go(5, self.mid.at[0], self.dst(self.left + k), 7, 5, self.right + k)
        self.slots[8].wait_recv()
        self.go(6, self.mid.at[1], self.dst(self.right + k), 8, 6, self.left + 1 - k)

    def finish(self):
        for slot in range(7):
            self.slots[slot].wait_recv()


def core_kernel(
    qn_h, qr_h, do_h, lat_h, kr_h, wk_h, wv_h, doc_h, img_h, flag_h,
    att_h, qng_h, qrg_h, latg_h, krg_h, wkg_h, wvg_h,
    att_ref, qng_ref, qrg_ref, latg_ref, krg_ref, wkg_ref, wvg_ref, rows_n, rows_r, outs,
    qn_v, qr_v, do_v, lat_v, kr_v, wk_v, wv_v, doc_ref, img_ref, flag_ref,
    comb, pack, q_all, q_mid, lat_all,
    w_all, w_t, lat_t, kc, kct, v, vt, qc, qct, dot_t, sc, pb, mj, gs_b, gk, gv, o_t, dq_t,
    o_out, o_in, o_mid, d_out, d_in, d_mid,
    lk, sw_in, yb, y_mid, y_up, y_dn, xb, x_mid, x_up, x_dn,
    zk_out, zv_out, zk_in, zv_in, z_out, w_in,
    loc, xs, xr, us, ur, ds, dr, fs, fr, ws, wr,
    qs, qrs, os, ors, gs, grs, ss, sr, ys, yr, x2s, x2r,
    zks, zkr, zvs, zvr, w2s, w2r,
):
    ctx = lax.axis_index("ctx")
    y = lax.axis_index("seq")
    z = lax.axis_index("dp")
    x = ctx // NC
    k = lax.rem(ctx, NC)
    xu, xd, xo = lax.rem(x + 1, NX), lax.rem(x + NX - 1, NX), lax.rem(x + 2, NX)
    yu, yd, yo = lax.rem(y + 1, NY), lax.rem(y + NY - 1, NY), lax.rem(y + 2, NY)
    sib = {"ctx": x * NC + 1 - k}
    right, left = {"ctx": xu * NC + k}, {"ctx": xd * NC + k}
    up, down = {"seq": yu}, {"seq": yd}

    loads = []
    for n, (a, b) in enumerate((
        (lat_h, lat_v), (kr_h, kr_v), (qn_h, qn_v), (qr_h, qr_v), (do_h, do_v),
        (wk_h, wk_v), (wv_h, wv_v), (doc_h, doc_ref), (img_h, img_ref), (flag_h, flag_ref),
    )):
        loads.append(pltpu.make_async_copy(a, b, loc.at[n]))
        loads[-1].start()

    barrier = pltpu.get_barrier_semaphore()
    greet = [{"ctx": lax.rem(ctx + d, NCTX)} for d in range(1, NCTX)]
    greet += [{"seq": lax.rem(y + d, NY)} for d in range(1, NY)]
    greet += [{"dp": lax.rem(z + d, NZ)} for d in range(1, NZ)]
    for dev in greet:
        pl.semaphore_signal(barrier, inc=1, device_id=dev, device_id_type=MESH)
    loads[0].wait()
    loads[1].wait()
    comb[:, 0:LAT] = lat_v[0]
    comb[:, LAT : LAT + RD] = kr_v[0]
    comb[:, LAT + RD :] = kr_v[0]
    lat_all[x, k, y] = comb[...]
    for n in range(2, 5):
        loads[n].wait()
    rows_n[...] = qn_v[0].astype(F32).reshape(TOK * HEADS, HD)
    rows_r[:, 0:RD] = qr_v[0].astype(F32).reshape(TOK * HEADS, RD)
    lane_t = lax.broadcasted_iota(jnp.int32, (TOK, 128), 1)

    def head(n):
        return pl.ds(n, TOK, stride=HEADS)

    for c in range(NCTX):
        for h in range(2):
            pack[c, :, h * 128 : (h + 1) * 128] = rows_n[head(2 * c + h), :].astype(BF)
        pack[c, :, 256:512] = do_v[0, :, c * 256 : (c + 1) * 256]
        pair = jnp.where(
            lane_t < RD, rows_r[head(2 * c), :], pltpu.roll(rows_r[head(2 * c + 1), :], RD, 1)
        )
        pack[c, :, 512:640] = pair.astype(BF)
    q_all[ctx] = pack[ctx]
    for n in range(5, 10):
        loads[n].wait()
    w_all[:, 0:256] = wk_v[...]
    w_all[:, 256:512] = wv_v[...]
    w_t[...] = w_all[...].T
    o_t[...] = jnp.zeros_like(o_t)
    dq_t[...] = jnp.zeros_like(dq_t)

    lane_q = lax.broadcasted_iota(jnp.int32, (1, NQ), 1)
    grp = lane_q // TOK
    qdoc = jnp.zeros((1, NQ), jnp.int32)
    qcode = jnp.zeros((1, NQ), jnp.int32)
    for c in range(NCTX):
        b = NY * c + y
        qdoc = jnp.where(grp == c, doc_ref[0, b], qdoc)
        code = jnp.where(flag_ref[0, b] == 1, doc_ref[0, b] * 64 + img_ref[0, b], -1)
        qcode = jnp.where(grp == c, code, qcode)
    qpos = (NY * grp + y) * TOK + lane_q % TOK
    sub = lax.broadcasted_iota(jnp.int32, (TOK, 1), 0)
    lane_k = lax.broadcasted_iota(jnp.int32, (CHUNK, 128), 1)
    row_k = lax.broadcasted_iota(jnp.int32, (128, CHUNK), 0)
    zero = jnp.zeros((), BF)

    pl.semaphore_wait(barrier, len(greet))
    sends = []

    def go(copy):
        copy.start()
        sends.append(copy)
        return copy

    mine = lat_all.at[x, k, y]
    xc = [go(rc(comb, mine, xs.at[0], xr.at[0], right)), go(rc(comb, mine, xs.at[1], xr.at[1], left))]
    ups = [go(rc(comb, mine, us.at[0], ur.at[0], up))]
    downs = [go(rc(comb, mine, ds.at[0], dr.at[0], down))]
    swaps = {0: go(rc(comb, mine, ws.at[0], wr.at[0], sib))}
    qx = Exchange(lambda c: pack.at[c], lambda c: q_all.at[c], q_mid, qs, qrs, sends)
    qx.start_far()
    half = TOK // 2
    top_r, bot_r = pl.ds(0, half), pl.ds(half, half)
    blocks = (x, xd, xu, xo)

    def blk(e, yy):
        return lat_all.at[blocks[e], k, yy]

    def swap(slot, b):
        swaps[slot] = go(rc(b, b, ws.at[slot], wr.at[slot], sib))

    def spread(e):
        b = blk(e, y)
        ups.append(go(rc(b, b, us.at[e], ur.at[e], up)))
        downs.append(go(rc(b, b, ds.at[e], dr.at[e], down)))
        swap(e, b)

    fwd = []

    def onward(e):
        ups[e].wait_recv()
        b = blk(e, yd)
        if e < 2:
            fwd.append(go(rc(b, b, fs.at[e], fr.at[e], up)))
        swap(4 + e, b)
        downs[e].wait_recv()
        b = blk(e, yu)
        if e >= 2:
            fwd.append(go(rc(b, b, fs.at[e], fr.at[e], down)))
        swap(8 + e, b)

    def last(e):
        fwd[e].wait_recv()
        swap(12 + e, blk(e, yo))

    def project(xx, kk):
        j = xx * NC + kk
        lat = lat_all[xx, kk, :, :, 0:LAT].reshape(CHUNK, LAT)
        kr = lat_all[xx, kk, :, :, LAT:PACK].reshape(CHUNK, 128)
        lt = lat.T
        lat_t[:, pl.ds(pl.multiple_of(j * CHUNK, CHUNK), CHUNK)] = lt
        kv = dot(lat, w_all[...]).astype(BF)
        kvt = dot(w_t[...], lt).astype(BF)
        krt = kr.T
        for h in range(2):
            kc[h, j, :, 0:128] = kv[:, h * 128 : (h + 1) * 128]
            kc[h, j, :, 128:256] = jnp.where((lane_k < RD) == (h == 0), kr, zero)
            kct[h, j, 0:128] = kvt[h * 128 : (h + 1) * 128]
            kct[h, j, 128:256] = jnp.where((row_k < RD) == (h == 0), krt, zero)
            v[h, j] = kv[:, 256 + h * 128 : 256 + (h + 1) * 128]
            vt[h, j] = kvt[256 + h * 128 : 256 + (h + 1) * 128]

    def queries():
        qx.finish()
        for h in range(2):
            for c in range(NCTX):
                r = slice(c * TOK, (c + 1) * TOK)
                qc[h, r, 0:128] = q_all[c, :, h * 128 : (h + 1) * 128]
                qc[h, r, 128:256] = q_all[c, :, 512:640]
            qct[h] = qc[h].T
            dot_t[h] = q_all[:, :, 256 + h * 128 : 256 + (h + 1) * 128].reshape(NQ, 128).T

    neg = jnp.full((1, NQ), NEG, F32)
    mx = [neg, neg]
    tot = [jnp.zeros((1, NQ), F32)] * 2

    def soften(xx, kk):
        j = xx * NC + kk
        thr = []
        for i in range(CHUNK // TOK):
            kb = j * (CHUNK // TOK) + i
            kcode = jnp.where(flag_ref[0, kb] == 1, doc_ref[0, kb] * 64 + img_ref[0, kb], -2)
            t = jnp.where(qdoc == doc_ref[0, kb], qpos - kb * TOK, -1)
            thr.append(jnp.where(qcode == kcode, NK, t))
        for h in range(2):
            raw = dot(kc[h, j], qct[h])
            top = None
            masked = []
            for i in range(CHUNK // TOK):
                m = jnp.where(sub <= thr[i], raw[i * TOK : (i + 1) * TOK] * SCALE2, NEG)
                masked.append(m)
                one = jnp.max(m, axis=0, keepdims=True)
                top = one if top is None else jnp.maximum(top, one)
            part = None
            for i in range(CHUNK // TOK):
                p = jnp.exp2(masked[i] - top)
                sc[h, j, i * TOK : (i + 1) * TOK, :] = p
                pb[h, i * TOK : (i + 1) * TOK, :] = p.astype(BF)
                one = jnp.sum(p, axis=0, keepdims=True)
                part = one if part is None else part + one
            mj[h, j] = top
            new = jnp.maximum(mx[h], top)
            old_f, new_f = jnp.exp2(mx[h] - new), jnp.exp2(top - new)
            o_t[h] = o_t[h] * old_f + dot(vt[h, j], pb[h]) * new_f
            tot[h] = tot[h] * old_f + part * new_f
            mx[h] = new

    xc[0].wait_recv()
    b = lat_all.at[xd, k, y, top_r]
    xc.append(go(rc(b, b, xs.at[2], xr.at[2], right)))
    xc[1].wait_recv()
    b = lat_all.at[xu, k, y, bot_r]
    xc.append(go(rc(b, b, xs.at[3], xr.at[3], left)))
    spread(1)
    spread(2)
    qx.start_near()
    onward(0)
    xc[2].wait_recv()
    xc[3].wait_recv()
    spread(3)
    qx.relay()
    onward(1)
    last(0)
    project(blocks[0], k)
    onward(2)
    onward(3)
    last(1)
    project(blocks[1], k)
    queries()
    soften(blocks[0], k)
    last(2)
    last(3)
    soften(blocks[1], k)
    for e in (2, 3):
        project(blocks[e], k)
        soften(blocks[e], k)
    for e in range(NX):
        for slot in (e, 4 + e, 8 + e, 12 + e):
            swaps[slot].wait_recv()
        project(blocks[e], 1 - k)
        soften(blocks[e], 1 - k)

    spans = []
    for j in range(NCH):
        lo = max(0, j - 1) // 2 * 2
        hi = min(NCTX, (min(NCTX, j + 5) + 1) // 2 * 2)
        spans.append((lo * TOK, hi * TOK))
    inv = [1.0 / tot[h] for h in range(2)]
    delta = []
    for h in range(2):
        out = o_t[h] * inv[h]
        o_out[:, :, h * 128 : (h + 1) * 128] = out.T.astype(BF).reshape(NCTX, TOK, 128)
        delta.append(jnp.sum(out * dot_t[h].astype(F32), axis=0, keepdims=True))
    ox = Exchange(lambda c: o_out.at[c], lambda c: o_in.at[c], o_mid, os, ors, sends)
    ox.start_far()
    ox.start_near()
    o_in[ctx] = o_out[ctx]

    for j in range(NCH):
        a, b = spans[j]
        r = slice(j * CHUNK, (j + 1) * CHUNK)
        for h in range(2):
            f = jnp.exp2(mj[h, j] - mx[h]) * inv[h]
            p = sc[h, j, :, a:b] * f[:, a:b]
            do = q_all[a // TOK : b // TOK, :, 256 + h * 128 : 256 + (h + 1) * 128].reshape(b - a, 128)
            gv[r, h * 128 : (h + 1) * 128] = dot(p.astype(BF), do).astype(BF)
            dp = dot(v[h, j], dot_t[h, :, a:b])
            g = (p * (dp - delta[h][:, a:b])).astype(BF)
            gs_b[h, j, :, a:b] = g
            dq_t[h, :, a:b] += dot(kct[h, j], g)
    d_cols = [(dq_t[h, 0:128, :] * SCALE).T.astype(BF) for h in range(2)]
    d_cols.append(((dq_t[0, 128:256, :] + dq_t[1, 128:256, :]) * SCALE).T.astype(BF))
    for n in range(3):
        d_out[:, :, n * 128 : (n + 1) * 128] = d_cols[n].reshape(NCTX, TOK, 128)
    dx = Exchange(lambda c: d_out.at[c], lambda c: d_in.at[c], d_mid, gs, grs, sends)
    dx.start_far()
    dx.start_near()
    d_in[ctx] = d_out[ctx]
    ox.relay()

    def weight_grad(buf, g):
        for i in range(2):
            part = dot(lat_t[i * 256 : (i + 1) * 256, :], g[...]).astype(BF)
            buf[i * 4 : (i + 1) * 4] = part.reshape(4, TOK, 256)

    def send_z(buf, inbox, s_sem, r_sem):
        out = []
        for d in (4, 3, 5, 2, 6, 1, 7):
            to = lax.rem(z + d, NZ)
            out.append(go(rc(buf.at[to], inbox.at[d - 1], s_sem.at[d - 1], r_sem.at[d - 1], {"dp": to})))
        return out

    weight_grad(zv_out, gv)
    zv = send_z(zv_out, zv_in, zvs, zvr)

    swc = []
    yc = {}

    def merge(xx):
        swc[xx].wait_recv()

        def add(i, carry):
            yb[xx, i] = (lk[xx, k, i].astype(F32) + sw_in[xx, i].astype(F32)).astype(BF)
            return carry

        lax.fori_loop(0, NY, add, 0)
        far, near, box, back = (up, down, y_dn, yd) if xx % 2 == 0 else (down, up, y_up, yu)
        yc[xx, 0] = go(rc(yb.at[xx, yo], y_mid.at[xx], ys.at[xx, 0], yr.at[xx, 0], far))
        yc[xx, 1] = go(rc(yb.at[xx, back], box.at[xx], ys.at[xx, 1], yr.at[xx, 1], near))

    def pass_on(xx):
        far, box, to = (up, y_up, yu) if xx % 2 == 0 else (down, y_dn, yd)
        yc[xx, 0].wait_recv()
        yb[xx, to] = (yb[xx, to].astype(F32) + y_mid[xx].astype(F32)).astype(BF)
        yc[xx, 2] = go(rc(yb.at[xx, to], box.at[xx], ys.at[xx, 2], yr.at[xx, 2], far))

    for j in range(NCH):
        a, b = spans[j]
        r = slice(j * CHUNK, (j + 1) * CHUNK)
        kr_g = []
        for h in range(2):
            dk = dot(gs_b[h, j, :, a:b], qc[h, a:b, :]) * SCALE
            gk[r, h * 128 : (h + 1) * 128] = dk[:, 0:128].astype(BF)
            kr_g.append(dk[:, 128:256])
        xx, kk = j // NC, j % NC
        kr_part = jnp.where(lane_k < RD, kr_g[0], kr_g[1]).astype(BF)
        lk[xx, kk, :, :, LAT:PACK] = kr_part.reshape(NY, TOK, 128)
        lat_part = (dot(gk[r, :], w_t[0:256, :]) + dot(gv[r, :], w_t[256:512, :])).astype(BF)
        lk[xx, kk, :, :, 0:LAT] = lat_part.reshape(NY, TOK, LAT)
        if kk == 1:
            swc.append(go(rc(lk.at[xx, 1 - k], sw_in.at[xx], ss.at[xx], sr.at[xx], sib)))
    merge(0)
    weight_grad(zk_out, gk)
    zk = send_z(zk_out, zk_in, zks, zkr)
    merge(1)
    pass_on(0)
    merge(2)
    merge(3)
    pass_on(1)
    dx.relay()
    pass_on(2)
    pass_on(3)

    results = []

    def put(n, a, b):
        results.append(pltpu.make_async_copy(a, b, outs.at[n]))
        results[-1].start()

    ox.finish()
    for c in range(NCTX):
        att_ref[0, :, c * 256 : (c + 1) * 256] = o_in[c]
    put(0, att_ref, att_h)

    def total_z(buf, inbox):
        t = buf[z].astype(F32)
        for d in range(NZ - 1):
            t = t + inbox[d].astype(F32)
        return t.astype(BF).reshape(NY, 16, 256)

    for copy in zv:
        copy.wait_recv()
    z_out[:, :, 256:512] = total_z(zv_out, zv_in)

    done = len(sends)
    for copy in sends[: done - 21]:
        copy.wait_send()
    for xx in range(NX):
        yc[xx, 1].wait_recv()
        yc[xx, 2].wait_recv()
        t = yb[xx, y].astype(F32) + y_up[xx].astype(F32) + y_dn[xx].astype(F32)
        xb[xx] = t.astype(BF)
    xcp = {}

    def x_go(n, src, dst, dev):
        xcp[n] = go(rc(src, dst, x2s.at[n], x2r.at[n], dev))

    x_go(0, xb.at[xo, top_r], x_mid.at[0], right)
    x_go(1, xb.at[xo, bot_r], x_mid.at[1], left)
    x_go(2, xb.at[xu, bot_r], x_up.at[bot_r], right)
    x_go(3, xb.at[xd, top_r], x_dn.at[top_r], left)
    for copy in zk:
        copy.wait_recv()
    z_out[:, :, 0:256] = total_z(zk_out, zk_in)
    wc = []
    for d in (2, 1, 3):
        to = lax.rem(y + d, NY)
        wc.append(go(rc(z_out.at[to], w_in.at[d - 1], w2s.at[d - 1], w2r.at[d - 1], {"seq": to})))
    xcp[0].wait_recv()
    xb[xu, top_r] = (xb[xu, top_r].astype(F32) + x_mid[0].astype(F32)).astype(BF)
    x_go(4, xb.at[xu, top_r], x_up.at[top_r], right)
    xcp[1].wait_recv()
    xb[xd, bot_r] = (xb[xd, bot_r].astype(F32) + x_mid[1].astype(F32)).astype(BF)
    x_go(5, xb.at[xd, bot_r], x_dn.at[bot_r], left)
    dx.finish()
    for c in range(NCTX):
        for h in range(2):
            rows_n[head(2 * c + h), :] = d_in[c, :, h * 128 : (h + 1) * 128].astype(F32)
        pair = d_in[c, :, 256:384].astype(F32)
        rows_r[head(2 * c), :] = pair
        rows_r[head(2 * c + 1), :] = pltpu.roll(pair, RD, 1)
    qng_ref[0] = rows_n[...].reshape(TOK, HEADS, HD).astype(BF)
    qrg_ref[0] = rows_r[:, 0:RD].reshape(TOK, HEADS, RD).astype(BF)
    put(1, qng_ref, qng_h)
    put(2, qrg_ref, qrg_h)
    for n in range(2, 6):
        xcp[n].wait_recv()
    t = xb[x].astype(F32) + x_up[...].astype(F32) + x_dn[...].astype(F32)
    latg_ref[0] = t[:, 0:LAT].astype(BF)
    krg_ref[0] = (t[:, LAT : LAT + RD] + t[:, LAT + RD :]).astype(BF)
    put(3, latg_ref, latg_h)
    put(4, krg_ref, krg_h)
    for copy in wc:
        copy.wait_recv()
    t = z_out[y].astype(F32)
    for d in range(NY - 1):
        t = t + w_in[d].astype(F32)
    wkg_ref[...] = t[:, 0:256]
    wvg_ref[...] = t[:, 256:512]
    put(5, wkg_ref, wkg_h)
    put(6, wvg_ref, wvg_h)
    for copy in sends[done - 21 :]:
        copy.wait_send()
    for copy in results:
        copy.wait()


OUTS = (
    ((1, TOK, HEADS * HD), BF),
    ((1, TOK, HEADS, HD), BF),
    ((1, TOK, HEADS, RD), BF),
    ((1, TOK, LAT), BF),
    ((1, TOK, RD), BF),
    ((16, 256), F32),
    ((16, 256), F32),
)


def core(*args):
    def vm(*shape, dtype=BF):
        return pltpu.VMEM(shape, dtype)

    half = TOK // 2
    table = pltpu.SMEM((1, NX * NC * NY), jnp.int32)
    return pl.pallas_call(
        core_kernel,
        out_shape=tuple(jax.ShapeDtypeStruct(s, d) for s, d in OUTS),
        in_specs=[ANY] * 10,
        out_specs=(ANY,) * 7,
        scratch_shapes=[
            *(pltpu.VMEM(s, d) for s, d in OUTS),
            vm(TOK * HEADS, 128, dtype=F32), vm(TOK * HEADS, 128, dtype=F32), DMA((7,)),
            vm(1, TOK, HEADS, HD), vm(1, TOK, HEADS, RD), vm(1, TOK, HEADS * HD),
            vm(1, TOK, LAT), vm(1, TOK, RD), vm(LAT, 256), vm(LAT, 256),
            table, table, table,
            vm(TOK, PACK), vm(NCTX, TOK, PACK), vm(NCTX, TOK, PACK), vm(2, TOK, PACK),
            vm(NX, NC, NY, TOK, PACK),
            vm(LAT, 512), vm(512, LAT), vm(LAT, NK),
            vm(2, NCH, CHUNK, 256), vm(2, NCH, 256, CHUNK),
            vm(2, NCH, CHUNK, 128), vm(2, NCH, 128, CHUNK),
            vm(2, NQ, 256), vm(2, 256, NQ), vm(2, 128, NQ),
            vm(2, NCH, CHUNK, NQ, dtype=F32), vm(2, CHUNK, NQ), vm(2, NCH, 1, NQ, dtype=F32),
            vm(2, NCH, CHUNK, NQ), vm(NK, 256), vm(NK, 256),
            vm(2, 128, NQ, dtype=F32), vm(2, 256, NQ, dtype=F32),
            vm(NCTX, TOK, 256), vm(NCTX, TOK, 256), vm(2, TOK, 256),
            vm(NCTX, TOK, 384), vm(NCTX, TOK, 384), vm(2, TOK, 384),
            vm(NX, NC, NY, TOK, PACK), vm(NX, NY, TOK, PACK), vm(NX, NY, TOK, PACK),
            vm(NX, TOK, PACK), vm(NX, TOK, PACK), vm(NX, TOK, PACK),
            vm(NX, TOK, PACK), vm(2, half, PACK), vm(TOK, PACK), vm(TOK, PACK),
            vm(NZ, TOK, 256), vm(NZ, TOK, 256), vm(NZ - 1, TOK, 256), vm(NZ - 1, TOK, 256),
            vm(NY, 16, 512), vm(NY - 1, 16, 512),
            DMA((10,)), DMA((4,)), DMA((4,)), DMA((4,)), DMA((4,)), DMA((4,)), DMA((4,)),
            DMA((4,)), DMA((4,)), DMA((16,)), DMA((16,)),
            DMA((9,)), DMA((9,)), DMA((9,)), DMA((9,)), DMA((9,)), DMA((9,)),
            DMA((4,)), DMA((4,)), DMA((4, 3)), DMA((4, 3)), DMA((6,)), DMA((6,)),
            DMA((7,)), DMA((7,)), DMA((7,)), DMA((7,)), DMA((3,)), DMA((3,)),
        ],
        compiler_params=pltpu.CompilerParams(
            collective_id=0, has_side_effects=True, vmem_limit_bytes=60 * 2**20
        ),
        name="core",
    )(*args)


def store_kernel(*refs):
    src, dst, mid, lsem, ssem = refs[0:7], refs[7:14], refs[14:21], refs[21], refs[22]
    reads = [pltpu.make_async_copy(src[n], mid[n], lsem.at[n]) for n in range(7)]
    writes = [pltpu.make_async_copy(mid[n], dst[n], ssem.at[n]) for n in range(7)]
    for copy in reads:
        copy.start()
    for n in range(7):
        reads[n].wait()
        writes[n].start()
    for copy in writes:
        copy.wait()


def store(*arrays):
    return pl.pallas_call(
        store_kernel,
        out_shape=tuple(jax.ShapeDtypeStruct(s, d) for s, d in OUTS),
        in_specs=[ANY] * 7,
        out_specs=(ANY,) * 7,
        scratch_shapes=[*(pltpu.VMEM(s, d) for s, d in OUTS), DMA((7,)), DMA((7,))],
        compiler_params=pltpu.CompilerParams(vmem_limit_bytes=60 * 2**20),
        name="store",
    )(*arrays)


def on_device(
    query_nope, query_rope, latent, key_rope, out_grad,
    key_weight, value_weight, block_doc, block_image, block_flag,
):
    return store(*core(
        query_nope, query_rope, out_grad, latent, key_rope,
        key_weight, value_weight, block_doc, block_image, block_flag,
    ))


def solution(mesh):
    return jax.shard_map(
        on_device,
        mesh=mesh,
        in_specs=(
            P("dp", ("ctx", "seq"), None, None),
            P("dp", ("ctx", "seq"), None, None),
            P("dp", ("ctx", "seq"), None),
            P("dp", ("ctx", "seq"), None),
            P("dp", ("ctx", "seq"), None),
            P(None, "ctx"),
            P(None, "ctx"),
            P("dp", None),
            P("dp", None),
            P("dp", None),
        ),
        out_specs=(
            P("dp", ("ctx", "seq"), None),
            P("dp", ("ctx", "seq"), None, None),
            P("dp", ("ctx", "seq"), None, None),
            P("dp", ("ctx", "seq"), None),
            P("dp", ("ctx", "seq"), None),
            P(("dp", "seq"), "ctx"),
            P(("dp", "seq"), "ctx"),
        ),
        check_vma=False,
    )
```

```python
import math

import jax
import jax.numpy as jnp
from jax import lax
from jax.experimental import pallas as pl
from jax.experimental.pallas import tpu as pltpu
from jax.sharding import PartitionSpec as P

NEG = -1e30
MESH = pl.DeviceIdType.MESH
ANY = pl.BlockSpec(memory_space=pl.ANY)
DMA = pltpu.SemaphoreType.DMA
BF = jnp.bfloat16
F32 = jnp.float32

NX, NC, NY, NZ = 4, 2, 4, 8
NCTX = NX * NC
TOK, HEADS, HD, RD, LAT = 64, 16, 128, 64, 512
PACK = 640
NQ = NCTX * TOK
NK = NX * NC * NY * TOK
CHUNK = 256
NCH = NK // CHUNK
SCALE = 1.0 / math.sqrt(HD + RD)
SCALE2 = SCALE * math.log2(math.e)


def rc(src, dst, send, recv, dev):
    return pltpu.make_async_remote_copy(
        src_ref=src, dst_ref=dst, send_sem=send, recv_sem=recv, device_id=dev, device_id_type=MESH
    )


def dot(a, b):
    return jnp.dot(a, b, preferred_element_type=F32)


class Exchange:
    def __init__(self, src, dst, relay, ss, rs, sends):
        ctx = lax.axis_index("ctx")
        self.me = ctx
        x, k = ctx // NC, lax.rem(ctx, NC)
        self.right, self.left = lax.rem(x + 1, NX) * NC, lax.rem(x + NX - 1, NX) * NC
        self.far = lax.rem(x + 2, NX) * NC
        self.x, self.k = x * NC, k
        self.src, self.dst, self.mid = src, dst, relay
        self.ss, self.rs, self.sends = ss, rs, sends
        self.slots = {}

    def go(self, slot, src, dst, send, recv, to):
        copy = rc(src, dst, self.ss.at[send], self.rs.at[recv], {"ctx": to})
        copy.start()
        self.sends.append(copy)
        self.slots[slot] = copy

    def start_far(self):
        k = self.k
        self.go(7, self.src(self.far + k), self.mid.at[0], 5, 7, self.right + k)
        self.go(8, self.src(self.far + 1 - k), self.mid.at[1], 6, 8, self.left + k)

    def start_near(self):
        k, me = self.k, self.me
        for slot, to in (
            (1, self.right + k), (3, self.left + k),
            (2, self.right + 1 - k), (4, self.left + 1 - k),
            (0, self.x + 1 - k),
        ):
            self.go(slot, self.src(to), self.dst(me), slot, slot, to)

    def relay(self):
        k = self.k
        self.slots[7].wait_recv()
        self.go(5, self.mid.at[0], self.dst(self.left + k), 7, 5, self.right + k)
        self.slots[8].wait_recv()
        self.go(6, self.mid.at[1], self.dst(self.right + k), 8, 6, self.left + 1 - k)

    def finish(self):
        for slot in range(7):
            self.slots[slot].wait_recv()


def vm(*shape, dtype=BF):
    return pltpu.VMEM(shape, dtype)


def greet_and_wait(devices):
    barrier = pltpu.get_barrier_semaphore()
    for dev in devices:
        pl.semaphore_signal(barrier, inc=1, device_id=dev, device_id_type=MESH)
    return barrier


def gather_kernel(
    qn_h, qr_h, do_h, lat_h, kr_h, q_all, lat_all,
    rows_n, rows_r, qn_v, qr_v, do_v, lat_v, kr_v, comb, pack, q_mid,
    loc, xs, xr, us, ur, ds, dr, fs, fr, ws, wr, qs, qrs,
):
    ctx = lax.axis_index("ctx")
    y = lax.axis_index("seq")
    x = ctx // NC
    k = lax.rem(ctx, NC)
    xu, xd, xo = lax.rem(x + 1, NX), lax.rem(x + NX - 1, NX), lax.rem(x + 2, NX)
    yu, yd, yo = lax.rem(y + 1, NY), lax.rem(y + NY - 1, NY), lax.rem(y + 2, NY)
    sib = {"ctx": x * NC + 1 - k}
    right, left = {"ctx": xu * NC + k}, {"ctx": xd * NC + k}
    up, down = {"seq": yu}, {"seq": yd}
    loads = []
    for n, (a, b) in enumerate((
        (lat_h, lat_v), (kr_h, kr_v), (qn_h, qn_v), (qr_h, qr_v), (do_h, do_v),
    )):
        loads.append(pltpu.make_async_copy(a, b, loc.at[n]))
        loads[-1].start()
    devices = [sib, right, left, {"ctx": xu * NC + 1 - k}, {"ctx": xd * NC + 1 - k}, up, down]
    devices += [{"seq": yy, "ctx": x * NC + 1 - k} for yy in (yu, yd)]
    barrier = greet_and_wait(devices)
    loads[0].wait()
    loads[1].wait()
    comb[:, 0:LAT] = lat_v[0]
    comb[:, LAT : LAT + RD] = kr_v[0]
    comb[:, LAT + RD :] = kr_v[0]
    pl.semaphore_wait(barrier, len(devices))
    sends = []

    def go(copy):
        copy.start()
        sends.append(copy)
        return copy

    mine = lat_all.at[x, k, y]
    xc = [go(rc(comb, mine, xs.at[0], xr.at[0], right)), go(rc(comb, mine, xs.at[1], xr.at[1], left))]
    ups = {0: go(rc(comb, mine, us.at[0], ur.at[0], up))}
    downs = {0: go(rc(comb, mine, ds.at[0], dr.at[0], down))}
    swaps = {0: go(rc(comb, mine, ws.at[0], wr.at[0], sib))}
    own = pltpu.make_async_copy(comb, mine, loc.at[5])
    own.start()
    for n in range(2, 5):
        loads[n].wait()
    rows_n[...] = qn_v[0].astype(F32).reshape(TOK * HEADS, HD)
    rows_r[:, 0:RD] = qr_v[0].astype(F32).reshape(TOK * HEADS, RD)
    lane_t = lax.broadcasted_iota(jnp.int32, (TOK, 128), 1)

    def head(n):
        return pl.ds(n, TOK, stride=HEADS)

    for c in range(NCTX):
        for h in range(2):
            pack[c, :, h * 128 : (h + 1) * 128] = rows_n[head(2 * c + h), :].astype(BF)
        pack[c, :, 256:512] = do_v[0, :, c * 256 : (c + 1) * 256]
        pair = jnp.where(
            lane_t < RD, rows_r[head(2 * c), :], pltpu.roll(rows_r[head(2 * c + 1), :], RD, 1)
        )
        pack[c, :, 512:640] = pair.astype(BF)
    qx = Exchange(lambda c: pack.at[c], lambda c: q_all.at[c], q_mid, qs, qrs, sends)
    qx.start_far()
    ownq = pltpu.make_async_copy(pack.at[ctx], q_all.at[ctx], loc.at[6])
    ownq.start()
    half = TOK // 2
    top_r, bot_r = pl.ds(0, half), pl.ds(half, half)
    turn = (k, 1 - k)
    blocks = (x, xd, xo, xu)

    def blk(e, yy):
        return lat_all.at[blocks[e], k, yy]

    def swap(slot, b):
        swaps[slot] = go(rc(b, b, ws.at[slot], wr.at[slot], sib))

    def spread(e):
        b = blk(e, y)
        ups[e] = go(rc(b, b, us.at[e], ur.at[e], up))
        downs[e] = go(rc(b, b, ds.at[e], dr.at[e], down))
        swap(e, b)

    fwd = {}

    def onward(e):
        way = turn[e // 2]
        ups[e].wait_recv()
        downs[e].wait_recv()
        b = blk(e, lax.rem(y + 3 + 2 * way, NY))
        to = lax.rem(y + 1 + 2 * way, NY)
        fwd[e] = go(rc(b, b, fs.at[e], fr.at[e], {"seq": to}))
        swaps[12 + e] = go(rc(b, b, ws.at[12 + e], wr.at[12 + e], {"seq": to, "ctx": x * NC + 1 - k}))
        swap(4 + e, blk(e, yd))
        swap(8 + e, blk(e, yu))

    xc[0].wait_recv()
    b = lat_all.at[xd, k, y, top_r]
    xc.append(go(rc(b, b, xs.at[2], xr.at[2], right)))
    xc[1].wait_recv()
    b = lat_all.at[xu, k, y, bot_r]
    xc.append(go(rc(b, b, xs.at[3], xr.at[3], left)))
    spread(1)
    spread(3)
    qx.start_near()
    onward(0)
    xc[2].wait_recv()
    xc[3].wait_recv()
    spread(2)
    qx.relay()
    onward(1)
    onward(3)
    onward(2)
    for e in (0, 1, 3, 2):
        fwd[e].wait_recv()
    for slot in range(16):
        swaps[slot].wait_recv()
    qx.finish()
    for copy in sends:
        copy.wait_send()
    own.wait()
    ownq.wait()


def gather(*args):
    return pl.pallas_call(
        gather_kernel,
        out_shape=(
            jax.ShapeDtypeStruct((NCTX, TOK, PACK), BF),
            jax.ShapeDtypeStruct((NX, NC, NY, TOK, PACK), BF),
        ),
        in_specs=[ANY] * 5,
        out_specs=(ANY, ANY),
        scratch_shapes=[
            vm(TOK * HEADS, 128, dtype=F32), vm(TOK * HEADS, 128, dtype=F32),
            vm(1, TOK, HEADS, HD), vm(1, TOK, HEADS, RD), vm(1, TOK, HEADS * HD),
            vm(1, TOK, LAT), vm(1, TOK, RD),
            vm(TOK, PACK), vm(NCTX, TOK, PACK), vm(2, TOK, PACK),
            DMA((7,)), DMA((4,)), DMA((4,)), DMA((4,)), DMA((4,)), DMA((4,)), DMA((4,)),
            DMA((4,)), DMA((4,)), DMA((16,)), DMA((16,)), DMA((9,)), DMA((9,)),
        ],
        compiler_params=pltpu.CompilerParams(
            collective_id=0, has_side_effects=True, vmem_limit_bytes=60 * 2**20
        ),
        name="gather",
    )(*args)


def attend_kernel(
    doc_h, img_h, flag_h, q_h, lat_h, wk_h, wv_h, oq_h, lk_h, wg_h,
    doc_ref, img_ref, flag_ref, q_v, lat_v, w_all, w_t, lat_t, kc, kct, v, vt,
    qc, qct, do_s, dot_t, qdoc, qcode, qpos, sc, pb, mj, mx, tot, delta, gk, gv, o_t, dq_t,
    oq, lk, wg, loc, latsem, outsem, lksem,
):
    y = lax.axis_index("seq")
    loads = []
    for n, (a, b) in enumerate((
        (wk_h, w_all.at[:, pl.ds(0, 256)]), (wv_h, w_all.at[:, pl.ds(256, 256)]), (q_h, q_v),
        (doc_h, doc_ref), (img_h, img_ref), (flag_h, flag_ref),
    )):
        loads.append(pltpu.make_async_copy(a, b, loc.at[n]))
        loads[-1].start()

    def lat_copy(j):
        return pltpu.make_async_copy(lat_h.at[j], lat_v.at[j], latsem.at[j])

    for j in range(NCH):
        lat_copy(j).start()
    for copy in loads:
        copy.wait()
    w_t[...] = w_all[...].T
    o_t[...] = jnp.zeros_like(o_t)
    dq_t[...] = jnp.zeros_like(dq_t)
    mx[...] = jnp.full_like(mx, NEG)
    tot[...] = jnp.zeros_like(tot)
    for h in range(2):
        qc[h, :, 0:128] = q_v[:, h * 128 : (h + 1) * 128]
        qc[h, :, 128:256] = q_v[:, 512:640]
        qct[h] = qc[h].T
        do_s[h] = q_v[:, 256 + h * 128 : 256 + (h + 1) * 128]
        dot_t[h] = do_s[h].T
    lane_q = lax.broadcasted_iota(jnp.int32, (1, NQ), 1)
    grp = lane_q // TOK
    one_doc = jnp.zeros((1, NQ), jnp.int32)
    one_code = jnp.zeros((1, NQ), jnp.int32)
    for c in range(NCTX):
        b = NY * c + y
        one_doc = jnp.where(grp == c, doc_ref[0, b], one_doc)
        code = jnp.where(flag_ref[0, b] == 1, doc_ref[0, b] * 64 + img_ref[0, b], -1)
        one_code = jnp.where(grp == c, code, one_code)
    qdoc[...] = one_doc
    qcode[...] = one_code
    qpos[...] = (NY * grp + y) * TOK + lane_q % TOK
    sub = lax.broadcasted_iota(jnp.int32, (TOK, 1), 0)
    lane_k = lax.broadcasted_iota(jnp.int32, (CHUNK, 128), 1)
    row_k = lax.broadcasted_iota(jnp.int32, (128, CHUNK), 0)
    zero = jnp.zeros((), BF)

    def by_width(body):
        for j in range(NCH):
            lo = max(0, j - 1) // 2 * 2
            hi = min(NCTX, (min(NCTX, j + 5) + 1) // 2 * 2)
            body(j, lo * TOK, (hi - lo) * TOK)

    def project(j):
        lat_copy(j).wait()
        lat = lat_v[j, :, 0:LAT]
        kr = lat_v[j, :, LAT:PACK]
        lt = lat.T
        lat_t[:, j * CHUNK : (j + 1) * CHUNK] = lt
        kv = dot(lat, w_all[...]).astype(BF)
        kvt = dot(w_t[...], lt).astype(BF)
        krt = kr.T
        for h in range(2):
            kc[h, j, :, 0:128] = kv[:, h * 128 : (h + 1) * 128]
            kc[h, j, :, 128:256] = jnp.where((lane_k < RD) == (h == 0), kr, zero)
            kct[h, j, 0:128] = kvt[h * 128 : (h + 1) * 128]
            kct[h, j, 128:256] = jnp.where((row_k < RD) == (h == 0), krt, zero)
            v[h, j] = kv[:, 256 + h * 128 : 256 + (h + 1) * 128]
            vt[h, j] = kvt[256 + h * 128 : 256 + (h + 1) * 128]

    def soften(j, a, width):
        q = pl.ds(a, width)
        thr = []
        for i in range(CHUNK // TOK):
            kb = j * (CHUNK // TOK) + i
            kcode = jnp.where(flag_ref[0, kb] == 1, doc_ref[0, kb] * 64 + img_ref[0, kb], -2)
            t = jnp.where(qdoc[:, q] == doc_ref[0, kb], qpos[:, q] - kb * TOK, -1)
            thr.append(jnp.where(qcode[:, q] == kcode, NK, t))
        for h in range(2):
            raw = dot(kc[h, j], qct[h, :, q])
            top = None
            masked = []
            for i in range(CHUNK // TOK):
                m = jnp.where(sub <= thr[i], raw[i * TOK : (i + 1) * TOK] * SCALE2, NEG)
                masked.append(m)
                one = jnp.max(m, axis=0, keepdims=True)
                top = one if top is None else jnp.maximum(top, one)
            part = None
            for i in range(CHUNK // TOK):
                p = jnp.exp2(masked[i] - top)
                sc[h, j, i * TOK : (i + 1) * TOK, q] = p
                pb[h, i * TOK : (i + 1) * TOK, 0:width] = p.astype(BF)
                one = jnp.sum(p, axis=0, keepdims=True)
                part = one if part is None else part + one
            mj[h, j, :, q] = top
            old = mx[h, :, q]
            new = jnp.maximum(old, top)
            old_f, new_f = jnp.exp2(old - new), jnp.exp2(top - new)
            o_t[h, :, q] = o_t[h, :, q] * old_f + dot(vt[h, j], pb[h, :, 0:width]) * new_f
            tot[h, :, q] = tot[h, :, q] * old_f + part * new_f
            mx[h, :, q] = new

    for j in range(NCH):
        project(j)
    by_width(soften)
    for h in range(2):
        tot[h] = 1.0 / tot[h]
        out = o_t[h] * tot[h]
        oq[:, h * 128 : (h + 1) * 128] = out.T.astype(BF)
        delta[h] = jnp.sum(out * dot_t[h].astype(F32), axis=0, keepdims=True)

    def grads(j, a, width):
        q = pl.ds(a, width)
        kr_g = []
        for h in range(2):
            f = jnp.exp2(mj[h, j, :, q] - mx[h, :, q]) * tot[h, :, q]
            p = sc[h, j, :, q] * f
            gv[j, :, h * 128 : (h + 1) * 128] = dot(p.astype(BF), do_s[h, q, :]).astype(BF)
            dp = dot(v[h, j], dot_t[h, :, q])
            g = (p * (dp - delta[h, :, q])).astype(BF)
            dk = dot(g, qc[h, q, :]) * SCALE
            dq_t[h, :, q] += dot(kct[h, j], g)
            gk[j, :, h * 128 : (h + 1) * 128] = dk[:, 0:128].astype(BF)
            kr_g.append(dk[:, 128:256])
        lk[j, :, LAT:PACK] = jnp.where(lane_k < RD, kr_g[0], kr_g[1]).astype(BF)

    by_width(grads)

    def lk_copy(j):
        return pltpu.make_async_copy(lk.at[j], lk_h.at[j], lksem.at[j])

    for j in range(NCH):
        lk[j, :, 0:LAT] = (dot(gk[j], w_t[0:256, :]) + dot(gv[j], w_t[256:512, :])).astype(BF)
        lk_copy(j).start()
    for n, g in enumerate((gk, gv)):
        for i in range(2):
            rows = slice(i * 256, (i + 1) * 256)
            wg[rows, n * 256 : (n + 1) * 256] = dot(lat_t[rows, :], g[...].reshape(NK, 256)).astype(BF)
    wg_copy = pltpu.make_async_copy(wg, wg_h, outsem.at[0])
    wg_copy.start()
    for h in range(2):
        oq[:, 256 + h * 128 : 256 + (h + 1) * 128] = (dq_t[h, 0:128, :] * SCALE).T.astype(BF)
    oq[:, 512:640] = ((dq_t[0, 128:256, :] + dq_t[1, 128:256, :]) * SCALE).T.astype(BF)
    oq_copy = pltpu.make_async_copy(oq, oq_h, outsem.at[1])
    oq_copy.start()
    for j in range(NCH):
        lk_copy(j).wait()
    wg_copy.wait()
    oq_copy.wait()


def attend(*args):
    table = pltpu.SMEM((1, NX * NC * NY), jnp.int32)
    row = vm(1, NQ, dtype=jnp.int32)
    return pl.pallas_call(
        attend_kernel,
        out_shape=(
            jax.ShapeDtypeStruct((NQ, PACK), BF),
            jax.ShapeDtypeStruct((NCH, CHUNK, PACK), BF),
            jax.ShapeDtypeStruct((LAT, 512), BF),
        ),
        in_specs=[ANY] * 7,
        out_specs=(ANY,) * 3,
        scratch_shapes=[
            table, table, table,
            vm(NQ, PACK), vm(NCH, CHUNK, PACK), vm(LAT, 512), vm(512, LAT), vm(LAT, NK),
            vm(2, NCH, CHUNK, 256), vm(2, NCH, 256, CHUNK),
            vm(2, NCH, CHUNK, 128), vm(2, NCH, 128, CHUNK),
            vm(2, NQ, 256), vm(2, 256, NQ), vm(2, NQ, 128), vm(2, 128, NQ),
            row, row, row,
            vm(2, NCH, CHUNK, NQ, dtype=F32), vm(2, CHUNK, NQ), vm(2, NCH, 1, NQ, dtype=F32),
            vm(2, 1, NQ, dtype=F32), vm(2, 1, NQ, dtype=F32), vm(2, 1, NQ, dtype=F32),
            vm(NCH, CHUNK, 256), vm(NCH, CHUNK, 256),
            vm(2, 128, NQ, dtype=F32), vm(2, 256, NQ, dtype=F32),
            vm(NQ, PACK), vm(NCH, CHUNK, PACK), vm(LAT, 512),
            DMA((6,)), DMA((NCH,)), DMA((2,)), DMA((NCH,)),
        ],
        compiler_params=pltpu.CompilerParams(vmem_limit_bytes=60 * 2**20),
        name="attend",
    )(*args)


def scatter_kernel(
    oq_h, lk_h, wg_h, att_h, qng_h, qrg_h, latg_h, krg_h, wkg_h, wvg_h,
    att_ref, qng_ref, qrg_ref, latg_ref, krg_ref, wkg_ref, wvg_ref, rows_n, rows_r, outs,
    lk, sw_in, yb, y_mid, y_up, y_dn, x_mid, x_up, x_dn, tb, ub, t_in, u_in,
    d_in, d_mid, wg, z_in, z_out, w_in,
    loc, ss, sr, ys, yr, x2s, x2r, ts, tr, vs, vr, gs, grs, zs, zr, w2s, w2r,
):
    ctx = lax.axis_index("ctx")
    y = lax.axis_index("seq")
    z = lax.axis_index("dp")
    x = ctx // NC
    k = lax.rem(ctx, NC)
    xu, xd, xo = lax.rem(x + 1, NX), lax.rem(x + NX - 1, NX), lax.rem(x + 2, NX)
    yo = lax.rem(y + 2, NY)
    sib = {"ctx": x * NC + 1 - k}
    right, left = {"ctx": xu * NC + k}, {"ctx": xd * NC + k}
    devices = [sib, right, left, {"ctx": xu * NC + 1 - k}, {"ctx": xd * NC + 1 - k}]
    devices += [{"ctx": xo * NC + k}]
    devices += [{"seq": lax.rem(y + d, NY)} for d in range(1, NY)]
    devices += [{"dp": lax.rem(z + d, NZ)} for d in range(1, NZ)]
    barrier = greet_and_wait(devices)
    loads = [pltpu.make_async_copy(lk_h.at[xx, k], lk.at[xx], loc.at[xx]) for xx in range(NX)]
    loads.append(pltpu.make_async_copy(wg_h.at[z], wg, loc.at[4]))
    loads.append(pltpu.make_async_copy(oq_h.at[ctx], d_in.at[ctx], loc.at[5]))
    for copy in loads:
        copy.start()
    pl.semaphore_wait(barrier, len(devices))
    sends = []

    def go(copy):
        copy.start()
        sends.append(copy)
        return copy

    swc = [
        go(rc(lk_h.at[xx, 1 - k], sw_in.at[xx], ss.at[xx], sr.at[xx], sib)) for xx in range(NX)
    ]
    zc = []
    for d in (4, 3, 5, 2, 6, 1, 7):
        to = lax.rem(z + d, NZ)
        zc.append(go(rc(wg_h.at[to], z_in.at[d - 1], zs.at[d - 1], zr.at[d - 1], {"dp": to})))
    dx = Exchange(lambda c: oq_h.at[c], lambda c: d_in.at[c], d_mid, gs, grs, sends)
    dx.start_far()
    dx.start_near()
    half = TOK // 2
    top_r, bot_r = pl.ds(0, half), pl.ds(half, half)
    turn = (k, 1 - k)
    yc = {}

    def merge(xx):
        loads[xx].wait()
        swc[xx].wait_recv()

        def add(i, carry):
            yb[xx, i] = (lk[xx, i].astype(F32) + sw_in[xx, i].astype(F32)).astype(BF)
            return carry

        lax.fori_loop(0, NY, add, 0)
        way = turn[xx % 2]
        far, back = lax.rem(y + 1 + 2 * way, NY), lax.rem(y + 3 + 2 * way, NY)
        yc[xx, 0] = go(rc(yb.at[xx, yo, top_r], y_mid.at[xx], ys.at[xx, 0], yr.at[xx, 0], {"seq": far}))
        yc[xx, 1] = go(rc(yb.at[xx, back, top_r], y_dn.at[xx], ys.at[xx, 1], yr.at[xx, 1], {"seq": back}))

    def pass_on(xx):
        far = lax.rem(y + 1 + 2 * turn[xx % 2], NY)
        yc[xx, 0].wait_recv()
        yb[xx, far, top_r] = (yb[xx, far, top_r].astype(F32) + y_mid[xx].astype(F32)).astype(BF)
        yc[xx, 2] = go(rc(yb.at[xx, far, top_r], y_up.at[xx], ys.at[xx, 2], yr.at[xx, 2], {"seq": far}))

    for xx in range(NX):
        merge(xx)
    xcp = {}

    def x_go(n, src, dst, dev):
        xcp[n] = go(rc(src, dst, x2s.at[n], x2r.at[n], dev))

    one, two = pl.ds(0, 2), pl.ds(2, 2)
    x_go(0, yb.at[xo, one, bot_r], x_mid.at[0], right)
    x_go(1, yb.at[xo, two, bot_r], x_mid.at[1], left)
    x_go(2, yb.at[xu, two, bot_r], x_up.at[two], right)
    x_go(3, yb.at[xd, one, bot_r], x_dn.at[one], left)
    for xx in range(NX):
        pass_on(xx)
    xcp[0].wait_recv()
    yb[xu, one, bot_r] = (yb[xu, one, bot_r].astype(F32) + x_mid[0].astype(F32)).astype(BF)
    x_go(4, yb.at[xu, one, bot_r], x_up.at[one], right)
    xcp[1].wait_recv()
    yb[xd, two, bot_r] = (yb[xd, two, bot_r].astype(F32) + x_mid[1].astype(F32)).astype(BF)
    x_go(5, yb.at[xd, two, bot_r], x_dn.at[two], left)
    dx.relay()
    for xx in range(NX):
        yc[xx, 1].wait_recv()
        yc[xx, 2].wait_recv()
        t = yb[xx, y, top_r].astype(F32) + y_up[xx].astype(F32) + y_dn[xx].astype(F32)
        tb[xx] = t.astype(BF)
    tc, uc = [], []
    for d in (2, 1, 3):
        to = lax.rem(x + d, NX)
        tc.append(go(rc(tb.at[to], t_in.at[d - 1], ts.at[d - 1], tr.at[d - 1], {"ctx": to * NC + k})))
    for n in range(2, 6):
        xcp[n].wait_recv()
    for i in range(NY):
        t = yb[x, i, bot_r].astype(F32) + x_up[i].astype(F32) + x_dn[i].astype(F32)
        ub[i] = t.astype(BF)
    for d in (2, 1, 3):
        to = lax.rem(y + d, NY)
        uc.append(go(rc(ub.at[to], u_in.at[d - 1], vs.at[d - 1], vr.at[d - 1], {"seq": to})))
    loads[4].wait()
    for copy in zc:
        copy.wait_recv()
    t = wg[...].astype(F32)
    for d in range(NZ - 1):
        t = t + z_in[d].astype(F32)
    z_out[...] = t.astype(BF).reshape(NY, 16, 512)
    wc = []
    for d in (2, 1, 3):
        to = lax.rem(y + d, NY)
        wc.append(go(rc(z_out.at[to], w_in.at[d - 1], w2s.at[d - 1], w2r.at[d - 1], {"seq": to})))
    results = []

    def put(n, a, b):
        results.append(pltpu.make_async_copy(a, b, outs.at[n]))
        results[-1].start()

    def head(n):
        return pl.ds(n, TOK, stride=HEADS)

    loads[5].wait()
    dx.finish()
    for c in range(NCTX):
        att_ref[0, :, c * 256 : (c + 1) * 256] = d_in[c, :, 0:256]
        for h in range(2):
            rows_n[head(2 * c + h), :] = d_in[c, :, 256 + h * 128 : 256 + (h + 1) * 128].astype(F32)
        pair = d_in[c, :, 512:640].astype(F32)
        rows_r[head(2 * c), :] = pair
        rows_r[head(2 * c + 1), :] = pltpu.roll(pair, RD, 1)
    qng_ref[0] = rows_n[...].reshape(TOK, HEADS, HD).astype(BF)
    qrg_ref[0] = rows_r[:, 0:RD].reshape(TOK, HEADS, RD).astype(BF)
    put(0, att_ref, att_h)
    put(1, qng_ref, qng_h)
    put(2, qrg_ref, qrg_h)
    for copy in wc:
        copy.wait_recv()
    t = z_out[y].astype(F32)
    for d in range(NY - 1):
        t = t + w_in[d].astype(F32)
    wkg_ref[...] = t[:, 0:256]
    wvg_ref[...] = t[:, 256:512]
    put(5, wkg_ref, wkg_h)
    put(6, wvg_ref, wvg_h)
    for own, inbox, copies, rows in ((tb.at[x], t_in, tc, top_r), (ub.at[y], u_in, uc, bot_r)):
        for copy in copies:
            copy.wait_recv()
        t = own[...].astype(F32)
        for d in range(3):
            t = t + inbox[d].astype(F32)
        latg_ref[0, rows] = t[:, 0:LAT].astype(BF)
        krg_ref[0, rows] = (t[:, LAT : LAT + RD] + t[:, LAT + RD :]).astype(BF)
    put(3, latg_ref, latg_h)
    put(4, krg_ref, krg_h)
    for copy in sends:
        copy.wait_send()
    for copy in results:
        copy.wait()


OUTS = (
    ((1, TOK, HEADS * HD), BF),
    ((1, TOK, HEADS, HD), BF),
    ((1, TOK, HEADS, RD), BF),
    ((1, TOK, LAT), BF),
    ((1, TOK, RD), BF),
    ((16, 256), F32),
    ((16, 256), F32),
)


def scatter(oq, lk, wg):
    half = TOK // 2
    return pl.pallas_call(
        scatter_kernel,
        out_shape=tuple(jax.ShapeDtypeStruct(s, d) for s, d in OUTS),
        in_specs=[ANY] * 3,
        out_specs=(ANY,) * 7,
        scratch_shapes=[
            *(pltpu.VMEM(s, d) for s, d in OUTS),
            vm(TOK * HEADS, 128, dtype=F32), vm(TOK * HEADS, 128, dtype=F32), DMA((7,)),
            vm(NX, NY, TOK, PACK), vm(NX, NY, TOK, PACK), vm(NX, NY, TOK, PACK),
            vm(NX, half, PACK), vm(NX, half, PACK), vm(NX, half, PACK),
            vm(2, 2, half, PACK), vm(NY, half, PACK), vm(NY, half, PACK),
            vm(NX, half, PACK), vm(NY, half, PACK), vm(3, half, PACK), vm(3, half, PACK),
            vm(NCTX, TOK, PACK), vm(2, TOK, PACK),
            vm(TOK, 512), vm(NZ - 1, TOK, 512), vm(NY, 16, 512), vm(NY - 1, 16, 512),
            DMA((6,)), DMA((4,)), DMA((4,)), DMA((4, 3)), DMA((4, 3)), DMA((6,)), DMA((6,)),
            DMA((3,)), DMA((3,)), DMA((3,)), DMA((3,)),
            DMA((9,)), DMA((9,)), DMA((7,)), DMA((7,)), DMA((3,)), DMA((3,)),
        ],
        compiler_params=pltpu.CompilerParams(
            collective_id=1, has_side_effects=True, vmem_limit_bytes=60 * 2**20
        ),
        name="scatter",
    )(
        oq.reshape(NCTX, TOK, PACK),
        lk.reshape(NX, NC, NY, TOK, PACK),
        wg.reshape(NZ, LAT // NZ, 512),
    )


def store_kernel(*refs):
    src, dst, mid, lsem, ssem = refs[0:7], refs[7:14], refs[14:21], refs[21], refs[22]
    reads = [pltpu.make_async_copy(src[n], mid[n], lsem.at[n]) for n in range(7)]
    writes = [pltpu.make_async_copy(mid[n], dst[n], ssem.at[n]) for n in range(7)]
    for copy in reads:
        copy.start()
    for n in range(7):
        reads[n].wait()
        writes[n].start()
    for copy in writes:
        copy.wait()


def store(*arrays):
    return pl.pallas_call(
        store_kernel,
        out_shape=tuple(jax.ShapeDtypeStruct(s, d) for s, d in OUTS),
        in_specs=[ANY] * 7,
        out_specs=(ANY,) * 7,
        scratch_shapes=[*(pltpu.VMEM(s, d) for s, d in OUTS), DMA((7,)), DMA((7,))],
        compiler_params=pltpu.CompilerParams(vmem_limit_bytes=60 * 2**20),
        name="store",
    )(*arrays)


def on_device(
    query_nope, query_rope, latent, key_rope, out_grad,
    key_weight, value_weight, block_doc, block_image, block_flag,
):
    q_all, lat_all = gather(query_nope, query_rope, out_grad, latent, key_rope)
    oq, lk, wg = attend(
        block_doc, block_image, block_flag,
        q_all.reshape(NQ, PACK), lat_all.reshape(NCH, CHUNK, PACK), key_weight, value_weight,
    )
    return store(*scatter(oq, lk, wg))


def solution(mesh):
    return jax.shard_map(
        on_device,
        mesh=mesh,
        in_specs=(
            P("dp", ("ctx", "seq"), None, None),
            P("dp", ("ctx", "seq"), None, None),
            P("dp", ("ctx", "seq"), None),
            P("dp", ("ctx", "seq"), None),
            P("dp", ("ctx", "seq"), None),
            P(None, "ctx"),
            P(None, "ctx"),
            P("dp", None),
            P("dp", None),
            P("dp", None),
        ),
        out_specs=(
            P("dp", ("ctx", "seq"), None),
            P("dp", ("ctx", "seq"), None, None),
            P("dp", ("ctx", "seq"), None, None),
            P("dp", ("ctx", "seq"), None),
            P("dp", ("ctx", "seq"), None),
            P(("dp", "seq"), "ctx"),
            P(("dp", "seq"), "ctx"),
        ),
        check_vma=False,
    )
```

```python
import math

import jax
import jax.numpy as jnp
from jax import lax
from jax.experimental import pallas as pl
from jax.experimental.pallas import tpu as pltpu
from jax.sharding import PartitionSpec as P

NEG = -1e30
MESH = pl.DeviceIdType.MESH
ANY = pl.BlockSpec(memory_space=pl.ANY)
DMA = pltpu.SemaphoreType.DMA
BF = jnp.bfloat16
F32 = jnp.float32

NX, NC, NY, NZ = 4, 2, 4, 8
NCTX = NX * NC
TOK, HEADS, HD, RD, LAT = 64, 16, 128, 64, 512
PACK = 640
NQ = NCTX * TOK
NK = NX * NC * NY * TOK
CHUNK = 256
NCH = NK // CHUNK
SCALE = 1.0 / math.sqrt(HD + RD)
SCALE2 = SCALE * math.log2(math.e)


def rc(src, dst, send, recv, dev):
    return pltpu.make_async_remote_copy(
        src_ref=src, dst_ref=dst, send_sem=send, recv_sem=recv, device_id=dev, device_id_type=MESH
    )


def dot(a, b):
    return jnp.dot(a, b, preferred_element_type=F32)


class Exchange:
    def __init__(self, src, dst, relay, ss, rs, sends):
        ctx = lax.axis_index("ctx")
        self.me = ctx
        x, k = ctx // NC, lax.rem(ctx, NC)
        self.right, self.left = lax.rem(x + 1, NX) * NC, lax.rem(x + NX - 1, NX) * NC
        self.far = lax.rem(x + 2, NX) * NC
        self.x, self.k = x * NC, k
        self.src, self.dst, self.mid = src, dst, relay
        self.ss, self.rs, self.sends = ss, rs, sends
        self.slots = {}

    def go(self, slot, src, dst, send, recv, to):
        copy = rc(src, dst, self.ss.at[send], self.rs.at[recv], {"ctx": to})
        copy.start()
        self.sends.append(copy)
        self.slots[slot] = copy

    def start_far(self):
        k = self.k
        self.go(7, self.src(self.far + k), self.mid.at[0], 5, 7, self.right + k)
        self.go(8, self.src(self.far + 1 - k), self.mid.at[1], 6, 8, self.left + k)

    def start_near(self):
        k, me = self.k, self.me
        for slot, to in (
            (1, self.right + k), (3, self.left + k),
            (2, self.right + 1 - k), (4, self.left + 1 - k),
            (0, self.x + 1 - k),
        ):
            self.go(slot, self.src(to), self.dst(me), slot, slot, to)

    def relay(self):
        k = self.k
        self.slots[7].wait_recv()
        self.go(5, self.mid.at[0], self.dst(self.left + k), 7, 5, self.right + k)
        self.slots[8].wait_recv()
        self.go(6, self.mid.at[1], self.dst(self.right + k), 8, 6, self.left + 1 - k)

    def finish(self):
        for slot in range(7):
            self.slots[slot].wait_recv()


def core_kernel(
    qn_h, qr_h, do_h, lat_h, kr_h, wk_h, wv_h, doc_h, img_h, flag_h,
    att_h, qng_h, qrg_h, latg_h, krg_h, wkg_h, wvg_h,
    att_ref, qng_ref, qrg_ref, latg_ref, krg_ref, wkg_ref, wvg_ref, rows_n, rows_r, outs,
    qn_v, qr_v, do_v, lat_v, kr_v, wk_v, wv_v, doc_ref, img_ref, flag_ref,
    comb, pack, q_all, q_mid, lat_all,
    w_all, w_t, lat_t, kc, kct, v, vt, qc, qct, dot_t, sc, gk, gv, o_t, dq_t,
    o_out, o_in, o_mid, d_out, d_in, d_mid,
    lk, sw_in, yb, y_mid, y_up, y_dn, x_mid, x_up, x_dn, tb, ub, t_in, u_in,
    zk_out, zv_out, zk_in, zv_in, z_out, w_in,
    loc, xs, xr, us, ur, ds, dr, fs, fr, ws, wr,
    qs, qrs, os, ors, gs, grs, ss, sr, ys, yr, x2s, x2r, ts, tr, vs, vr,
    zks, zkr, zvs, zvr, w2s, w2r,
):
    ctx = lax.axis_index("ctx")
    y = lax.axis_index("seq")
    z = lax.axis_index("dp")
    x = ctx // NC
    k = lax.rem(ctx, NC)
    xu, xd, xo = lax.rem(x + 1, NX), lax.rem(x + NX - 1, NX), lax.rem(x + 2, NX)
    yu, yd, yo = lax.rem(y + 1, NY), lax.rem(y + NY - 1, NY), lax.rem(y + 2, NY)
    sib = {"ctx": x * NC + 1 - k}
    right, left = {"ctx": xu * NC + k}, {"ctx": xd * NC + k}
    up, down = {"seq": yu}, {"seq": yd}

    loads = []
    for n, (a, b) in enumerate((
        (lat_h, lat_v), (kr_h, kr_v), (qn_h, qn_v), (qr_h, qr_v), (do_h, do_v),
        (wk_h, wk_v), (wv_h, wv_v), (doc_h, doc_ref), (img_h, img_ref), (flag_h, flag_ref),
    )):
        loads.append(pltpu.make_async_copy(a, b, loc.at[n]))
        loads[-1].start()

    barrier = pltpu.get_barrier_semaphore()
    greet = [{"ctx": lax.rem(ctx + d, NCTX)} for d in range(1, NCTX)]
    greet += [{"seq": lax.rem(y + d, NY)} for d in range(1, NY)]
    greet += [{"dp": lax.rem(z + d, NZ)} for d in range(1, NZ)]
    for dev in greet:
        pl.semaphore_signal(barrier, inc=1, device_id=dev, device_id_type=MESH)
    loads[0].wait()
    loads[1].wait()
    comb[:, 0:LAT] = lat_v[0]
    comb[:, LAT : LAT + RD] = kr_v[0]
    comb[:, LAT + RD :] = kr_v[0]
    lat_all[x, k, y] = comb[...]
    pl.semaphore_wait(barrier, len(greet))
    sends = []

    def go(copy):
        copy.start()
        sends.append(copy)
        return copy

    mine = lat_all.at[x, k, y]
    xc = [go(rc(comb, mine, xs.at[0], xr.at[0], right)), go(rc(comb, mine, xs.at[1], xr.at[1], left))]
    ups = [go(rc(comb, mine, us.at[0], ur.at[0], up))]
    downs = [go(rc(comb, mine, ds.at[0], dr.at[0], down))]
    swaps = {0: go(rc(comb, mine, ws.at[0], wr.at[0], sib))}
    for n in range(2, 5):
        loads[n].wait()
    rows_n[...] = qn_v[0].astype(F32).reshape(TOK * HEADS, HD)
    rows_r[:, 0:RD] = qr_v[0].astype(F32).reshape(TOK * HEADS, RD)
    lane_t = lax.broadcasted_iota(jnp.int32, (TOK, 128), 1)

    def head(n):
        return pl.ds(n, TOK, stride=HEADS)

    for c in range(NCTX):
        for h in range(2):
            pack[c, :, h * 128 : (h + 1) * 128] = rows_n[head(2 * c + h), :].astype(BF)
        pack[c, :, 256:512] = do_v[0, :, c * 256 : (c + 1) * 256]
        pair = jnp.where(
            lane_t < RD, rows_r[head(2 * c), :], pltpu.roll(rows_r[head(2 * c + 1), :], RD, 1)
        )
        pack[c, :, 512:640] = pair.astype(BF)
    q_all[ctx] = pack[ctx]
    qx = Exchange(lambda c: pack.at[c], lambda c: q_all.at[c], q_mid, qs, qrs, sends)
    qx.start_far()
    half = TOK // 2
    top_r, bot_r = pl.ds(0, half), pl.ds(half, half)
    turn = (k, 1 - k)
    blocks = (x, xd, xu, xo)

    def blk(e, yy):
        return lat_all.at[blocks[e], k, yy]

    def swap(slot, b):
        swaps[slot] = go(rc(b, b, ws.at[slot], wr.at[slot], sib))

    def spread(e):
        b = blk(e, y)
        ups.append(go(rc(b, b, us.at[e], ur.at[e], up)))
        downs.append(go(rc(b, b, ds.at[e], dr.at[e], down)))
        swap(e, b)

    fwd = []

    def onward(e):
        way = turn[e // 2]
        ups[e].wait_recv()
        downs[e].wait_recv()
        b = blk(e, lax.rem(y + 3 + 2 * way, NY))
        fwd.append(go(rc(b, b, fs.at[e], fr.at[e], {"seq": lax.rem(y + 1 + 2 * way, NY)})))
        swap(4 + e, blk(e, yd))
        swap(8 + e, blk(e, yu))

    def last(e):
        fwd[e].wait_recv()
        swap(12 + e, blk(e, yo))

    def project(xx, kk):
        j = xx * NC + kk
        lat = lat_all[xx, kk, :, :, 0:LAT].reshape(CHUNK, LAT)
        kr = lat_all[xx, kk, :, :, LAT:PACK].reshape(CHUNK, 128)
        lt = lat.T
        lat_t[:, pl.ds(pl.multiple_of(j * CHUNK, CHUNK), CHUNK)] = lt
        kv = dot(lat, w_all[...]).astype(BF)
        kvt = dot(w_t[...], lt).astype(BF)
        krt = kr.T
        for h in range(2):
            kc[h, j, :, 0:128] = kv[:, h * 128 : (h + 1) * 128]
            kc[h, j, :, 128:256] = jnp.where((lane_k < RD) == (h == 0), kr, zero)
            kct[h, j, 0:128] = kvt[h * 128 : (h + 1) * 128]
            kct[h, j, 128:256] = jnp.where((row_k < RD) == (h == 0), krt, zero)
            v[h, j] = kv[:, 256 + h * 128 : 256 + (h + 1) * 128]
            vt[h, j] = kvt[256 + h * 128 : 256 + (h + 1) * 128]

    def queries():
        qx.finish()
        for h in range(2):
            for c in range(NCTX):
                r = slice(c * TOK, (c + 1) * TOK)
                qc[h, r, 0:128] = q_all[c, :, h * 128 : (h + 1) * 128]
                qc[h, r, 128:256] = q_all[c, :, 512:640]
            qct[h] = qc[h].T
            dot_t[h] = q_all[:, :, 256 + h * 128 : 256 + (h + 1) * 128].reshape(NQ, 128).T

    xc[0].wait_recv()
    b = lat_all.at[xd, k, y, top_r]
    xc.append(go(rc(b, b, xs.at[2], xr.at[2], right)))
    xc[1].wait_recv()
    b = lat_all.at[xu, k, y, bot_r]
    xc.append(go(rc(b, b, xs.at[3], xr.at[3], left)))
    spread(1)
    spread(2)
    qx.start_near()
    for n in range(5, 10):
        loads[n].wait()
    w_all[:, 0:256] = wk_v[...]
    w_all[:, 256:512] = wv_v[...]
    w_t[...] = w_all[...].T
    o_t[...] = jnp.zeros_like(o_t)
    dq_t[...] = jnp.zeros_like(dq_t)

    lane_q = lax.broadcasted_iota(jnp.int32, (1, NQ), 1)
    grp = lane_q // TOK
    qdoc = jnp.zeros((1, NQ), jnp.int32)
    qcode = jnp.zeros((1, NQ), jnp.int32)
    for c in range(NCTX):
        b = NY * c + y
        qdoc = jnp.where(grp == c, doc_ref[0, b], qdoc)
        code = jnp.where(flag_ref[0, b] == 1, doc_ref[0, b] * 64 + img_ref[0, b], -1)
        qcode = jnp.where(grp == c, code, qcode)
    qpos = (NY * grp + y) * TOK + lane_q % TOK
    sub = lax.broadcasted_iota(jnp.int32, (TOK, 1), 0)
    lane_k = lax.broadcasted_iota(jnp.int32, (CHUNK, 128), 1)
    row_k = lax.broadcasted_iota(jnp.int32, (128, CHUNK), 0)
    zero = jnp.zeros((), BF)

    qx.relay()
    onward(0)
    xc[2].wait_recv()
    xc[3].wait_recv()
    spread(3)
    onward(1)
    last(0)
    project(blocks[0], k)
    onward(2)
    onward(3)
    last(1)
    project(blocks[1], k)
    last(2)
    project(blocks[2], k)
    last(3)
    project(blocks[3], k)
    for e in range(NX):
        for slot in (e, 4 + e, 8 + e, 12 + e):
            swaps[slot].wait_recv()
        project(blocks[e], 1 - k)

    queries()

    spans = []
    for j in range(NCH):
        lo = max(0, j - 1) // 2 * 2
        hi = min(NCTX, (min(NCTX, j + 5) + 1) // 2 * 2)
        spans.append((lo * TOK, hi * TOK))

    def splice(full, part, a, b):
        pieces = [full[:, 0:a]] if a else []
        pieces.append(part)
        if b < NQ:
            pieces.append(full[:, b:])
        return jnp.concatenate(pieces, axis=1) if len(pieces) > 1 else part

    neg = jnp.full((1, NQ), NEG, F32)
    mx = [neg, neg]
    for j in range(NCH):
        a, b = spans[j]
        thr = []
        for i in range(CHUNK // TOK):
            kb = j * (CHUNK // TOK) + i
            kcode = jnp.where(flag_ref[0, kb] == 1, doc_ref[0, kb] * 64 + img_ref[0, kb], -2)
            t = jnp.where(qdoc[:, a:b] == doc_ref[0, kb], qpos[:, a:b] - kb * TOK, -1)
            thr.append(jnp.where(qcode[:, a:b] == kcode, NK, t))
        for h in range(2):
            raw = dot(kc[h, j], qct[h, :, a:b])
            top = None
            for i in range(CHUNK // TOK):
                m = jnp.where(sub <= thr[i], raw[i * TOK : (i + 1) * TOK] * SCALE2, NEG)
                sc[h, j, i * TOK : (i + 1) * TOK, a:b] = m
                one = jnp.max(m, axis=0, keepdims=True)
                top = one if top is None else jnp.maximum(top, one)
            mx[h] = splice(mx[h], jnp.maximum(mx[h][:, a:b], top), a, b)
    tot = [jnp.zeros((1, NQ), F32)] * 2
    for j in range(NCH):
        a, b = spans[j]
        for h in range(2):
            p = jnp.exp2(sc[h, j, :, a:b] - mx[h][:, a:b])
            sc[h, j, :, a:b] = p
            tot[h] = splice(tot[h], tot[h][:, a:b] + jnp.sum(p, axis=0, keepdims=True), a, b)
            o_t[h, :, a:b] += dot(vt[h, j], p.astype(BF))

    inv = [1.0 / tot[h] for h in range(2)]
    delta = []
    for h in range(2):
        out = o_t[h] * inv[h]
        o_out[:, :, h * 128 : (h + 1) * 128] = out.T.astype(BF).reshape(NCTX, TOK, 128)
        delta.append(jnp.sum(out * dot_t[h].astype(F32), axis=0, keepdims=True))
    ox = Exchange(lambda c: o_out.at[c], lambda c: o_in.at[c], o_mid, os, ors, sends)
    ox.start_far()
    ox.start_near()
    o_in[ctx] = o_out[ctx]

    for j in range(NCH):
        a, b = spans[j]
        r = slice(j * CHUNK, (j + 1) * CHUNK)
        for h in range(2):
            p = sc[h, j, :, a:b] * inv[h][:, a:b]
            do = q_all[a // TOK : b // TOK, :, 256 + h * 128 : 256 + (h + 1) * 128].reshape(b - a, 128)
            gv[r, h * 128 : (h + 1) * 128] = dot(p.astype(BF), do).astype(BF)

    def weight_grad(buf, g):
        for i in range(2):
            part = dot(lat_t[i * 256 : (i + 1) * 256, :], g[...]).astype(BF)
            buf[i * 4 : (i + 1) * 4] = part.reshape(4, TOK, 256)

    def send_z(buf, inbox, s_sem, r_sem):
        out = []
        for d in (4, 3, 5, 2, 6, 1, 7):
            to = lax.rem(z + d, NZ)
            out.append(go(rc(buf.at[to], inbox.at[d - 1], s_sem.at[d - 1], r_sem.at[d - 1], {"dp": to})))
        return out

    weight_grad(zv_out, gv)
    zv = send_z(zv_out, zv_in, zvs, zvr)

    swc = []
    yc = {}

    def merge(xx):
        swc[xx].wait_recv()

        def add(i, carry):
            yb[xx, i] = (lk[xx, k, i].astype(F32) + sw_in[xx, i].astype(F32)).astype(BF)
            return carry

        lax.fori_loop(0, NY, add, 0)
        way = turn[xx % 2]
        far, back = lax.rem(y + 1 + 2 * way, NY), lax.rem(y + 3 + 2 * way, NY)
        yc[xx, 0] = go(rc(yb.at[xx, yo, top_r], y_mid.at[xx], ys.at[xx, 0], yr.at[xx, 0], {"seq": far}))
        yc[xx, 1] = go(rc(yb.at[xx, back, top_r], y_dn.at[xx], ys.at[xx, 1], yr.at[xx, 1], {"seq": back}))

    def pass_on(xx):
        far = lax.rem(y + 1 + 2 * turn[xx % 2], NY)
        yc[xx, 0].wait_recv()
        yb[xx, far, top_r] = (yb[xx, far, top_r].astype(F32) + y_mid[xx].astype(F32)).astype(BF)
        yc[xx, 2] = go(rc(yb.at[xx, far, top_r], y_up.at[xx], ys.at[xx, 2], yr.at[xx, 2], {"seq": far}))

    for j in range(NCH):
        a, b = spans[j]
        r = slice(j * CHUNK, (j + 1) * CHUNK)
        kr_g = []
        for h in range(2):
            dp = dot(v[h, j], dot_t[h, :, a:b])
            g = (sc[h, j, :, a:b] * ((dp - delta[h][:, a:b]) * inv[h][:, a:b])).astype(BF)
            dk = dot(g, qc[h, a:b, :]) * SCALE
            dq_t[h, :, a:b] += dot(kct[h, j], g)
            gk[r, h * 128 : (h + 1) * 128] = dk[:, 0:128].astype(BF)
            kr_g.append(dk[:, 128:256])
        xx, kk = j // NC, j % NC
        kr_part = jnp.where(lane_k < RD, kr_g[0], kr_g[1]).astype(BF)
        lk[xx, kk, :, :, LAT:PACK] = kr_part.reshape(NY, TOK, 128)
        lat_part = (dot(gk[r, :], w_t[0:256, :]) + dot(gv[r, :], w_t[256:512, :])).astype(BF)
        lk[xx, kk, :, :, 0:LAT] = lat_part.reshape(NY, TOK, LAT)
        if kk == 1:
            swc.append(go(rc(lk.at[xx, 1 - k], sw_in.at[xx], ss.at[xx], sr.at[xx], sib)))
        if j == 3:
            ox.relay()
        if j == 4:
            merge(0)
        if j == 6:
            merge(1)
        if j == 7:
            pass_on(0)
    d_cols = [(dq_t[h, 0:128, :] * SCALE).T.astype(BF) for h in range(2)]
    d_cols.append(((dq_t[0, 128:256, :] + dq_t[1, 128:256, :]) * SCALE).T.astype(BF))
    for n in range(3):
        d_out[:, :, n * 128 : (n + 1) * 128] = d_cols[n].reshape(NCTX, TOK, 128)
    dx = Exchange(lambda c: d_out.at[c], lambda c: d_in.at[c], d_mid, gs, grs, sends)
    dx.start_far()
    d_in[ctx] = d_out[ctx]
    merge(2)
    weight_grad(zk_out, gk)
    zk = send_z(zk_out, zk_in, zks, zkr)
    pass_on(1)
    merge(3)
    xcp = {}

    def x_go(n, src, dst, dev):
        xcp[n] = go(rc(src, dst, x2s.at[n], x2r.at[n], dev))

    one, two = pl.ds(0, 2), pl.ds(2, 2)
    x_go(0, yb.at[xo, one, bot_r], x_mid.at[0], right)
    x_go(1, yb.at[xo, two, bot_r], x_mid.at[1], left)
    x_go(2, yb.at[xu, two, bot_r], x_up.at[two], right)
    x_go(3, yb.at[xd, one, bot_r], x_dn.at[one], left)
    dx.start_near()
    pass_on(2)
    pass_on(3)
    xcp[0].wait_recv()
    yb[xu, one, bot_r] = (yb[xu, one, bot_r].astype(F32) + x_mid[0].astype(F32)).astype(BF)
    x_go(4, yb.at[xu, one, bot_r], x_up.at[one], right)
    xcp[1].wait_recv()
    yb[xd, two, bot_r] = (yb[xd, two, bot_r].astype(F32) + x_mid[1].astype(F32)).astype(BF)
    x_go(5, yb.at[xd, two, bot_r], x_dn.at[two], left)
    dx.relay()

    results = []

    def put(n, a, b):
        results.append(pltpu.make_async_copy(a, b, outs.at[n]))
        results[-1].start()

    ox.finish()
    for c in range(NCTX):
        att_ref[0, :, c * 256 : (c + 1) * 256] = o_in[c]
    put(0, att_ref, att_h)

    def total_z(buf, inbox):
        t = buf[z].astype(F32)
        for d in range(NZ - 1):
            t = t + inbox[d].astype(F32)
        return t.astype(BF).reshape(NY, 16, 256)

    for copy in zv:
        copy.wait_recv()
    z_out[:, :, 256:512] = total_z(zv_out, zv_in)

    for xx in range(NX):
        yc[xx, 1].wait_recv()
        yc[xx, 2].wait_recv()
        t = yb[xx, y, top_r].astype(F32) + y_up[xx].astype(F32) + y_dn[xx].astype(F32)
        tb[xx] = t.astype(BF)
    tc, uc = [], []
    for d in (2, 1, 3):
        to = lax.rem(x + d, NX)
        tc.append(go(rc(tb.at[to], t_in.at[d - 1], ts.at[d - 1], tr.at[d - 1], {"ctx": to * NC + k})))
    for n in range(2, 6):
        xcp[n].wait_recv()
    for i in range(NY):
        t = yb[x, i, bot_r].astype(F32) + x_up[i].astype(F32) + x_dn[i].astype(F32)
        ub[i] = t.astype(BF)
    for d in (2, 1, 3):
        to = lax.rem(y + d, NY)
        uc.append(go(rc(ub.at[to], u_in.at[d - 1], vs.at[d - 1], vr.at[d - 1], {"seq": to})))
    for copy in zk:
        copy.wait_recv()
    z_out[:, :, 0:256] = total_z(zk_out, zk_in)
    wc = []
    for d in (2, 1, 3):
        to = lax.rem(y + d, NY)
        wc.append(go(rc(z_out.at[to], w_in.at[d - 1], w2s.at[d - 1], w2r.at[d - 1], {"seq": to})))
    dx.finish()
    for c in range(NCTX):
        for h in range(2):
            rows_n[head(2 * c + h), :] = d_in[c, :, h * 128 : (h + 1) * 128].astype(F32)
        pair = d_in[c, :, 256:384].astype(F32)
        rows_r[head(2 * c), :] = pair
        rows_r[head(2 * c + 1), :] = pltpu.roll(pair, RD, 1)
    qng_ref[0] = rows_n[...].reshape(TOK, HEADS, HD).astype(BF)
    qrg_ref[0] = rows_r[:, 0:RD].reshape(TOK, HEADS, RD).astype(BF)
    put(1, qng_ref, qng_h)
    put(2, qrg_ref, qrg_h)
    for own, inbox, copies, rows in ((tb.at[x], t_in, tc, top_r), (ub.at[y], u_in, uc, bot_r)):
        for copy in copies:
            copy.wait_recv()
        t = own[...].astype(F32)
        for d in range(3):
            t = t + inbox[d].astype(F32)
        latg_ref[0, rows] = t[:, 0:LAT].astype(BF)
        krg_ref[0, rows] = (t[:, LAT : LAT + RD] + t[:, LAT + RD :]).astype(BF)
    put(3, latg_ref, latg_h)
    put(4, krg_ref, krg_h)
    for copy in wc:
        copy.wait_recv()
    t = z_out[y].astype(F32)
    for d in range(NY - 1):
        t = t + w_in[d].astype(F32)
    wkg_ref[...] = t[:, 0:256]
    wvg_ref[...] = t[:, 256:512]
    put(5, wkg_ref, wkg_h)
    put(6, wvg_ref, wvg_h)
    for copy in sends:
        copy.wait_send()
    for copy in results:
        copy.wait()


OUTS = (
    ((1, TOK, HEADS * HD), BF),
    ((1, TOK, HEADS, HD), BF),
    ((1, TOK, HEADS, RD), BF),
    ((1, TOK, LAT), BF),
    ((1, TOK, RD), BF),
    ((16, 256), F32),
    ((16, 256), F32),
)


def core(*args):
    def vm(*shape, dtype=BF):
        return pltpu.VMEM(shape, dtype)

    half = TOK // 2
    table = pltpu.SMEM((1, NX * NC * NY), jnp.int32)
    return pl.pallas_call(
        core_kernel,
        out_shape=tuple(jax.ShapeDtypeStruct(s, d) for s, d in OUTS),
        in_specs=[ANY] * 10,
        out_specs=(ANY,) * 7,
        scratch_shapes=[
            *(pltpu.VMEM(s, d) for s, d in OUTS),
            vm(TOK * HEADS, 128, dtype=F32), vm(TOK * HEADS, 128, dtype=F32), DMA((7,)),
            vm(1, TOK, HEADS, HD), vm(1, TOK, HEADS, RD), vm(1, TOK, HEADS * HD),
            vm(1, TOK, LAT), vm(1, TOK, RD), vm(LAT, 256), vm(LAT, 256),
            table, table, table,
            vm(TOK, PACK), vm(NCTX, TOK, PACK), vm(NCTX, TOK, PACK), vm(2, TOK, PACK),
            vm(NX, NC, NY, TOK, PACK),
            vm(LAT, 512), vm(512, LAT), vm(LAT, NK),
            vm(2, NCH, CHUNK, 256), vm(2, NCH, 256, CHUNK),
            vm(2, NCH, CHUNK, 128), vm(2, NCH, 128, CHUNK),
            vm(2, NQ, 256), vm(2, 256, NQ), vm(2, 128, NQ),
            vm(2, NCH, CHUNK, NQ, dtype=F32),
            vm(NK, 256), vm(NK, 256),
            vm(2, 128, NQ, dtype=F32), vm(2, 256, NQ, dtype=F32),
            vm(NCTX, TOK, 256), vm(NCTX, TOK, 256), vm(2, TOK, 256),
            vm(NCTX, TOK, 384), vm(NCTX, TOK, 384), vm(2, TOK, 384),
            vm(NX, NC, NY, TOK, PACK), vm(NX, NY, TOK, PACK), vm(NX, NY, TOK, PACK),
            vm(NX, half, PACK), vm(NX, half, PACK), vm(NX, half, PACK),
            vm(2, 2, half, PACK), vm(NY, half, PACK), vm(NY, half, PACK),
            vm(NX, half, PACK), vm(NY, half, PACK), vm(3, half, PACK), vm(3, half, PACK),
            vm(NZ, TOK, 256), vm(NZ, TOK, 256), vm(NZ - 1, TOK, 256), vm(NZ - 1, TOK, 256),
            vm(NY, 16, 512), vm(NY - 1, 16, 512),
            DMA((10,)), DMA((4,)), DMA((4,)), DMA((4,)), DMA((4,)), DMA((4,)), DMA((4,)),
            DMA((4,)), DMA((4,)), DMA((16,)), DMA((16,)),
            DMA((9,)), DMA((9,)), DMA((9,)), DMA((9,)), DMA((9,)), DMA((9,)),
            DMA((4,)), DMA((4,)), DMA((4, 3)), DMA((4, 3)), DMA((6,)), DMA((6,)),
            DMA((3,)), DMA((3,)), DMA((3,)), DMA((3,)),
            DMA((7,)), DMA((7,)), DMA((7,)), DMA((7,)), DMA((3,)), DMA((3,)),
        ],
        compiler_params=pltpu.CompilerParams(
            collective_id=0, has_side_effects=True, vmem_limit_bytes=60 * 2**20
        ),
        name="core",
    )(*args)


def store_kernel(*refs):
    src, dst, mid, lsem, ssem = refs[0:7], refs[7:14], refs[14:21], refs[21], refs[22]
    reads = [pltpu.make_async_copy(src[n], mid[n], lsem.at[n]) for n in range(7)]
    writes = [pltpu.make_async_copy(mid[n], dst[n], ssem.at[n]) for n in range(7)]
    for copy in reads:
        copy.start()
    for n in range(7):
        reads[n].wait()
        writes[n].start()
    for copy in writes:
        copy.wait()


def store(*arrays):
    return pl.pallas_call(
        store_kernel,
        out_shape=tuple(jax.ShapeDtypeStruct(s, d) for s, d in OUTS),
        in_specs=[ANY] * 7,
        out_specs=(ANY,) * 7,
        scratch_shapes=[*(pltpu.VMEM(s, d) for s, d in OUTS), DMA((7,)), DMA((7,))],
        compiler_params=pltpu.CompilerParams(vmem_limit_bytes=60 * 2**20),
        name="store",
    )(*arrays)


def on_device(
    query_nope, query_rope, latent, key_rope, out_grad,
    key_weight, value_weight, block_doc, block_image, block_flag,
):
    return store(*core(
        query_nope, query_rope, out_grad, latent, key_rope,
        key_weight, value_weight, block_doc, block_image, block_flag,
    ))


def solution(mesh):
    return jax.shard_map(
        on_device,
        mesh=mesh,
        in_specs=(
            P("dp", ("ctx", "seq"), None, None),
            P("dp", ("ctx", "seq"), None, None),
            P("dp", ("ctx", "seq"), None),
            P("dp", ("ctx", "seq"), None),
            P("dp", ("ctx", "seq"), None),
            P(None, "ctx"),
            P(None, "ctx"),
            P("dp", None),
            P("dp", None),
            P("dp", None),
        ),
        out_specs=(
            P("dp", ("ctx", "seq"), None),
            P("dp", ("ctx", "seq"), None, None),
            P("dp", ("ctx", "seq"), None, None),
            P("dp", ("ctx", "seq"), None),
            P("dp", ("ctx", "seq"), None),
            P(("dp", "seq"), "ctx"),
            P(("dp", "seq"), "ctx"),
        ),
        check_vma=False,
    )
```

```python
import math

import jax
import jax.numpy as jnp
from jax import lax
from jax.experimental import pallas as pl
from jax.experimental.pallas import tpu as pltpu
from jax.sharding import PartitionSpec as P

NEG = -1e30
MESH = pl.DeviceIdType.MESH
ANY = pl.BlockSpec(memory_space=pl.ANY)
DMA = pltpu.SemaphoreType.DMA
BF = jnp.bfloat16
F32 = jnp.float32

NX, NC, NY, NZ = 4, 2, 4, 8
NCTX = NX * NC
TOK, HEADS, HD, RD, LAT = 64, 16, 128, 64, 512
PACK = 640
NQ = NCTX * TOK
NK = NX * NC * NY * TOK
CHUNK = 256
NCH = NK // CHUNK
SCALE = 1.0 / math.sqrt(HD + RD)
SCALE2 = SCALE * math.log2(math.e)


def rc(src, dst, send, recv, dev):
    return pltpu.make_async_remote_copy(
        src_ref=src, dst_ref=dst, send_sem=send, recv_sem=recv, device_id=dev, device_id_type=MESH
    )


def dot(a, b):
    return jnp.dot(a, b, preferred_element_type=F32)


class Exchange:
    def __init__(self, src, dst, relay, ss, rs, sends):
        ctx = lax.axis_index("ctx")
        self.me = ctx
        x, k = ctx // NC, lax.rem(ctx, NC)
        self.right, self.left = lax.rem(x + 1, NX) * NC, lax.rem(x + NX - 1, NX) * NC
        self.far = lax.rem(x + 2, NX) * NC
        self.x, self.k = x * NC, k
        self.src, self.dst, self.mid = src, dst, relay
        self.ss, self.rs, self.sends = ss, rs, sends
        self.slots = {}

    def go(self, slot, src, dst, send, recv, to):
        copy = rc(src, dst, self.ss.at[send], self.rs.at[recv], {"ctx": to})
        copy.start()
        self.sends.append(copy)
        self.slots[slot] = copy

    def start_far(self):
        k = self.k
        self.go(7, self.src(self.far + k), self.mid.at[0], 5, 7, self.right + k)
        self.go(8, self.src(self.far + 1 - k), self.mid.at[1], 6, 8, self.left + k)

    def start_near(self):
        k, me = self.k, self.me
        for slot, to in (
            (1, self.right + k), (3, self.left + k),
            (2, self.right + 1 - k), (4, self.left + 1 - k),
            (0, self.x + 1 - k),
        ):
            self.go(slot, self.src(to), self.dst(me), slot, slot, to)

    def relay(self):
        k = self.k
        self.slots[7].wait_recv()
        self.go(5, self.mid.at[0], self.dst(self.left + k), 7, 5, self.right + k)
        self.slots[8].wait_recv()
        self.go(6, self.mid.at[1], self.dst(self.right + k), 8, 6, self.left + 1 - k)

    def finish(self):
        for slot in range(7):
            self.slots[slot].wait_recv()


def core_kernel(
    qn_h, qr_h, do_h, lat_h, kr_h, wk_h, wv_h, doc_h, img_h, flag_h,
    att_h, qng_h, qrg_h, latg_h, krg_h, wkg_h, wvg_h,
    att_ref, qng_ref, qrg_ref, latg_ref, krg_ref, wkg_ref, wvg_ref, rows_n, rows_r, outs,
    qn_v, qr_v, do_v, lat_v, kr_v, wk_v, wv_v, doc_ref, img_ref, flag_ref,
    comb, pack, q_all, q_mid, lat_all,
    w_all, w_t, lat_t, kc, kct, v, vt, qc, qct, dot_t, sc, mx, gk, gv, o_t, dq_t,
    o_out, o_in, o_mid, d_out, d_in, d_mid,
    lk, sw_in, yb, y_mid, y_up, y_dn, x_mid, x_up, x_dn, tb, ub, t_in, u_in,
    zk_out, zv_out, zk_in, zv_in, z_out, w_in,
    loc, xs, xr, us, ur, ds, dr, fs, fr, ws, wr,
    qs, qrs, os, ors, gs, grs, ss, sr, ys, yr, x2s, x2r, ts, tr, vs, vr,
    zks, zkr, zvs, zvr, w2s, w2r,
):
    ctx = lax.axis_index("ctx")
    y = lax.axis_index("seq")
    z = lax.axis_index("dp")
    x = ctx // NC
    k = lax.rem(ctx, NC)
    xu, xd, xo = lax.rem(x + 1, NX), lax.rem(x + NX - 1, NX), lax.rem(x + 2, NX)
    yu, yd, yo = lax.rem(y + 1, NY), lax.rem(y + NY - 1, NY), lax.rem(y + 2, NY)
    sib = {"ctx": x * NC + 1 - k}
    right, left = {"ctx": xu * NC + k}, {"ctx": xd * NC + k}
    up, down = {"seq": yu}, {"seq": yd}

    loads = []
    for n, (a, b) in enumerate((
        (lat_h, lat_v), (kr_h, kr_v), (qn_h, qn_v), (qr_h, qr_v), (do_h, do_v),
        (wk_h, wk_v), (wv_h, wv_v), (doc_h, doc_ref), (img_h, img_ref), (flag_h, flag_ref),
    )):
        loads.append(pltpu.make_async_copy(a, b, loc.at[n]))
        loads[-1].start()

    barrier = pltpu.get_barrier_semaphore()
    greet = [{"ctx": lax.rem(ctx + d, NCTX)} for d in range(1, NCTX)]
    greet += [{"seq": lax.rem(y + d, NY)} for d in range(1, NY)]
    greet += [{"dp": lax.rem(z + d, NZ)} for d in range(1, NZ)]
    for dev in greet:
        pl.semaphore_signal(barrier, inc=1, device_id=dev, device_id_type=MESH)
    loads[0].wait()
    loads[1].wait()
    comb[:, 0:LAT] = lat_v[0]
    comb[:, LAT : LAT + RD] = kr_v[0]
    comb[:, LAT + RD :] = kr_v[0]
    lat_all[x, k, y] = comb[...]
    pl.semaphore_wait(barrier, len(greet))
    sends = []

    def go(copy):
        copy.start()
        sends.append(copy)
        return copy

    mine = lat_all.at[x, k, y]
    xc = [go(rc(comb, mine, xs.at[0], xr.at[0], right)), go(rc(comb, mine, xs.at[1], xr.at[1], left))]
    ups = [go(rc(comb, mine, us.at[0], ur.at[0], up))]
    downs = [go(rc(comb, mine, ds.at[0], dr.at[0], down))]
    swaps = {0: go(rc(comb, mine, ws.at[0], wr.at[0], sib))}
    for n in range(2, 5):
        loads[n].wait()
    rows_n[...] = qn_v[0].astype(F32).reshape(TOK * HEADS, HD)
    rows_r[:, 0:RD] = qr_v[0].astype(F32).reshape(TOK * HEADS, RD)
    lane_t = lax.broadcasted_iota(jnp.int32, (TOK, 128), 1)

    def head(n):
        return pl.ds(n, TOK, stride=HEADS)

    for c in range(NCTX):
        for h in range(2):
            pack[c, :, h * 128 : (h + 1) * 128] = rows_n[head(2 * c + h), :].astype(BF)
        pack[c, :, 256:512] = do_v[0, :, c * 256 : (c + 1) * 256]
        pair = jnp.where(
            lane_t < RD, rows_r[head(2 * c), :], pltpu.roll(rows_r[head(2 * c + 1), :], RD, 1)
        )
        pack[c, :, 512:640] = pair.astype(BF)
    q_all[ctx] = pack[ctx]
    qx = Exchange(lambda c: pack.at[c], lambda c: q_all.at[c], q_mid, qs, qrs, sends)
    qx.start_far()
    half = TOK // 2
    top_r, bot_r = pl.ds(0, half), pl.ds(half, half)
    turn = (k, 1 - k)
    blocks = (x, xd, xu, xo)

    def blk(e, yy):
        return lat_all.at[blocks[e], k, yy]

    def swap(slot, b):
        swaps[slot] = go(rc(b, b, ws.at[slot], wr.at[slot], sib))

    def spread(e):
        b = blk(e, y)
        ups.append(go(rc(b, b, us.at[e], ur.at[e], up)))
        downs.append(go(rc(b, b, ds.at[e], dr.at[e], down)))
        swap(e, b)

    fwd = []

    def onward(e):
        way = turn[e // 2]
        ups[e].wait_recv()
        downs[e].wait_recv()
        b = blk(e, lax.rem(y + 3 + 2 * way, NY))
        fwd.append(go(rc(b, b, fs.at[e], fr.at[e], {"seq": lax.rem(y + 1 + 2 * way, NY)})))
        swap(4 + e, blk(e, yd))
        swap(8 + e, blk(e, yu))

    def last(e):
        fwd[e].wait_recv()
        swap(12 + e, blk(e, yo))

    def project(xx, kk):
        j = xx * NC + kk
        lat = lat_all[xx, kk, :, :, 0:LAT].reshape(CHUNK, LAT)
        kr = lat_all[xx, kk, :, :, LAT:PACK].reshape(CHUNK, 128)
        lt = lat.T
        lat_t[:, pl.ds(pl.multiple_of(j * CHUNK, CHUNK), CHUNK)] = lt
        kv = dot(lat, w_all[...]).astype(BF)
        kvt = dot(w_t[...], lt).astype(BF)
        krt = kr.T
        for h in range(2):
            kc[h, j, :, 0:128] = kv[:, h * 128 : (h + 1) * 128]
            kc[h, j, :, 128:256] = jnp.where((lane_k < RD) == (h == 0), kr, zero)
            kct[h, j, 0:128] = kvt[h * 128 : (h + 1) * 128]
            kct[h, j, 128:256] = jnp.where((row_k < RD) == (h == 0), krt, zero)
            v[h, j] = kv[:, 256 + h * 128 : 256 + (h + 1) * 128]
            vt[h, j] = kvt[256 + h * 128 : 256 + (h + 1) * 128]

    def queries():
        qx.finish()
        for h in range(2):
            for c in range(NCTX):
                r = slice(c * TOK, (c + 1) * TOK)
                qc[h, r, 0:128] = q_all[c, :, h * 128 : (h + 1) * 128]
                qc[h, r, 128:256] = q_all[c, :, 512:640]
            qct[h] = qc[h].T
            dot_t[h] = q_all[:, :, 256 + h * 128 : 256 + (h + 1) * 128].reshape(NQ, 128).T

    def score(xx, kk):
        j = xx * NC + kk
        thr = []
        for i in range(CHUNK // TOK):
            kb = j * (CHUNK // TOK) + i
            kcode = jnp.where(flag_ref[0, kb] == 1, doc_ref[0, kb] * 64 + img_ref[0, kb], -2)
            t = jnp.where(qdoc == doc_ref[0, kb], qpos - kb * TOK, -1)
            thr.append(jnp.where(qcode == kcode, NK, t))
        for h in range(2):
            raw = dot(kc[h, j], qct[h])
            top = mx[h]
            for i in range(CHUNK // TOK):
                m = jnp.where(sub <= thr[i], raw[i * TOK : (i + 1) * TOK] * SCALE2, NEG)
                sc[h, j, i * TOK : (i + 1) * TOK, :] = m
                top = jnp.maximum(top, jnp.max(m, axis=0, keepdims=True))
            mx[h] = top

    xc[0].wait_recv()
    b = lat_all.at[xd, k, y, top_r]
    xc.append(go(rc(b, b, xs.at[2], xr.at[2], right)))
    xc[1].wait_recv()
    b = lat_all.at[xu, k, y, bot_r]
    xc.append(go(rc(b, b, xs.at[3], xr.at[3], left)))
    spread(1)
    spread(2)
    qx.start_near()
    for n in range(5, 10):
        loads[n].wait()
    w_all[:, 0:256] = wk_v[...]
    w_all[:, 256:512] = wv_v[...]
    w_t[...] = w_all[...].T
    o_t[...] = jnp.zeros_like(o_t)
    mx[...] = jnp.full_like(mx, NEG)
    dq_t[...] = jnp.zeros_like(dq_t)

    lane_q = lax.broadcasted_iota(jnp.int32, (1, NQ), 1)
    grp = lane_q // TOK
    qdoc = jnp.zeros((1, NQ), jnp.int32)
    qcode = jnp.zeros((1, NQ), jnp.int32)
    for c in range(NCTX):
        b = NY * c + y
        qdoc = jnp.where(grp == c, doc_ref[0, b], qdoc)
        code = jnp.where(flag_ref[0, b] == 1, doc_ref[0, b] * 64 + img_ref[0, b], -1)
        qcode = jnp.where(grp == c, code, qcode)
    qpos = (NY * grp + y) * TOK + lane_q % TOK
    sub = lax.broadcasted_iota(jnp.int32, (TOK, 1), 0)
    lane_k = lax.broadcasted_iota(jnp.int32, (CHUNK, 128), 1)
    row_k = lax.broadcasted_iota(jnp.int32, (128, CHUNK), 0)
    zero = jnp.zeros((), BF)

    qx.relay()
    onward(0)
    xc[2].wait_recv()
    xc[3].wait_recv()
    spread(3)
    onward(1)
    last(0)
    project(blocks[0], k)
    onward(2)
    onward(3)
    last(1)
    project(blocks[1], k)
    last(2)
    project(blocks[2], k)
    last(3)
    project(blocks[3], k)
    queries()
    for e in range(NX):
        score(blocks[e], k)
    for e in range(NX):
        for slot in (e, 4 + e, 8 + e, 12 + e):
            swaps[slot].wait_recv()
        project(blocks[e], 1 - k)
        score(blocks[e], 1 - k)


    spans = []
    for j in range(NCH):
        lo = max(0, j - 1) // 2 * 2
        hi = min(NCTX, (min(NCTX, j + 5) + 1) // 2 * 2)
        spans.append((lo * TOK, hi * TOK))

    def splice(full, part, a, b):
        pieces = [full[:, 0:a]] if a else []
        pieces.append(part)
        if b < NQ:
            pieces.append(full[:, b:])
        return jnp.concatenate(pieces, axis=1) if len(pieces) > 1 else part

    top_s = [mx[h] for h in range(2)]
    tot = [jnp.zeros((1, NQ), F32)] * 2
    for j in range(NCH):
        a, b = spans[j]
        for h in range(2):
            p = jnp.exp2(sc[h, j, :, a:b] - top_s[h][:, a:b])
            sc[h, j, :, a:b] = p
            tot[h] = splice(tot[h], tot[h][:, a:b] + jnp.sum(p, axis=0, keepdims=True), a, b)
            o_t[h, :, a:b] += dot(vt[h, j], p.astype(BF))

    inv = [1.0 / tot[h] for h in range(2)]
    delta = []
    for h in range(2):
        out = o_t[h] * inv[h]
        o_out[:, :, h * 128 : (h + 1) * 128] = out.T.astype(BF).reshape(NCTX, TOK, 128)
        delta.append(jnp.sum(out * dot_t[h].astype(F32), axis=0, keepdims=True))
    ox = Exchange(lambda c: o_out.at[c], lambda c: o_in.at[c], o_mid, os, ors, sends)
    ox.start_far()
    ox.start_near()
    o_in[ctx] = o_out[ctx]

    for j in range(NCH):
        a, b = spans[j]
        r = slice(j * CHUNK, (j + 1) * CHUNK)
        for h in range(2):
            p = sc[h, j, :, a:b] * inv[h][:, a:b]
            do = q_all[a // TOK : b // TOK, :, 256 + h * 128 : 256 + (h + 1) * 128].reshape(b - a, 128)
            gv[r, h * 128 : (h + 1) * 128] = dot(p.astype(BF), do).astype(BF)

    def weight_grad(buf, g):
        for i in range(2):
            part = dot(lat_t[i * 256 : (i + 1) * 256, :], g[...]).astype(BF)
            buf[i * 4 : (i + 1) * 4] = part.reshape(4, TOK, 256)

    def send_z(buf, inbox, s_sem, r_sem):
        out = []
        for d in (4, 3, 5, 2, 6, 1, 7):
            to = lax.rem(z + d, NZ)
            out.append(go(rc(buf.at[to], inbox.at[d - 1], s_sem.at[d - 1], r_sem.at[d - 1], {"dp": to})))
        return out

    weight_grad(zv_out, gv)
    before = len(sends)
    zv = send_z(zv_out, zv_in, zvs, zvr)

    swc = []
    yc = {}

    def merge(xx):
        swc[xx].wait_recv()

        def add(i, carry):
            yb[xx, i] = (lk[xx, k, i].astype(F32) + sw_in[xx, i].astype(F32)).astype(BF)
            return carry

        lax.fori_loop(0, NY, add, 0)
        way = turn[xx % 2]
        far, back = lax.rem(y + 1 + 2 * way, NY), lax.rem(y + 3 + 2 * way, NY)
        yc[xx, 0] = go(rc(yb.at[xx, yo, top_r], y_mid.at[xx], ys.at[xx, 0], yr.at[xx, 0], {"seq": far}))
        yc[xx, 1] = go(rc(yb.at[xx, back, top_r], y_dn.at[xx], ys.at[xx, 1], yr.at[xx, 1], {"seq": back}))

    def pass_on(xx):
        far = lax.rem(y + 1 + 2 * turn[xx % 2], NY)
        yc[xx, 0].wait_recv()
        yb[xx, far, top_r] = (yb[xx, far, top_r].astype(F32) + y_mid[xx].astype(F32)).astype(BF)
        yc[xx, 2] = go(rc(yb.at[xx, far, top_r], y_up.at[xx], ys.at[xx, 2], yr.at[xx, 2], {"seq": far}))

    for j in range(NCH):
        a, b = spans[j]
        r = slice(j * CHUNK, (j + 1) * CHUNK)
        kr_g = []
        for h in range(2):
            dp = dot(v[h, j], dot_t[h, :, a:b])
            g = (sc[h, j, :, a:b] * ((dp - delta[h][:, a:b]) * inv[h][:, a:b])).astype(BF)
            dk = dot(g, qc[h, a:b, :]) * SCALE
            dq_t[h, :, a:b] += dot(kct[h, j], g)
            gk[r, h * 128 : (h + 1) * 128] = dk[:, 0:128].astype(BF)
            kr_g.append(dk[:, 128:256])
        xx, kk = j // NC, j % NC
        kr_part = jnp.where(lane_k < RD, kr_g[0], kr_g[1]).astype(BF)
        lk[xx, kk, :, :, LAT:PACK] = kr_part.reshape(NY, TOK, 128)
        lat_part = (dot(gk[r, :], w_t[0:256, :]) + dot(gv[r, :], w_t[256:512, :])).astype(BF)
        lk[xx, kk, :, :, 0:LAT] = lat_part.reshape(NY, TOK, LAT)
        if kk == 1:
            swc.append(go(rc(lk.at[xx, 1 - k], sw_in.at[xx], ss.at[xx], sr.at[xx], sib)))
        if j == 3:
            ox.relay()
        if j == 4:
            merge(0)
        if j == 6:
            merge(1)
        if j == 7:
            pass_on(0)
    d_cols = [(dq_t[h, 0:128, :] * SCALE).T.astype(BF) for h in range(2)]
    d_cols.append(((dq_t[0, 128:256, :] + dq_t[1, 128:256, :]) * SCALE).T.astype(BF))
    for n in range(3):
        d_out[:, :, n * 128 : (n + 1) * 128] = d_cols[n].reshape(NCTX, TOK, 128)
    dx = Exchange(lambda c: d_out.at[c], lambda c: d_in.at[c], d_mid, gs, grs, sends)
    dx.start_far()
    d_in[ctx] = d_out[ctx]
    merge(2)
    weight_grad(zk_out, gk)
    zk = send_z(zk_out, zk_in, zks, zkr)
    pass_on(1)
    merge(3)
    xcp = {}

    def x_go(n, src, dst, dev):
        xcp[n] = go(rc(src, dst, x2s.at[n], x2r.at[n], dev))

    one, two = pl.ds(0, 2), pl.ds(2, 2)
    x_go(0, yb.at[xo, one, bot_r], x_mid.at[0], right)
    x_go(1, yb.at[xo, two, bot_r], x_mid.at[1], left)
    x_go(2, yb.at[xu, two, bot_r], x_up.at[two], right)
    x_go(3, yb.at[xd, one, bot_r], x_dn.at[one], left)
    dx.start_near()
    for copy in sends[:before]:
        copy.wait_send()
    pass_on(2)
    pass_on(3)
    xcp[0].wait_recv()
    yb[xu, one, bot_r] = (yb[xu, one, bot_r].astype(F32) + x_mid[0].astype(F32)).astype(BF)
    x_go(4, yb.at[xu, one, bot_r], x_up.at[one], right)
    xcp[1].wait_recv()
    yb[xd, two, bot_r] = (yb[xd, two, bot_r].astype(F32) + x_mid[1].astype(F32)).astype(BF)
    x_go(5, yb.at[xd, two, bot_r], x_dn.at[two], left)
    dx.relay()

    results = []

    def put(n, a, b):
        results.append(pltpu.make_async_copy(a, b, outs.at[n]))
        results[-1].start()

    ox.finish()
    for c in range(NCTX):
        att_ref[0, :, c * 256 : (c + 1) * 256] = o_in[c]
    put(0, att_ref, att_h)

    def total_z(buf, inbox):
        t = buf[z].astype(F32)
        for d in range(NZ - 1):
            t = t + inbox[d].astype(F32)
        return t.astype(BF).reshape(NY, 16, 256)

    for copy in zv:
        copy.wait_recv()
    z_out[:, :, 256:512] = total_z(zv_out, zv_in)

    for xx in range(NX):
        yc[xx, 1].wait_recv()
        yc[xx, 2].wait_recv()
        t = yb[xx, y, top_r].astype(F32) + y_up[xx].astype(F32) + y_dn[xx].astype(F32)
        tb[xx] = t.astype(BF)
    tc, uc = [], []
    for d in (2, 1, 3):
        to = lax.rem(x + d, NX)
        tc.append(go(rc(tb.at[to], t_in.at[d - 1], ts.at[d - 1], tr.at[d - 1], {"ctx": to * NC + k})))
    for n in range(2, 6):
        xcp[n].wait_recv()
    for i in range(NY):
        t = yb[x, i, bot_r].astype(F32) + x_up[i].astype(F32) + x_dn[i].astype(F32)
        ub[i] = t.astype(BF)
    for d in (2, 1, 3):
        to = lax.rem(y + d, NY)
        uc.append(go(rc(ub.at[to], u_in.at[d - 1], vs.at[d - 1], vr.at[d - 1], {"seq": to})))
    for copy in zk:
        copy.wait_recv()
    z_out[:, :, 0:256] = total_z(zk_out, zk_in)
    wc = []
    for d in (2, 1, 3):
        to = lax.rem(y + d, NY)
        wc.append(go(rc(z_out.at[to], w_in.at[d - 1], w2s.at[d - 1], w2r.at[d - 1], {"seq": to})))
    dx.finish()
    for c in range(NCTX):
        for h in range(2):
            rows_n[head(2 * c + h), :] = d_in[c, :, h * 128 : (h + 1) * 128].astype(F32)
        pair = d_in[c, :, 256:384].astype(F32)
        rows_r[head(2 * c), :] = pair
        rows_r[head(2 * c + 1), :] = pltpu.roll(pair, RD, 1)
    qng_ref[0] = rows_n[...].reshape(TOK, HEADS, HD).astype(BF)
    qrg_ref[0] = rows_r[:, 0:RD].reshape(TOK, HEADS, RD).astype(BF)
    put(1, qng_ref, qng_h)
    put(2, qrg_ref, qrg_h)
    for own, inbox, copies, rows in ((tb.at[x], t_in, tc, top_r), (ub.at[y], u_in, uc, bot_r)):
        for copy in copies:
            copy.wait_recv()
        t = own[...].astype(F32)
        for d in range(3):
            t = t + inbox[d].astype(F32)
        latg_ref[0, rows] = t[:, 0:LAT].astype(BF)
        krg_ref[0, rows] = (t[:, LAT : LAT + RD] + t[:, LAT + RD :]).astype(BF)
    put(3, latg_ref, latg_h)
    put(4, krg_ref, krg_h)
    for copy in wc:
        copy.wait_recv()
    t = z_out[y].astype(F32)
    for d in range(NY - 1):
        t = t + w_in[d].astype(F32)
    wkg_ref[...] = t[:, 0:256]
    wvg_ref[...] = t[:, 256:512]
    put(5, wkg_ref, wkg_h)
    put(6, wvg_ref, wvg_h)
    for copy in sends[before:]:
        copy.wait_send()
    for copy in results:
        copy.wait()


OUTS = (
    ((1, TOK, HEADS * HD), BF),
    ((1, TOK, HEADS, HD), BF),
    ((1, TOK, HEADS, RD), BF),
    ((1, TOK, LAT), BF),
    ((1, TOK, RD), BF),
    ((16, 256), F32),
    ((16, 256), F32),
)


def core(*args):
    def vm(*shape, dtype=BF):
        return pltpu.VMEM(shape, dtype)

    half = TOK // 2
    table = pltpu.SMEM((1, NX * NC * NY), jnp.int32)
    return pl.pallas_call(
        core_kernel,
        out_shape=tuple(jax.ShapeDtypeStruct(s, d) for s, d in OUTS),
        in_specs=[ANY] * 10,
        out_specs=(ANY,) * 7,
        scratch_shapes=[
            *(pltpu.VMEM(s, d) for s, d in OUTS),
            vm(TOK * HEADS, 128, dtype=F32), vm(TOK * HEADS, 128, dtype=F32), DMA((7,)),
            vm(1, TOK, HEADS, HD), vm(1, TOK, HEADS, RD), vm(1, TOK, HEADS * HD),
            vm(1, TOK, LAT), vm(1, TOK, RD), vm(LAT, 256), vm(LAT, 256),
            table, table, table,
            vm(TOK, PACK), vm(NCTX, TOK, PACK), vm(NCTX, TOK, PACK), vm(2, TOK, PACK),
            vm(NX, NC, NY, TOK, PACK),
            vm(LAT, 512), vm(512, LAT), vm(LAT, NK),
            vm(2, NCH, CHUNK, 256), vm(2, NCH, 256, CHUNK),
            vm(2, NCH, CHUNK, 128), vm(2, NCH, 128, CHUNK),
            vm(2, NQ, 256), vm(2, 256, NQ), vm(2, 128, NQ),
            vm(2, NCH, CHUNK, NQ, dtype=F32), vm(2, 1, NQ, dtype=F32),
            vm(NK, 256), vm(NK, 256),
            vm(2, 128, NQ, dtype=F32), vm(2, 256, NQ, dtype=F32),
            vm(NCTX, TOK, 256), vm(NCTX, TOK, 256), vm(2, TOK, 256),
            vm(NCTX, TOK, 384), vm(NCTX, TOK, 384), vm(2, TOK, 384),
            vm(NX, NC, NY, TOK, PACK), vm(NX, NY, TOK, PACK), vm(NX, NY, TOK, PACK),
            vm(NX, half, PACK), vm(NX, half, PACK), vm(NX, half, PACK),
            vm(2, 2, half, PACK), vm(NY, half, PACK), vm(NY, half, PACK),
            vm(NX, half, PACK), vm(NY, half, PACK), vm(3, half, PACK), vm(3, half, PACK),
            vm(NZ, TOK, 256), vm(NZ, TOK, 256), vm(NZ - 1, TOK, 256), vm(NZ - 1, TOK, 256),
            vm(NY, 16, 512), vm(NY - 1, 16, 512),
            DMA((10,)), DMA((4,)), DMA((4,)), DMA((4,)), DMA((4,)), DMA((4,)), DMA((4,)),
            DMA((4,)), DMA((4,)), DMA((16,)), DMA((16,)),
            DMA((9,)), DMA((9,)), DMA((9,)), DMA((9,)), DMA((9,)), DMA((9,)),
            DMA((4,)), DMA((4,)), DMA((4, 3)), DMA((4, 3)), DMA((6,)), DMA((6,)),
            DMA((3,)), DMA((3,)), DMA((3,)), DMA((3,)),
            DMA((7,)), DMA((7,)), DMA((7,)), DMA((7,)), DMA((3,)), DMA((3,)),
        ],
        compiler_params=pltpu.CompilerParams(
            collective_id=0, has_side_effects=True, vmem_limit_bytes=60 * 2**20
        ),
        name="core",
    )(*args)


def store_kernel(*refs):
    src, dst, mid, lsem, ssem = refs[0:7], refs[7:14], refs[14:21], refs[21], refs[22]
    reads = [pltpu.make_async_copy(src[n], mid[n], lsem.at[n]) for n in range(7)]
    writes = [pltpu.make_async_copy(mid[n], dst[n], ssem.at[n]) for n in range(7)]
    for copy in reads:
        copy.start()
    for n in range(7):
        reads[n].wait()
        writes[n].start()
    for copy in writes:
        copy.wait()


def store(*arrays):
    return pl.pallas_call(
        store_kernel,
        out_shape=tuple(jax.ShapeDtypeStruct(s, d) for s, d in OUTS),
        in_specs=[ANY] * 7,
        out_specs=(ANY,) * 7,
        scratch_shapes=[*(pltpu.VMEM(s, d) for s, d in OUTS), DMA((7,)), DMA((7,))],
        compiler_params=pltpu.CompilerParams(vmem_limit_bytes=60 * 2**20),
        name="store",
    )(*arrays)


def on_device(
    query_nope, query_rope, latent, key_rope, out_grad,
    key_weight, value_weight, block_doc, block_image, block_flag,
):
    return store(*core(
        query_nope, query_rope, out_grad, latent, key_rope,
        key_weight, value_weight, block_doc, block_image, block_flag,
    ))


def solution(mesh):
    return jax.shard_map(
        on_device,
        mesh=mesh,
        in_specs=(
            P("dp", ("ctx", "seq"), None, None),
            P("dp", ("ctx", "seq"), None, None),
            P("dp", ("ctx", "seq"), None),
            P("dp", ("ctx", "seq"), None),
            P("dp", ("ctx", "seq"), None),
            P(None, "ctx"),
            P(None, "ctx"),
            P("dp", None),
            P("dp", None),
            P("dp", None),
        ),
        out_specs=(
            P("dp", ("ctx", "seq"), None),
            P("dp", ("ctx", "seq"), None, None),
            P("dp", ("ctx", "seq"), None, None),
            P("dp", ("ctx", "seq"), None),
            P("dp", ("ctx", "seq"), None),
            P(("dp", "seq"), "ctx"),
            P(("dp", "seq"), "ctx"),
        ),
        check_vma=False,
    )
```

```python
import math

import jax
import jax.numpy as jnp
from jax import lax
from jax.experimental import pallas as pl
from jax.experimental.pallas import tpu as pltpu
from jax.sharding import PartitionSpec as P

NEG = -1e30
MESH = pl.DeviceIdType.MESH
ANY = pl.BlockSpec(memory_space=pl.ANY)
DMA = pltpu.SemaphoreType.DMA
BF = jnp.bfloat16
F32 = jnp.float32

NX, NC, NY, NZ = 4, 2, 4, 8
NCTX = NX * NC
TOK, HEADS, HD, RD, LAT = 64, 16, 128, 64, 512
PACK = 640
ROWS = TOK * LAT // 128 + TOK * RD // 128
KROW = TOK * LAT // 128
NQ = NCTX * TOK
NK = NX * NC * NY * TOK
CHUNK = 256
NCH = NK // CHUNK
SCALE = 1.0 / math.sqrt(HD + RD)
SCALE2 = SCALE * math.log2(math.e)


def rc(src, dst, send, recv, dev):
    return pltpu.make_async_remote_copy(
        src_ref=src, dst_ref=dst, send_sem=send, recv_sem=recv, device_id=dev, device_id_type=MESH
    )


def dot(a, b):
    return jnp.dot(a, b, preferred_element_type=F32)


class Exchange:
    def __init__(self, src, dst, relay, ss, rs, sends):
        ctx = lax.axis_index("ctx")
        self.me = ctx
        x, k = ctx // NC, lax.rem(ctx, NC)
        self.right, self.left = lax.rem(x + 1, NX) * NC, lax.rem(x + NX - 1, NX) * NC
        self.far = lax.rem(x + 2, NX) * NC
        self.x, self.k = x * NC, k
        self.src, self.dst, self.mid = src, dst, relay
        self.ss, self.rs, self.sends = ss, rs, sends
        self.slots = {}

    def go(self, slot, src, dst, send, recv, to):
        copy = rc(src, dst, self.ss.at[send], self.rs.at[recv], {"ctx": to})
        copy.start()
        self.sends.append(copy)
        self.slots[slot] = copy

    def start_far(self):
        k = self.k
        self.go(7, self.src(self.far + k), self.mid.at[0], 5, 7, self.right + k)
        self.go(8, self.src(self.far + 1 - k), self.mid.at[1], 6, 8, self.left + k)

    def start_near(self):
        k, me = self.k, self.me
        for slot, to in (
            (1, self.right + k), (3, self.left + k),
            (2, self.right + 1 - k), (4, self.left + 1 - k),
            (0, self.x + 1 - k),
        ):
            self.go(slot, self.src(to), self.dst(me), slot, slot, to)

    def relay(self):
        k = self.k
        self.slots[7].wait_recv()
        self.go(5, self.mid.at[0], self.dst(self.left + k), 7, 5, self.right + k)
        self.slots[8].wait_recv()
        self.go(6, self.mid.at[1], self.dst(self.right + k), 8, 6, self.left + 1 - k)

    def finish(self):
        for slot in range(7):
            self.slots[slot].wait_recv()


def core_kernel(
    qn_h, qr_h, do_h, lat_h, kr_h, wk_h, wv_h, doc_h, img_h, flag_h,
    att_h, qng_h, qrg_h, latg_h, krg_h, wkg_h, wvg_h,
    att_ref, qng_ref, qrg_ref, latg_ref, krg_ref, wkg_ref, wvg_ref, rows_n, rows_r, outs,
    qn_v, qr_v, do_v, lat_v, kr_v, wk_v, wv_v, doc_ref, img_ref, flag_ref,
    comb, pack, q_all, q_mid, lat_all,
    w_all, w_t, lat_t, kc, kct, v, vt, qc, qct, dot_t, sc, mx, pb, do_s, gk, gv, o_t, dq_t,
    o_out, o_in, o_mid, d_out, d_in, d_mid,
    lk, sw_in, yb, y_mid, y_up, y_dn, x_mid, x_up, x_dn, tb, ub, t_in, u_in,
    zk_out, zv_out, zk_in, zv_in, z_out, w_in,
    loc, xs, xr, us, ur, ds, dr, fs, fr, ws, wr,
    qs, qrs, os, ors, gs, grs, ss, sr, ys, yr, x2s, x2r, ts, tr, vs, vr,
    zks, zkr, zvs, zvr, w2s, w2r,
):
    ctx = lax.axis_index("ctx")
    y = lax.axis_index("seq")
    z = lax.axis_index("dp")
    x = ctx // NC
    k = lax.rem(ctx, NC)
    xu, xd, xo = lax.rem(x + 1, NX), lax.rem(x + NX - 1, NX), lax.rem(x + 2, NX)
    yu, yd, yo = lax.rem(y + 1, NY), lax.rem(y + NY - 1, NY), lax.rem(y + 2, NY)
    sib = {"ctx": x * NC + 1 - k}
    right, left = {"ctx": xu * NC + k}, {"ctx": xd * NC + k}
    up, down = {"seq": yu}, {"seq": yd}

    loads = []
    for n, (a, b) in enumerate((
        (lat_h, lat_v), (kr_h, kr_v), (qn_h, qn_v), (qr_h, qr_v), (do_h, do_v),
        (wk_h, wk_v), (wv_h, wv_v), (doc_h, doc_ref), (img_h, img_ref), (flag_h, flag_ref),
    )):
        loads.append(pltpu.make_async_copy(a, b, loc.at[n]))
        loads[-1].start()

    barrier = pltpu.get_barrier_semaphore()
    greet = [{"ctx": lax.rem(ctx + d, NCTX)} for d in range(1, NCTX)]
    greet += [{"seq": lax.rem(y + d, NY)} for d in range(1, NY)]
    greet += [{"dp": lax.rem(z + d, NZ)} for d in range(1, NZ)]
    for dev in greet:
        pl.semaphore_signal(barrier, inc=1, device_id=dev, device_id_type=MESH)
    loads[0].wait()
    loads[1].wait()
    for t in range(LAT // 128):
        comb[t * TOK : (t + 1) * TOK, :] = lat_v[0, :, t * 128 : (t + 1) * 128]
    comb[KROW:ROWS, 0:RD] = kr_v[0, 0 : TOK // 2]
    comb[KROW:ROWS, RD:] = kr_v[0, TOK // 2 :]
    lat_all[x, k, y] = comb[...]
    pl.semaphore_wait(barrier, len(greet))
    sends = []

    def go(copy):
        copy.start()
        sends.append(copy)
        return copy

    mine = lat_all.at[x, k, y]
    xc = [go(rc(comb, mine, xs.at[0], xr.at[0], right)), go(rc(comb, mine, xs.at[1], xr.at[1], left))]
    ups = [go(rc(comb, mine, us.at[0], ur.at[0], up))]
    downs = [go(rc(comb, mine, ds.at[0], dr.at[0], down))]
    swaps = {0: go(rc(comb, mine, ws.at[0], wr.at[0], sib))}
    for n in range(2, 5):
        loads[n].wait()
    rows_n[...] = qn_v[0].astype(F32).reshape(TOK * HEADS, HD)
    rows_r[:, 0:RD] = qr_v[0].astype(F32).reshape(TOK * HEADS, RD)
    lane_t = lax.broadcasted_iota(jnp.int32, (TOK, 128), 1)

    def head(n):
        return pl.ds(n, TOK, stride=HEADS)

    for c in range(NCTX):
        for h in range(2):
            pack[c, :, h * 128 : (h + 1) * 128] = rows_n[head(2 * c + h), :].astype(BF)
        pack[c, :, 256:512] = do_v[0, :, c * 256 : (c + 1) * 256]
        pair = jnp.where(
            lane_t < RD, rows_r[head(2 * c), :], pltpu.roll(rows_r[head(2 * c + 1), :], RD, 1)
        )
        pack[c, :, 512:640] = pair.astype(BF)
    q_all[ctx] = pack[ctx]
    qx = Exchange(lambda c: pack.at[c], lambda c: q_all.at[c], q_mid, qs, qrs, sends)
    qx.start_far()
    half = ROWS // 2
    top_r, bot_r = pl.ds(0, half), pl.ds(half, half)
    turn = (k, 1 - k)
    blocks = (x, xd, xu, xo)

    def blk(e, yy):
        return lat_all.at[blocks[e], k, yy]

    def swap(slot, b):
        swaps[slot] = go(rc(b, b, ws.at[slot], wr.at[slot], sib))

    def spread(e):
        b = blk(e, y)
        ups.append(go(rc(b, b, us.at[e], ur.at[e], up)))
        downs.append(go(rc(b, b, ds.at[e], dr.at[e], down)))
        swap(e, b)

    fwd = []

    def onward(e):
        way = turn[e // 2]
        ups[e].wait_recv()
        downs[e].wait_recv()
        b = blk(e, lax.rem(y + 3 + 2 * way, NY))
        fwd.append(go(rc(b, b, fs.at[e], fr.at[e], {"seq": lax.rem(y + 1 + 2 * way, NY)})))
        swap(4 + e, blk(e, yd))
        swap(8 + e, blk(e, yu))

    def last(e):
        fwd[e].wait_recv()
        swap(12 + e, blk(e, yo))

    def project(xx, kk):
        j = xx * NC + kk
        lat = jnp.concatenate(
            [lat_all[xx, kk, :, t * TOK : (t + 1) * TOK, :].reshape(CHUNK, 128) for t in range(LAT // 128)],
            axis=1,
        )
        side = lat_all[xx, kk, :, KROW:ROWS, :].reshape(128, 128).astype(F32)
        swung = pltpu.roll(side, RD, 1)
        first = jnp.where(lane_h < RD, side, swung).reshape(NY, TOK // 2, 128)
        second = jnp.where(lane_h < RD, swung, side).reshape(NY, TOK // 2, 128)
        kr = jnp.concatenate([first, second], axis=1).reshape(CHUNK, 128).astype(BF)
        lt = lat.T
        lat_t[:, pl.ds(pl.multiple_of(j * CHUNK, CHUNK), CHUNK)] = lt
        kv = dot(lat, w_all[...]).astype(BF)
        kvt = dot(w_t[...], lt).astype(BF)
        krt = kr.T
        for h in range(2):
            kc[h, j, :, 0:128] = kv[:, h * 128 : (h + 1) * 128]
            kc[h, j, :, 128:256] = jnp.where((lane_k < RD) == (h == 0), kr, zero)
            kct[h, j, 0:128] = kvt[h * 128 : (h + 1) * 128]
            kct[h, j, 128:256] = jnp.where((row_k < RD) == (h == 0), krt, zero)
            v[h, j] = kv[:, 256 + h * 128 : 256 + (h + 1) * 128]
            vt[h, j] = kvt[256 + h * 128 : 256 + (h + 1) * 128]

    def queries():
        qx.finish()
        for h in range(2):
            for c in range(NCTX):
                r = slice(c * TOK, (c + 1) * TOK)
                qc[h, r, 0:128] = q_all[c, :, h * 128 : (h + 1) * 128]
                qc[h, r, 128:256] = q_all[c, :, 512:640]
            qct[h] = qc[h].T
            dot_t[h] = q_all[:, :, 256 + h * 128 : 256 + (h + 1) * 128].reshape(NQ, 128).T

    def score(xx, kk):
        j = xx * NC + kk
        thr = []
        for i in range(CHUNK // TOK):
            kb = j * (CHUNK // TOK) + i
            kcode = jnp.where(flag_ref[0, kb] == 1, doc_ref[0, kb] * 64 + img_ref[0, kb], -2)
            t = jnp.where(qdoc == doc_ref[0, kb], qpos - kb * TOK, -1)
            thr.append(jnp.where(qcode == kcode, NK, t))
        for h in range(2):
            raw = dot(kc[h, j], qct[h])
            top = mx[h]
            for i in range(CHUNK // TOK):
                m = jnp.where(sub <= thr[i], raw[i * TOK : (i + 1) * TOK] * SCALE2, NEG)
                sc[h, j, i * TOK : (i + 1) * TOK, :] = m
                top = jnp.maximum(top, jnp.max(m, axis=0, keepdims=True))
            mx[h] = top

    xc[0].wait_recv()
    b = lat_all.at[xd, k, y, top_r]
    xc.append(go(rc(b, b, xs.at[2], xr.at[2], right)))
    xc[1].wait_recv()
    b = lat_all.at[xu, k, y, bot_r]
    xc.append(go(rc(b, b, xs.at[3], xr.at[3], left)))
    spread(1)
    spread(2)
    qx.start_near()
    for n in range(5, 10):
        loads[n].wait()
    w_all[:, 0:256] = wk_v[...]
    w_all[:, 256:512] = wv_v[...]
    w_t[...] = w_all[...].T
    o_t[...] = jnp.zeros_like(o_t)
    mx[...] = jnp.full_like(mx, NEG)
    dq_t[...] = jnp.zeros_like(dq_t)

    lane_q = lax.broadcasted_iota(jnp.int32, (1, NQ), 1)
    grp = lane_q // TOK
    qdoc = jnp.zeros((1, NQ), jnp.int32)
    qcode = jnp.zeros((1, NQ), jnp.int32)
    for c in range(NCTX):
        b = NY * c + y
        qdoc = jnp.where(grp == c, doc_ref[0, b], qdoc)
        code = jnp.where(flag_ref[0, b] == 1, doc_ref[0, b] * 64 + img_ref[0, b], -1)
        qcode = jnp.where(grp == c, code, qcode)
    qpos = (NY * grp + y) * TOK + lane_q % TOK
    sub = lax.broadcasted_iota(jnp.int32, (TOK, 1), 0)
    lane_k = lax.broadcasted_iota(jnp.int32, (CHUNK, 128), 1)
    row_k = lax.broadcasted_iota(jnp.int32, (128, CHUNK), 0)
    lane_h = lax.broadcasted_iota(jnp.int32, (128, 128), 1)
    zero = jnp.zeros((), BF)

    qx.relay()
    onward(0)
    xc[2].wait_recv()
    xc[3].wait_recv()
    spread(3)
    onward(1)
    last(0)
    project(blocks[0], k)
    onward(2)
    onward(3)
    last(1)
    project(blocks[1], k)
    last(2)
    project(blocks[2], k)
    last(3)
    project(blocks[3], k)
    queries()
    for e in range(NX):
        score(blocks[e], k)
    for e in range(NX):
        for slot in (e, 4 + e, 8 + e, 12 + e):
            swaps[slot].wait_recv()
        project(blocks[e], 1 - k)
        score(blocks[e], 1 - k)


    spans = []
    for j in range(NCH):
        lo = max(0, j - 1) // 2 * 2
        hi = min(NCTX, (min(NCTX, j + 5) + 1) // 2 * 2)
        spans.append((lo * TOK, hi * TOK))

    def splice(full, part, a, b):
        pieces = [full[:, 0:a]] if a else []
        pieces.append(part)
        if b < NQ:
            pieces.append(full[:, b:])
        return jnp.concatenate(pieces, axis=1) if len(pieces) > 1 else part

    top_s = [mx[h] for h in range(2)]
    tot = [jnp.zeros((1, NQ), F32)] * 2
    for j in range(NCH):
        a, b = spans[j]
        for h in range(2):
            p = jnp.exp2(sc[h, j, :, a:b] - top_s[h][:, a:b])
            pb[h, j, :, a:b] = p.astype(BF)
            tot[h] = splice(tot[h], tot[h][:, a:b] + jnp.sum(p, axis=0, keepdims=True), a, b)
            o_t[h, :, a:b] += dot(vt[h, j], pb[h, j, :, a:b])

    inv = [1.0 / tot[h] for h in range(2)]
    delta = []
    for h in range(2):
        out = o_t[h] * inv[h]
        o_out[:, :, h * 128 : (h + 1) * 128] = out.T.astype(BF).reshape(NCTX, TOK, 128)
        cot = dot_t[h].astype(F32)
        delta.append(jnp.sum(out * cot, axis=0, keepdims=True))
        do_s[h] = (cot * inv[h]).astype(BF).T
    scaled = [inv[h] * SCALE for h in range(2)]
    ox = Exchange(lambda c: o_out.at[c], lambda c: o_in.at[c], o_mid, os, ors, sends)
    ox.start_far()
    ox.start_near()
    o_in[ctx] = o_out[ctx]

    for j in range(NCH):
        a, b = spans[j]
        r = slice(j * CHUNK, (j + 1) * CHUNK)
        for h in range(2):
            part = dot(pb[h, j, :, a:b], do_s[h, a:b, :])
            gv[r, h * 128 : (h + 1) * 128] = part.astype(BF)

    def weight_grad(buf, g):
        for i in range(2):
            part = dot(lat_t[i * 256 : (i + 1) * 256, :], g[...]).astype(BF)
            buf[i * 4 : (i + 1) * 4] = part.reshape(4, TOK, 256)

    def send_z(buf, inbox, s_sem, r_sem):
        out = []
        for d in (4, 3, 5, 2, 6, 1, 7):
            to = lax.rem(z + d, NZ)
            out.append(go(rc(buf.at[to], inbox.at[d - 1], s_sem.at[d - 1], r_sem.at[d - 1], {"dp": to})))
        return out

    weight_grad(zv_out, gv)
    before = len(sends)
    zv = send_z(zv_out, zv_in, zvs, zvr)

    swc = []
    yc = {}

    def merge(xx):
        swc[xx].wait_recv()

        def add(i, carry):
            yb[xx, i] = (lk[xx, k, i].astype(F32) + sw_in[xx, i].astype(F32)).astype(BF)
            return carry

        lax.fori_loop(0, NY, add, 0)
        way = turn[xx % 2]
        far, back = lax.rem(y + 1 + 2 * way, NY), lax.rem(y + 3 + 2 * way, NY)
        yc[xx, 0] = go(rc(yb.at[xx, yo, top_r], y_mid.at[xx], ys.at[xx, 0], yr.at[xx, 0], {"seq": far}))
        yc[xx, 1] = go(rc(yb.at[xx, back, top_r], y_dn.at[xx], ys.at[xx, 1], yr.at[xx, 1], {"seq": back}))

    def pass_on(xx):
        far = lax.rem(y + 1 + 2 * turn[xx % 2], NY)
        yc[xx, 0].wait_recv()
        yb[xx, far, top_r] = (yb[xx, far, top_r].astype(F32) + y_mid[xx].astype(F32)).astype(BF)
        yc[xx, 2] = go(rc(yb.at[xx, far, top_r], y_up.at[xx], ys.at[xx, 2], yr.at[xx, 2], {"seq": far}))

    for j in range(NCH):
        a, b = spans[j]
        r = slice(j * CHUNK, (j + 1) * CHUNK)
        kr_g = []
        for h in range(2):
            dp = dot(v[h, j], dot_t[h, :, a:b])
            g = pb[h, j, :, a:b].astype(F32) * ((dp - delta[h][:, a:b]) * scaled[h][:, a:b])
            g = g.astype(BF)
            dk = dot(g, qc[h, a:b, :])
            dq_t[h, :, a:b] += dot(kct[h, j], g)
            gk[r, h * 128 : (h + 1) * 128] = dk[:, 0:128].astype(BF)
            kr_g.append(dk[:, 128:256])
        xx, kk = j // NC, j % NC
        both = kr_g[0] + pltpu.roll(kr_g[1], RD, 1)
        moved = pltpu.roll(both, RD, 1).reshape(NY, TOK, 128)[:, TOK // 2 :]
        both = both.reshape(NY, TOK, 128)[:, : TOK // 2]
        kr_part = jnp.where(lane_h < RD, both.reshape(128, 128), moved.reshape(128, 128)).astype(BF)
        lk[xx, kk, :, KROW:ROWS, :] = kr_part.reshape(NY, TOK // 2, 128)
        lat_part = (dot(gk[r, :], w_t[0:256, :]) + dot(gv[r, :], w_t[256:512, :])).astype(BF)
        for t in range(LAT // 128):
            tile = lat_part[:, t * 128 : (t + 1) * 128].reshape(NY, TOK, 128)
            lk[xx, kk, :, t * TOK : (t + 1) * TOK, :] = tile
        if kk == 1:
            swc.append(go(rc(lk.at[xx, 1 - k], sw_in.at[xx], ss.at[xx], sr.at[xx], sib)))
        if j == 3:
            ox.relay()
        if j == 4:
            merge(0)
        if j == 6:
            merge(1)
        if j == 7:
            pass_on(0)
    merge(2)
    weight_grad(zk_out, gk)
    zk = send_z(zk_out, zk_in, zks, zkr)
    d_cols = [dq_t[h, 0:128, :].T.astype(BF) for h in range(2)]
    d_cols.append((dq_t[0, 128:256, :] + dq_t[1, 128:256, :]).T.astype(BF))
    for n in range(3):
        d_out[:, :, n * 128 : (n + 1) * 128] = d_cols[n].reshape(NCTX, TOK, 128)
    dx = Exchange(lambda c: d_out.at[c], lambda c: d_in.at[c], d_mid, gs, grs, sends)
    dx.start_far()
    d_in[ctx] = d_out[ctx]
    pass_on(1)
    merge(3)
    xcp = {}

    def x_go(n, src, dst, dev):
        xcp[n] = go(rc(src, dst, x2s.at[n], x2r.at[n], dev))

    one, two = pl.ds(0, 2), pl.ds(2, 2)
    x_go(0, yb.at[xo, one, bot_r], x_mid.at[0], right)
    x_go(1, yb.at[xo, two, bot_r], x_mid.at[1], left)
    x_go(2, yb.at[xu, two, bot_r], x_up.at[two], right)
    x_go(3, yb.at[xd, one, bot_r], x_dn.at[one], left)
    dx.start_near()
    for copy in sends[:before]:
        copy.wait_send()
    pass_on(2)
    pass_on(3)
    xcp[0].wait_recv()
    yb[xu, one, bot_r] = (yb[xu, one, bot_r].astype(F32) + x_mid[0].astype(F32)).astype(BF)
    x_go(4, yb.at[xu, one, bot_r], x_up.at[one], right)
    xcp[1].wait_recv()
    yb[xd, two, bot_r] = (yb[xd, two, bot_r].astype(F32) + x_mid[1].astype(F32)).astype(BF)
    x_go(5, yb.at[xd, two, bot_r], x_dn.at[two], left)
    dx.relay()

    results = []

    def put(n, a, b):
        results.append(pltpu.make_async_copy(a, b, outs.at[n]))
        results[-1].start()

    ox.finish()
    for c in range(NCTX):
        att_ref[0, :, c * 256 : (c + 1) * 256] = o_in[c]
    put(0, att_ref, att_h)

    def total_z(buf, inbox):
        t = buf[z].astype(F32)
        for d in range(NZ - 1):
            t = t + inbox[d].astype(F32)
        return t.astype(BF).reshape(NY, 16, 256)

    for copy in zv:
        copy.wait_recv()
    z_out[:, :, 256:512] = total_z(zv_out, zv_in)

    for xx in range(NX):
        yc[xx, 1].wait_recv()
        yc[xx, 2].wait_recv()
        t = yb[xx, y, top_r].astype(F32) + y_up[xx].astype(F32) + y_dn[xx].astype(F32)
        tb[xx] = t.astype(BF)
    tc, uc = [], []
    for d in (2, 1, 3):
        to = lax.rem(x + d, NX)
        tc.append(go(rc(tb.at[to], t_in.at[d - 1], ts.at[d - 1], tr.at[d - 1], {"ctx": to * NC + k})))
    for n in range(2, 6):
        xcp[n].wait_recv()
    for i in range(NY):
        t = yb[x, i, bot_r].astype(F32) + x_up[i].astype(F32) + x_dn[i].astype(F32)
        ub[i] = t.astype(BF)
    for d in (2, 1, 3):
        to = lax.rem(y + d, NY)
        uc.append(go(rc(ub.at[to], u_in.at[d - 1], vs.at[d - 1], vr.at[d - 1], {"seq": to})))
    for copy in zk:
        copy.wait_recv()
    z_out[:, :, 0:256] = total_z(zk_out, zk_in)
    wc = []
    for d in (2, 1, 3):
        to = lax.rem(y + d, NY)
        wc.append(go(rc(z_out.at[to], w_in.at[d - 1], w2s.at[d - 1], w2r.at[d - 1], {"seq": to})))
    dx.finish()
    for c in range(NCTX):
        for h in range(2):
            rows_n[head(2 * c + h), :] = d_in[c, :, h * 128 : (h + 1) * 128].astype(F32)
        pair = d_in[c, :, 256:384].astype(F32)
        rows_r[head(2 * c), :] = pair
        rows_r[head(2 * c + 1), :] = pltpu.roll(pair, RD, 1)
    qng_ref[0] = rows_n[...].reshape(TOK, HEADS, HD).astype(BF)
    qrg_ref[0] = rows_r[:, 0:RD].reshape(TOK, HEADS, RD).astype(BF)
    put(1, qng_ref, qng_h)
    put(2, qrg_ref, qrg_h)
    for own, inbox, copies, rows in ((tb.at[x], t_in, tc, top_r), (ub.at[y], u_in, uc, bot_r)):
        for copy in copies:
            copy.wait_recv()
        t = own[...].astype(F32)
        for d in range(3):
            t = t + inbox[d].astype(F32)
        rows_n[rows] = t
    for t in range(LAT // 128):
        latg_ref[0, :, t * 128 : (t + 1) * 128] = rows_n[t * TOK : (t + 1) * TOK, :].astype(BF)
    krg_ref[0, 0 : TOK // 2] = rows_n[KROW:ROWS, 0:RD].astype(BF)
    krg_ref[0, TOK // 2 :] = rows_n[KROW:ROWS, RD:].astype(BF)
    put(3, latg_ref, latg_h)
    put(4, krg_ref, krg_h)
    for copy in wc:
        copy.wait_recv()
    t = z_out[y].astype(F32)
    for d in range(NY - 1):
        t = t + w_in[d].astype(F32)
    wkg_ref[...] = t[:, 0:256]
    wvg_ref[...] = t[:, 256:512]
    put(5, wkg_ref, wkg_h)
    put(6, wvg_ref, wvg_h)
    for copy in sends[before:]:
        copy.wait_send()
    for copy in results:
        copy.wait()


OUTS = (
    ((1, TOK, HEADS * HD), BF),
    ((1, TOK, HEADS, HD), BF),
    ((1, TOK, HEADS, RD), BF),
    ((1, TOK, LAT), BF),
    ((1, TOK, RD), BF),
    ((16, 256), F32),
    ((16, 256), F32),
)


def core(*args):
    def vm(*shape, dtype=BF):
        return pltpu.VMEM(shape, dtype)

    half = ROWS // 2
    table = pltpu.SMEM((1, NX * NC * NY), jnp.int32)
    return pl.pallas_call(
        core_kernel,
        out_shape=tuple(jax.ShapeDtypeStruct(s, d) for s, d in OUTS),
        in_specs=[ANY] * 10,
        out_specs=(ANY,) * 7,
        scratch_shapes=[
            *(pltpu.VMEM(s, d) for s, d in OUTS),
            vm(TOK * HEADS, 128, dtype=F32), vm(TOK * HEADS, 128, dtype=F32), DMA((7,)),
            vm(1, TOK, HEADS, HD), vm(1, TOK, HEADS, RD), vm(1, TOK, HEADS * HD),
            vm(1, TOK, LAT), vm(1, TOK, RD), vm(LAT, 256), vm(LAT, 256),
            table, table, table,
            vm(ROWS, 128), vm(NCTX, TOK, PACK), vm(NCTX, TOK, PACK), vm(2, TOK, PACK),
            vm(NX, NC, NY, ROWS, 128),
            vm(LAT, 512), vm(512, LAT), vm(LAT, NK),
            vm(2, NCH, CHUNK, 256), vm(2, NCH, 256, CHUNK),
            vm(2, NCH, CHUNK, 128), vm(2, NCH, 128, CHUNK),
            vm(2, NQ, 256), vm(2, 256, NQ), vm(2, 128, NQ),
            vm(2, NCH, CHUNK, NQ, dtype=F32), vm(2, 1, NQ, dtype=F32),
            vm(2, NCH, CHUNK, NQ), vm(2, NQ, 128),
            vm(NK, 256), vm(NK, 256),
            vm(2, 128, NQ, dtype=F32), vm(2, 256, NQ, dtype=F32),
            vm(NCTX, TOK, 256), vm(NCTX, TOK, 256), vm(2, TOK, 256),
            vm(NCTX, TOK, 384), vm(NCTX, TOK, 384), vm(2, TOK, 384),
            vm(NX, NC, NY, ROWS, 128), vm(NX, NY, ROWS, 128), vm(NX, NY, ROWS, 128),
            vm(NX, half, 128), vm(NX, half, 128), vm(NX, half, 128),
            vm(2, 2, half, 128), vm(NY, half, 128), vm(NY, half, 128),
            vm(NX, half, 128), vm(NY, half, 128), vm(3, half, 128), vm(3, half, 128),
            vm(NZ, TOK, 256), vm(NZ, TOK, 256), vm(NZ - 1, TOK, 256), vm(NZ - 1, TOK, 256),
            vm(NY, 16, 512), vm(NY - 1, 16, 512),
            DMA((10,)), DMA((4,)), DMA((4,)), DMA((4,)), DMA((4,)), DMA((4,)), DMA((4,)),
            DMA((4,)), DMA((4,)), DMA((16,)), DMA((16,)),
            DMA((9,)), DMA((9,)), DMA((9,)), DMA((9,)), DMA((9,)), DMA((9,)),
            DMA((4,)), DMA((4,)), DMA((4, 3)), DMA((4, 3)), DMA((6,)), DMA((6,)),
            DMA((3,)), DMA((3,)), DMA((3,)), DMA((3,)),
            DMA((7,)), DMA((7,)), DMA((7,)), DMA((7,)), DMA((3,)), DMA((3,)),
        ],
        compiler_params=pltpu.CompilerParams(
            collective_id=0, has_side_effects=True, vmem_limit_bytes=60 * 2**20
        ),
        name="core",
    )(*args)


def store_kernel(*refs):
    src, dst, mid, lsem, ssem = refs[0:7], refs[7:14], refs[14:21], refs[21], refs[22]
    reads = [pltpu.make_async_copy(src[n], mid[n], lsem.at[n]) for n in range(7)]
    writes = [pltpu.make_async_copy(mid[n], dst[n], ssem.at[n]) for n in range(7)]
    for copy in reads:
        copy.start()
    for n in range(7):
        reads[n].wait()
        writes[n].start()
    for copy in writes:
        copy.wait()


def store(*arrays):
    return pl.pallas_call(
        store_kernel,
        out_shape=tuple(jax.ShapeDtypeStruct(s, d) for s, d in OUTS),
        in_specs=[ANY] * 7,
        out_specs=(ANY,) * 7,
        scratch_shapes=[*(pltpu.VMEM(s, d) for s, d in OUTS), DMA((7,)), DMA((7,))],
        compiler_params=pltpu.CompilerParams(vmem_limit_bytes=60 * 2**20),
        name="store",
    )(*arrays)


def on_device(
    query_nope, query_rope, latent, key_rope, out_grad,
    key_weight, value_weight, block_doc, block_image, block_flag,
):
    return store(*core(
        query_nope, query_rope, out_grad, latent, key_rope,
        key_weight, value_weight, block_doc, block_image, block_flag,
    ))


def solution(mesh):
    return jax.shard_map(
        on_device,
        mesh=mesh,
        in_specs=(
            P("dp", ("ctx", "seq"), None, None),
            P("dp", ("ctx", "seq"), None, None),
            P("dp", ("ctx", "seq"), None),
            P("dp", ("ctx", "seq"), None),
            P("dp", ("ctx", "seq"), None),
            P(None, "ctx"),
            P(None, "ctx"),
            P("dp", None),
            P("dp", None),
            P("dp", None),
        ),
        out_specs=(
            P("dp", ("ctx", "seq"), None),
            P("dp", ("ctx", "seq"), None, None),
            P("dp", ("ctx", "seq"), None, None),
            P("dp", ("ctx", "seq"), None),
            P("dp", ("ctx", "seq"), None),
            P(("dp", "seq"), "ctx"),
            P(("dp", "seq"), "ctx"),
        ),
        check_vma=False,
    )
```
